32 devices in a mesh: group: 2 (over y), gx: 4 (over x, core), gy: 4 (over z).
Axes of the slice: x: 2, y: 2, z: 4, core: 2. Of those that a mesh axis runs over, the one named last changes fastest.
Arguments:
- hidden: bfloat16 [16, 2, 8192], P(('group', 'gy'), None, 'gx'), parts along dimension 0, may hold values from -168 to 168
- norm_gain: bfloat16 [8192], P('gx'), may hold values from 0.099609375 to 1.8984375
- w_qkv: bfloat16 [8192, 10240], P('gx', 'gy'), may hold values from -0.0625 to 0.0625
- w_out: bfloat16 [8192, 8192], P('gy', 'gx'), may hold values from -0.5 to 0.5
- k_cache: bfloat16 [16, 1536, 1024], P(('group', 'gy'), 'gx'), parts along dimension 0, may hold values from -408 to 408
- v_cache: bfloat16 [16, 1536, 1024], P(('group', 'gy'), 'gx'), parts along dimension 0, may hold values from -6 to 6
- cache_len: int32 [16], P(('group', 'gy')), parts along dimension 0, may hold values from 192 to 1536, as said below
- positions: int32 [16], P(('group', 'gy')), parts along dimension 0, may hold values from 1536 to 6143
Outputs:
- layer_out: bfloat16 [16, 2, 8192], P(('group', 'gy'), None, 'gx'), parts along dimension 0
The draws below stay inside these ranges and needn't reach their ends.
There are 2 independent parts, one for each index of `group`. The reference program is written for one: setup_inputs(seed, part) draws one part's arguments, and reference() takes and returns one part's arrays. A program takes and returns all parts, laid end to end along the dimension named above; an argument that names none is the same for every part. Nothing has to cross between parts.
Inputs may be any that keep to these rules, and one draw needn't show every extreme that they name: Timeline b's keys and values sit in slots 0 to cache_len[b] - 1; later slots hold stale entries. Some timeline fills all 1536 slots.
All inputs are finite; a program needn't handle non-finite values.
Results may differ from the reference program's by a relative error of at most 0.013.
Values may be sent and summed in bfloat16 or wider, within the bound.
No kernel may reach another device: no remote copies, remote signals or barrier semaphores. Data moves between devices by JAX's collectives and lax.ppermute only.
A program may use at most 64 MiB of HBM per device.

```python
import math
import jax
import jax.numpy as jnp
from jax import lax

D = 8192
H = 64
KVH = 8
HD = 128
SPAN_DEV = 384
TIMELINES = 8
CACHE = 1536
N_GX = 4


def draw_hidden(key, part):
    key = jax.random.fold_in(key, 7)
    key_base, key_columns = jax.random.split(key, 2)
    base = jnp.clip(jax.random.normal(key_base, (TIMELINES, 2, D), jnp.float32), -4.0, 4.0)
    columns = jnp.exp(jax.random.uniform(key_columns, (1, 1, D), jnp.float32, 0.0, math.log(3.0)))
    return (base * columns).astype(jnp.bfloat16)


def draw_k_cache(key, part):
    key = jax.random.fold_in(key, 9)
    key_base = jax.random.fold_in(key, 0)
    base = jnp.clip(jax.random.normal(key_base, (TIMELINES, CACHE, KVH * HD), jnp.float32), -6.0, 6.0)
    return base.astype(jnp.bfloat16)


def draw_cache_len(key, part):
    key = jax.random.fold_in(key, 5)
    key_lengths, key_full = jax.random.split(key)
    lengths = jax.random.randint(key_lengths, (TIMELINES,), CACHE // 8, CACHE + 1)
    filled = jax.random.randint(key_full, (), 0, TIMELINES)
    return jnp.where(jnp.arange(TIMELINES, dtype=jnp.int32) == filled, CACHE, lengths).astype(jnp.int32)


def plant(drawn, key, least, top_value):
    longest = drawn.shape.index(max(drawn.shape))
    spots = []
    for shift in (0, 1):
        where = [jax.random.randint(jax.random.fold_in(key, axis), (), 0, length) for axis, length in enumerate(drawn.shape)]
        where[longest] = (where[longest] + shift) % drawn.shape[longest]
        spots.append(tuple(where))
    return drawn.at[spots[0]].set(least).at[spots[1]].set(top_value)


def level_of(key, shape, cuts, smallest, top_value):
    gain = 1.0
    for axis_at, blocks in cuts:
        draws = jax.random.uniform(jax.random.fold_in(jax.random.fold_in(key, 6), axis_at), (blocks,), jnp.float32, smallest / len(cuts), top_value / len(cuts))
        gain = gain * jnp.repeat(jnp.exp(draws), shape[axis_at] // blocks).reshape((-1,) + (1,) * (len(shape) - 1 - axis_at))
    return gain


def gaussian(rng, dims, width, bound, shards=(), held_as=jnp.bfloat16):
    result = width * jax.random.normal(rng, dims, jnp.float32)
    if shards:
        result = result * level_of(rng, dims, shards, -0.22, 0.18)
    return jnp.clip(result, -bound, bound).astype(held_as)


def setup_inputs(seed: int = 0, part: int = 0) -> dict:
    splits = jax.random.split(jax.random.key(seed), 9)
    part_keys = jax.random.split(jax.random.fold_in(splits[8], part), 9)
    hidden = draw_hidden(jax.random.fold_in(jax.random.fold_in(splits[8], part), 71), part)
    norm_gain = jnp.clip(1.0 + 0.18 * jax.random.normal(splits[1], (D,), jnp.float32), 0.099609375, 1.8984375).astype(jnp.bfloat16)
    w_qkv = gaussian(splits[2], (D, (H + 2 * KVH) * HD), D ** -0.5, 0.0625, ((0, 4), (1, 4)))
    w_out = gaussian(splits[3], (H * HD, D), (H * HD // 64) ** -0.5, 0.5, ((0, 4), (1, 4)))
    k_cache = draw_k_cache(jax.random.fold_in(jax.random.fold_in(splits[8], part), 71), part)
    v_cache = gaussian(part_keys[5], (TIMELINES, CACHE, KVH * HD), 1.0, 6.0, ((0, 4), (1, 4)))
    cache_len = draw_cache_len(jax.random.fold_in(jax.random.fold_in(splits[8], part), 71), part)
    positions = plant(jax.random.randint(part_keys[7], (TIMELINES,), CACHE, 4 * CACHE), jax.random.fold_in(part_keys[7], 1), CACHE, (4 * CACHE) - 1).astype(jnp.int32)
    return dict(hidden=hidden, norm_gain=norm_gain, w_qkv=w_qkv, w_out=w_out, k_cache=k_cache, v_cache=v_cache, cache_len=cache_len, positions=positions)


NEGATIVE = -1e+30
ROPE_BASE = 500000.0
EPSILON = 1e-05

def rotate(inputs, positions, offset):
    halfway = HD // 2
    frequency = ROPE_BASE ** (-2.0 * jnp.arange(halfway, dtype=jnp.float32) / HD)
    places = (positions[:, None] + offset + jnp.arange(inputs.shape[1], dtype=jnp.int32)[None, :]).astype(jnp.float32)
    angles = places[:, :, None] * frequency[None, None, :]
    cosine = jnp.cos(angles)[:, :, None, :]
    sines = jnp.sin(angles)[:, :, None, :]
    leading = inputs[..., :halfway]
    trailing = inputs[..., halfway:]
    return jnp.concatenate([leading * cosine - trailing * sines, trailing * cosine + leading * sines], axis=-1)

def block_terms(scores, usable):
    maxima = lax.optimization_barrier(jnp.max(jnp.where(usable, scores, NEGATIVE), axis=-1))
    weights = jnp.exp(jnp.where(usable, scores - maxima[..., None], NEGATIVE))
    return (maxima, lax.optimization_barrier(jnp.sum(weights, axis=-1)), weights)

def attend_one(bundle):
    queries, cached_keys, cached_values, new_keys, new_values, length = bundle
    scaling = HD ** (-0.5)
    queries_wide = queries.astype(jnp.float32)
    keys_wide = cached_keys.reshape(N_GX, SPAN_DEV, KVH, HD).astype(jnp.float32)
    values_wide = cached_values.reshape(N_GX, SPAN_DEV, KVH, HD).astype(jnp.float32)
    scores = jnp.einsum('tgqd,nsgd->ntgqs', queries_wide, keys_wide) * scaling
    slot_ids = jnp.arange(CACHE, dtype=jnp.int32).reshape(N_GX, 1, 1, 1, SPAN_DEV)
    maxima, totals, weights = block_terms(scores, slot_ids < length)
    rounded = lax.optimization_barrier(weights.astype(jnp.bfloat16)).astype(jnp.float32)
    partials = jnp.einsum('ntgqs,nsgd->ntgqd', rounded, values_wide)
    fresh_scores = jnp.einsum('tgqd,jgd->tgqj', queries_wide, new_keys.astype(jnp.float32)) * scaling
    indices = jnp.arange(2, dtype=jnp.int32)
    allowed = (indices[None, :] <= indices[:, None]).reshape(2, 1, 1, 2)
    fresh_maxima, fresh_totals, fresh_weights = block_terms(fresh_scores, allowed)
    fresh_rounded = lax.optimization_barrier(fresh_weights.astype(jnp.bfloat16)).astype(jnp.float32)
    fresh_partials = jnp.einsum('tgqj,jgd->tgqd', fresh_rounded, new_values.astype(jnp.float32))
    highest = jnp.maximum(lax.optimization_barrier(jnp.max(maxima, axis=0)), fresh_maxima)
    factors = jnp.exp(maxima - highest)
    fresh_factor = jnp.exp(fresh_maxima - highest)
    denominator = lax.optimization_barrier(jnp.sum(totals * factors, axis=0)) + fresh_totals * fresh_factor
    numerator = lax.optimization_barrier(jnp.sum(partials * factors[..., None], axis=0)) + fresh_partials * fresh_factor[..., None]
    return (numerator / denominator[..., None]).astype(jnp.bfloat16).reshape(2, H * HD)

def reference(hidden, norm_gain, w_qkv, w_out, k_cache, v_cache, cache_len, positions):
    floats = hidden.astype(jnp.float32)
    squares = lax.optimization_barrier(jnp.sum(floats * floats, axis=-1, keepdims=True))
    normed = (floats * lax.rsqrt(squares / D + EPSILON) * norm_gain.astype(jnp.float32)).astype(jnp.bfloat16)
    projected = jnp.dot(normed.reshape(TIMELINES * 2, D), w_qkv, preferred_element_type=jnp.float32)
    projected = lax.optimization_barrier(projected.astype(jnp.bfloat16)).reshape(TIMELINES, 2, (H + 2 * KVH) * HD)
    widened = projected.astype(jnp.float32)
    queries = rotate(widened[..., :H * HD].reshape(TIMELINES, 2, H, HD), positions, 0).astype(jnp.bfloat16)
    new_keys = rotate(widened[..., H * HD:(H + KVH) * HD].reshape(TIMELINES, 2, KVH, HD), positions, 0).astype(jnp.bfloat16)
    new_values = projected[..., (H + KVH) * HD:].reshape(TIMELINES, 2, KVH, HD)
    grouped = lax.optimization_barrier(queries).reshape(TIMELINES, 2, KVH, H // KVH, HD)
    attended = lax.map(attend_one, (grouped, k_cache, v_cache, lax.optimization_barrier(new_keys), new_values, cache_len))
    layer_out = jnp.dot(attended.reshape(TIMELINES * 2, H * HD), w_out, preferred_element_type=jnp.float32)
    return layer_out.astype(jnp.bfloat16).reshape(TIMELINES, 2, D)
```

```python
import jax
import jax.numpy as jnp
from jax import lax
from jax.experimental import pallas as pl
from jax.experimental.pallas import tpu as pltpu
from jax.sharding import PartitionSpec as P

D = 8192
H = 64
KVH = 8
HD = 128
SPAN_DEV = 384


NEGATIVE = -1e30
ROPE_BASE = 500000.0
EPSILON = 1e-05


def combined_all(shard, axis, combine):
    everything = jax.tree.map(lambda part: lax.all_gather(part, axis), shard)
    first = jax.tree.map(lambda part: part[0], everything)

    def turn(k, so_far):
        return combine(so_far, jax.tree.map(lambda part: part[k], everything))

    return lax.fori_loop(1, lax.axis_size(axis), turn, first)


def rotate(inputs, positions, offset):
    halfway = HD // 2
    frequency = ROPE_BASE ** (-2.0 * jnp.arange(halfway, dtype=jnp.float32) / HD)
    places = (
        positions[:, None] + offset + jnp.arange(inputs.shape[1], dtype=jnp.int32)[None, :]
    ).astype(jnp.float32)
    angles = places[:, :, None] * frequency[None, None, :]
    cosine = jnp.cos(angles)[:, :, None, :]
    sines = jnp.sin(angles)[:, :, None, :]
    leading = inputs[..., :halfway]
    trailing = inputs[..., halfway:]
    return jnp.concatenate(
        [leading * cosine - trailing * sines, trailing * cosine + leading * sines], axis=-1
    )


def block_terms(scores, usable):
    maxima = jnp.max(jnp.where(usable, scores, NEGATIVE), axis=-1)
    weights = jnp.exp(jnp.where(usable, scores - maxima[..., None], NEGATIVE))
    return (maxima, jnp.sum(weights, axis=-1), weights)


def combine(first_part, second_part):
    maxima_a, totals_a, partials_a = first_part
    maxima_b, totals_b, partials_b = second_part
    highest = jnp.maximum(maxima_a, maxima_b)
    factor_a = jnp.exp(maxima_a - highest)
    factor_b = jnp.exp(maxima_b - highest)
    return (
        highest,
        totals_a * factor_a + totals_b * factor_b,
        partials_a * factor_a[..., None] + partials_b * factor_b[..., None],
    )


def general_body(hidden, norm_gain, w_qkv, w_out, k_cache, v_cache, cache_len, positions):
    timelines_here = hidden.shape[0]
    tokens_here = hidden.shape[1]
    floats = hidden.astype(jnp.float32)
    squares = lax.psum(jnp.sum(floats * floats, axis=-1), "gx")
    normed = (
        floats * lax.rsqrt(squares[..., None] / D + EPSILON) * norm_gain.astype(jnp.float32)
    ).astype(jnp.bfloat16)
    partial_sums = jnp.einsum(
        "rkc,ce->rke",
        lax.all_gather(normed, "gy", axis=0, tiled=True),
        w_qkv,
        preferred_element_type=jnp.float32,
    )
    summed = lax.psum(partial_sums, "gx").astype(jnp.bfloat16)
    projected = lax.all_to_all(summed, "gy", split_axis=0, concat_axis=2, tiled=True)
    widened = projected.astype(jnp.float32)
    queries = rotate(
        widened[..., : H * HD].reshape(timelines_here, tokens_here, H, HD), positions, 0
    ).astype(jnp.bfloat16)
    fresh_keys = rotate(
        widened[..., H * HD : (H + KVH) * HD].reshape(timelines_here, tokens_here, KVH, HD),
        positions,
        0,
    ).astype(jnp.bfloat16)
    fresh_values = projected[..., (H + KVH) * HD :].reshape(timelines_here, tokens_here, KVH, HD)
    grouped = queries.reshape(timelines_here, tokens_here, KVH, H // KVH, HD)
    cached_keys = k_cache.reshape(timelines_here, SPAN_DEV, KVH, HD)
    cached_values = v_cache.reshape(timelines_here, SPAN_DEV, KVH, HD)
    scaling = HD ** (-0.5)
    scores = (
        jnp.einsum("tkgqd,tsgd->tkgqs", grouped, cached_keys, preferred_element_type=jnp.float32)
        * scaling
    )
    slot_ids = lax.axis_index("gx") * SPAN_DEV + jnp.arange(SPAN_DEV, dtype=jnp.int32)
    usable = (slot_ids[None, :] < cache_len[:, None]).reshape(timelines_here, 1, 1, 1, SPAN_DEV)
    maxima, totals, weights = block_terms(scores, usable)
    partials = jnp.einsum(
        "tkgqs,tsgd->tkgqd",
        weights.astype(jnp.bfloat16),
        cached_values,
        preferred_element_type=jnp.float32,
    )
    merged = combined_all((maxima, totals, partials), "gx", combine)
    fresh_scores = (
        jnp.einsum("tkgqd,tjgd->tkgqj", grouped, fresh_keys, preferred_element_type=jnp.float32)
        * scaling
    )
    key_ids = jnp.arange(tokens_here, dtype=jnp.int32)
    allowed = (key_ids[None, :] <= key_ids[:, None]).reshape(1, tokens_here, 1, 1, tokens_here)
    fresh_maxima, fresh_totals, fresh_weights = block_terms(fresh_scores, allowed)
    fresh_partials = jnp.einsum(
        "tkgqj,tjgd->tkgqd",
        fresh_weights.astype(jnp.bfloat16),
        fresh_values,
        preferred_element_type=jnp.float32,
    )
    _, denominator, numerator = combine(merged, (fresh_maxima, fresh_totals, fresh_partials))
    attended = (
        (numerator / denominator[..., None])
        .astype(jnp.bfloat16)
        .reshape(timelines_here, tokens_here, H * HD)
    )
    heads_in = lax.all_to_all(attended, "gy", split_axis=2, concat_axis=0, tiled=True)
    return lax.psum_scatter(
        jnp.einsum("rke,ed->rkd", heads_in, w_out, preferred_element_type=jnp.float32),
        "gy",
        scatter_dimension=0,
        tiled=True,
    ).astype(jnp.bfloat16)


NX = 4
NY = 4
ROWS = 4
QKV_ROWS = (H + 2 * KVH) // NY * ROWS
OUT_HEADS = H // NY
OUT_ROWS = OUT_HEADS * ROWS
QUERIES = H * ROWS
VMEM_SPEC = pl.BlockSpec(memory_space=pltpu.VMEM)
SMEM_SPEC = pl.BlockSpec(memory_space=pltpu.SMEM)
F32 = jnp.float32
BF16 = jnp.bfloat16


def call(kernel, name, out_shape, operands, scratch=(), scalars=0, mib=8):
    many = isinstance(out_shape, (list, tuple))
    return pl.pallas_call(
        kernel,
        in_specs=[SMEM_SPEC] * scalars + [VMEM_SPEC] * (len(operands) - scalars),
        out_specs=[VMEM_SPEC] * len(out_shape) if many else VMEM_SPEC,
        out_shape=out_shape,
        scratch_shapes=list(scratch),
        compiler_params=pltpu.CompilerParams(vmem_limit_bytes=mib << 20),
        name=name,
    )(*operands)


def high_rest(values):
    high = values.astype(BF16).astype(F32)
    return high, values - high


def square_kernel(h0, h1, h2, h3, out):
    for shift, hidden in enumerate((h0, h1, h2, h3)):
        for timeline in range(2):
            wide = hidden[timeline].astype(F32)
            total = jnp.sum(wide * wide, axis=-1, keepdims=True)
            at = ROWS * shift + 2 * timeline
            out[at : at + 2, :] = jnp.broadcast_to(total, (2, HD))


def project_kernel(h0, h1, h2, h3, s0, s1, s2, s3, gain, w, out, rows):
    for shift, hidden in enumerate((h0, h1, h2, h3)):
        for timeline in range(2):
            at = ROWS * shift + 2 * timeline
            rows[at : at + 2, :] = hidden[timeline].astype(F32)
    squares = ((s0[...] + s1[...]) + (s2[...] + s3[...]))[:, 0:1]
    normed = rows[...] * lax.rsqrt(squares / D + EPSILON) * gain[...].astype(F32)
    normed = normed.astype(BF16)
    width = 512
    for step in range(w.shape[1] // width):
        part = jnp.dot(
            normed, w[:, width * step : width * (step + 1)], preferred_element_type=F32
        )
        for head in range(width // HD):
            at = (step * (width // HD) + head) * ROWS
            for shift in range(NY):
                out[shift, at : at + ROWS, :] = part[
                    ROWS * shift : ROWS * (shift + 1), HD * head : HD * (head + 1)
                ]


def add_kernel(a, b, out):
    out[...] = a[...] + b[...]


def round_kernel(a, b, *outs):
    for shift, out in enumerate(outs):
        out[...] = (a[shift] + b[shift]).astype(BF16)


def attend_kernel(
    lengths, r0, r1, r2, r3, cosine, sine, keys, values, out, projected, turns, spread
):
    my_x = lax.axis_index("gx")
    my_y = lax.axis_index("gy")
    for shift, received in enumerate((r0, r1, r2, r3)):
        at = pl.multiple_of((my_y ^ shift) * QKV_ROWS, 16)
        projected[pl.ds(at, QKV_ROWS), :] = received[...].astype(F32)
    for t in range(4):
        turns[0, 2 * t : 2 * t + 2, :] = cosine[t % 2]
        turns[1, 2 * t : 2 * t + 2, :] = sine[t % 2]
    turned = projected[: QUERIES + KVH * ROWS, :]
    swapped = pltpu.roll(turned, HD // 2, 1)
    turned = (
        turned.reshape(-1, 8, HD) * turns[0][None] + swapped.reshape(-1, 8, HD) * turns[1][None]
    ).reshape(-1, HD)
    queries = turned[:QUERIES].astype(BF16)
    new_keys = turned[QUERIES:].astype(BF16)
    new_values = projected[QUERIES + KVH * ROWS :, :].astype(BF16)

    row = lax.broadcasted_iota(jnp.int32, (QUERIES, 1), 0)
    token = row & 1
    timeline = (row >> 1) & 1
    group_rows = QUERIES // KVH
    spread[...] = jnp.zeros_like(spread)
    scores = jnp.zeros((QUERIES, SPAN_DEV), F32)
    for t in range(2):
        mine = jnp.where(timeline == t, queries, jnp.zeros_like(queries))
        for g in range(KVH):
            at = slice(group_rows * g, group_rows * (g + 1))
            spread[t, at, HD * g : HD * (g + 1)] = mine[at]
        scores += lax.dot_general(
            spread[t], keys[t], (((1,), (1,)), ((), ())), preferred_element_type=F32
        )
    scaling = HD ** (-0.5)
    scores = scores * scaling
    slot = my_x * SPAN_DEV + lax.broadcasted_iota(jnp.int32, (QUERIES, SPAN_DEV), 1)
    usable = slot < jnp.where(timeline == 0, lengths[0], lengths[1])
    maxima = jnp.max(jnp.where(usable, scores, NEGATIVE), axis=-1, keepdims=True)

    wide_queries = queries.astype(F32)
    column = lax.broadcasted_iota(jnp.int32, (QUERIES, KVH * ROWS), 1)
    fresh = []
    for j in range(2):
        pick = jnp.where(column == (row // group_rows) * ROWS + timeline * 2 + j, 1.0, 0.0)
        pick = pick.astype(BF16)
        key = jnp.dot(pick, new_keys, preferred_element_type=F32)
        value = jnp.dot(pick, new_values, preferred_element_type=F32)
        score = jnp.sum(wide_queries * key, axis=-1, keepdims=True) * scaling
        allowed = (token >= j) & (my_x == 0)
        maxima = jnp.maximum(maxima, jnp.where(allowed, score, NEGATIVE))
        fresh.append((score, allowed, value))
    weights = jnp.exp(jnp.where(usable, scores - maxima, NEGATIVE))
    totals = jnp.sum(weights, axis=-1, keepdims=True)
    rounded = weights.astype(BF16)
    added = jnp.zeros((QUERIES, HD), F32)
    for score, allowed, value in fresh:
        weight = jnp.exp(jnp.where(allowed, score - maxima, NEGATIVE))
        totals += weight
        added += weight.astype(BF16).astype(F32) * value
    sums = jnp.zeros((QUERIES, KVH * HD), F32)
    for t in range(2):
        mine = jnp.where(timeline == t, rounded, jnp.zeros_like(rounded))
        sums += jnp.dot(mine, values[t], preferred_element_type=F32)
    for g in range(KVH):
        at = slice(group_rows * g, group_rows * (g + 1))
        out[at, :] = sums[at, HD * g : HD * (g + 1)] + added[at]

    lane = lax.broadcasted_iota(jnp.int32, (QUERIES, HD), 1)
    sheet = jnp.where(lane == 0, maxima, jnp.where(lane == 1, totals, 0.0))
    flat = jnp.transpose(sheet)[0:8]
    out[QUERIES : QUERIES + 8, :] = flat[:, :HD]
    out[QUERIES + 8 : QUERIES + 16, :] = flat[:, HD:]


def factor_columns(rows, sheets):
    columns = []
    for half in range(2):
        sheets[half] = jnp.zeros((HD, HD), F32)
        for k in range(2):
            sheets[half, k : k + 1, :] = rows[half][k]
    turned = [jnp.transpose(sheets[half]) for half in range(2)]
    for k in range(2):
        columns.append(
            jnp.concatenate([turned[half][:, k : k + 1] for half in range(2)], axis=0)
        )
    return columns


def merge_kernel(a, b, kept, sent, sheets):
    rows = []
    for half in range(2):
        at = QUERIES + 8 * half
        highest = jnp.maximum(a[at : at + 1, :], b[at : at + 1, :])
        high, rest = high_rest(highest)
        middle, low = high_rest(rest)
        power_a = jnp.exp(a[at : at + 1, :] - highest)
        power_b = jnp.exp(b[at : at + 1, :] - highest)
        total = a[at + 1 : at + 2, :] * power_a + b[at + 1 : at + 2, :] * power_b
        line = lax.broadcasted_iota(jnp.int32, (8, HD), 0)
        stats = jnp.zeros((8, HD), F32)
        for k, piece in enumerate((high, middle, low, *high_rest(total))):
            stats = jnp.where(line == k, piece, stats)
        kept[at : at + 8, :] = jnp.where(line == 0, highest, jnp.where(line == 1, total, 0.0))
        sheets[half, 0:8, :] = stats
        rows.append((power_a, power_b))
    sent[QUERIES : QUERIES + 16, :] = jnp.concatenate(
        [sheets[0, 0:8, :], sheets[1, 0:8, :]], axis=0
    ).astype(BF16)
    factor_a, factor_b = factor_columns(rows, sheets)
    merged = a[:QUERIES, :] * factor_a + b[:QUERIES, :] * factor_b
    kept[:QUERIES, :] = merged
    sent[:QUERIES, :] = merged.astype(BF16)


def settle_kernel(a, b, o0, o1, o2, o3, attended, sheets):
    my_y = lax.axis_index("gy")
    other = b[QUERIES : QUERIES + 16, :].astype(F32)
    rows = []
    for half in range(2):
        at = QUERIES + 8 * half
        stats = other[8 * half : 8 * half + 8]
        maximum = (stats[0:1] + stats[1:2]) + stats[2:3]
        total = stats[3:4] + stats[4:5]
        own_maximum, own_total = a[at : at + 1, :], a[at + 1 : at + 2, :]
        highest = jnp.maximum(own_maximum, maximum)
        power_a = jnp.exp(own_maximum - highest)
        power_b = jnp.exp(maximum - highest)
        whole = own_total * power_a + total * power_b
        rows.append((power_a / whole, power_b / whole))
    factor_a, factor_b = factor_columns(rows, sheets)
    attended[...] = a[:QUERIES, :] * factor_a + b[:QUERIES, :].astype(F32) * factor_b
    for shift, out in enumerate((o0, o1, o2, o3)):
        at = pl.multiple_of((my_y ^ shift) * OUT_ROWS, OUT_ROWS)
        out[...] = attended[pl.ds(at, OUT_ROWS), :].astype(BF16)


def output_kernel(a0, a1, a2, a3, w, o0, o1, o2, o3, wide, sums):
    for shift, attended in enumerate((a0, a1, a2, a3)):
        block = attended[...].astype(F32)
        for head in range(OUT_HEADS):
            wide[ROWS * shift : ROWS * (shift + 1), HD * head : HD * (head + 1)] = block[
                ROWS * head : ROWS * (head + 1)
            ]
    left = wide[...].astype(BF16)
    width = 512
    for step in range(w.shape[1] // width):
        part = jnp.dot(left, w[:, width * step : width * (step + 1)], preferred_element_type=F32)
        for chunk in range(width // HD):
            at = (step * (width // HD) + chunk) * ROWS
            for shift in range(NY):
                sums[shift, at : at + ROWS, :] = part[
                    ROWS * shift : ROWS * (shift + 1), HD * chunk : HD * (chunk + 1)
                ]
    o0[...] = sums[0]
    for shift, out in ((1, o1), (2, o2), (3, o3)):
        out[...] = sums[shift].astype(BF16)


def finish_kernel(a, b, c, d, out, total):
    total[...] = (a[...] + b[...].astype(F32)) + (c[...].astype(F32) + d[...].astype(F32))
    for chunk in range(out.shape[2] // HD):
        for timeline in range(2):
            at = ROWS * chunk + 2 * timeline
            out[timeline, :, HD * chunk : HD * (chunk + 1)] = total[at : at + 2, :].astype(BF16)


def rotation(positions):
    halfway = HD // 2
    frequency = ROPE_BASE ** (-2.0 * jnp.arange(halfway, dtype=F32) / HD)
    places = positions[:, None] + jnp.arange(2, dtype=jnp.int32)[None, :]
    angles = places.astype(F32)[:, :, None] * frequency[None, None, :]
    cosine, sine = jnp.cos(angles), jnp.sin(angles)
    return jnp.concatenate([cosine, cosine], axis=2), jnp.concatenate([-sine, sine], axis=2)


def partner(part, axis, distance):
    if distance == 0:
        return part
    return lax.ppermute(part, axis, [(k, k ^ distance) for k in range(lax.axis_size(axis))])


def small_body(hidden, norm_gain, w_qkv, w_out, k_cache, v_cache, cache_len, positions):
    def shape(*dims, dtype=BF16):
        return jax.ShapeDtypeStruct(dims, dtype)

    columns = w_out.shape[1]
    features = hidden.shape[2]
    w_qkv = pltpu.with_memory_space_constraint(w_qkv, pltpu.VMEM)
    k_cache = pltpu.with_memory_space_constraint(k_cache, pltpu.VMEM)
    v_cache = pltpu.with_memory_space_constraint(v_cache, pltpu.VMEM)
    w_out = pltpu.with_memory_space_constraint(w_out, pltpu.VMEM)
    cosine, sine = rotation(positions)
    hiddens = [partner(hidden, "gy", y) for y in range(NY)]
    squares = call(square_kernel, "square", shape(NY * ROWS, HD, dtype=F32), hiddens)
    squares = [partner(squares, "gx", x) for x in range(NX)]
    sums = call(
        project_kernel,
        "project",
        shape(NY, QKV_ROWS, HD, dtype=F32),
        [*hiddens, *squares, norm_gain[None], w_qkv],
        [pltpu.VMEM((NY * ROWS, features), F32)],
    )
    sums = call(
        add_kernel, "add", shape(NY, QKV_ROWS, HD, dtype=F32), [sums, partner(sums, "gx", 1)]
    )
    blocks = call(
        round_kernel, "round", [shape(QKV_ROWS, HD)] * NY, [sums, partner(sums, "gx", 2)]
    )
    blocks = [partner(block, "gy", y) for y, block in enumerate(blocks)]
    partial = call(
        attend_kernel,
        "attend",
        shape(QUERIES + 16, HD, dtype=F32),
        [cache_len, *blocks, cosine, sine, k_cache, v_cache],
        [
            pltpu.VMEM((NY * QKV_ROWS, HD), F32),
            pltpu.VMEM((2, 8, HD), F32),
            pltpu.VMEM((2, QUERIES, KVH * HD), BF16),
        ],
        scalars=1,
        mib=16,
    )
    kept, sent = call(
        merge_kernel,
        "merge",
        [shape(QUERIES + 16, HD, dtype=F32), shape(QUERIES + 16, HD)],
        [partial, partner(partial, "gx", 1)],
        [pltpu.VMEM((2, HD, HD), F32)],
    )
    blocks = call(
        settle_kernel,
        "settle",
        [shape(OUT_ROWS, HD)] * NY,
        [kept, partner(sent, "gx", 2)],
        [pltpu.VMEM((QUERIES, HD), F32), pltpu.VMEM((2, HD, HD), F32)],
    )
    blocks = [partner(block, "gy", y) for y, block in enumerate(blocks)]
    count = columns // HD * ROWS
    blocks = call(
        output_kernel,
        "output",
        [shape(count, HD, dtype=F32)] + [shape(count, HD)] * (NY - 1),
        [*blocks, w_out],
        [
            pltpu.VMEM((NY * ROWS, w_out.shape[0]), F32),
            pltpu.VMEM((NY, count, HD), F32),
        ],
    )
    blocks = [partner(block, "gy", y) for y, block in enumerate(blocks)]
    return call(
        finish_kernel,
        "finish",
        shape(2, 2, columns),
        blocks,
        [pltpu.VMEM((count, HD), F32)],
    )


def solution(mesh):
    small = mesh.shape["gx"] == NX and mesh.shape["gy"] == NY
    body = small_body if small else general_body
    in_specs = (
        P(("group", "gy"), None, "gx"),
        P("gx"),
        P("gx", "gy"),
        P("gy", "gx"),
        P(("group", "gy"), "gx", None),
        P(("group", "gy"), "gx", None),
        P(("group", "gy")),
        P(("group", "gy")),
    )
    out_specs = P(("group", "gy"), None, "gx")
    return jax.shard_map(body, mesh=mesh, in_specs=in_specs, out_specs=out_specs, check_vma=False)
```

```python
import jax
import jax.numpy as jnp
from jax import lax
from jax.experimental import pallas as pl
from jax.experimental.pallas import tpu as pltpu
from jax.sharding import PartitionSpec as P

D = 8192
H = 64
KVH = 8
HD = 128
SPAN_DEV = 384


NEGATIVE = -1e30
ROPE_BASE = 500000.0
EPSILON = 1e-05


def combined_all(shard, axis, combine):
    everything = jax.tree.map(lambda part: lax.all_gather(part, axis), shard)
    first = jax.tree.map(lambda part: part[0], everything)

    def turn(k, so_far):
        return combine(so_far, jax.tree.map(lambda part: part[k], everything))

    return lax.fori_loop(1, lax.axis_size(axis), turn, first)


def rotate(inputs, positions, offset):
    halfway = HD // 2
    frequency = ROPE_BASE ** (-2.0 * jnp.arange(halfway, dtype=jnp.float32) / HD)
    places = (
        positions[:, None] + offset + jnp.arange(inputs.shape[1], dtype=jnp.int32)[None, :]
    ).astype(jnp.float32)
    angles = places[:, :, None] * frequency[None, None, :]
    cosine = jnp.cos(angles)[:, :, None, :]
    sines = jnp.sin(angles)[:, :, None, :]
    leading = inputs[..., :halfway]
    trailing = inputs[..., halfway:]
    return jnp.concatenate(
        [leading * cosine - trailing * sines, trailing * cosine + leading * sines], axis=-1
    )


def block_terms(scores, usable):
    maxima = jnp.max(jnp.where(usable, scores, NEGATIVE), axis=-1)
    weights = jnp.exp(jnp.where(usable, scores - maxima[..., None], NEGATIVE))
    return (maxima, jnp.sum(weights, axis=-1), weights)


def combine(first_part, second_part):
    maxima_a, totals_a, partials_a = first_part
    maxima_b, totals_b, partials_b = second_part
    highest = jnp.maximum(maxima_a, maxima_b)
    factor_a = jnp.exp(maxima_a - highest)
    factor_b = jnp.exp(maxima_b - highest)
    return (
        highest,
        totals_a * factor_a + totals_b * factor_b,
        partials_a * factor_a[..., None] + partials_b * factor_b[..., None],
    )


def general_body(hidden, norm_gain, w_qkv, w_out, k_cache, v_cache, cache_len, positions):
    timelines_here = hidden.shape[0]
    tokens_here = hidden.shape[1]
    floats = hidden.astype(jnp.float32)
    squares = lax.psum(jnp.sum(floats * floats, axis=-1), "gx")
    normed = (
        floats * lax.rsqrt(squares[..., None] / D + EPSILON) * norm_gain.astype(jnp.float32)
    ).astype(jnp.bfloat16)
    partial_sums = jnp.einsum(
        "rkc,ce->rke",
        lax.all_gather(normed, "gy", axis=0, tiled=True),
        w_qkv,
        preferred_element_type=jnp.float32,
    )
    summed = lax.psum(partial_sums, "gx").astype(jnp.bfloat16)
    projected = lax.all_to_all(summed, "gy", split_axis=0, concat_axis=2, tiled=True)
    widened = projected.astype(jnp.float32)
    queries = rotate(
        widened[..., : H * HD].reshape(timelines_here, tokens_here, H, HD), positions, 0
    ).astype(jnp.bfloat16)
    fresh_keys = rotate(
        widened[..., H * HD : (H + KVH) * HD].reshape(timelines_here, tokens_here, KVH, HD),
        positions,
        0,
    ).astype(jnp.bfloat16)
    fresh_values = projected[..., (H + KVH) * HD :].reshape(timelines_here, tokens_here, KVH, HD)
    grouped = queries.reshape(timelines_here, tokens_here, KVH, H // KVH, HD)
    cached_keys = k_cache.reshape(timelines_here, SPAN_DEV, KVH, HD)
    cached_values = v_cache.reshape(timelines_here, SPAN_DEV, KVH, HD)
    scaling = HD ** (-0.5)
    scores = (
        jnp.einsum("tkgqd,tsgd->tkgqs", grouped, cached_keys, preferred_element_type=jnp.float32)
        * scaling
    )
    slot_ids = lax.axis_index("gx") * SPAN_DEV + jnp.arange(SPAN_DEV, dtype=jnp.int32)
    usable = (slot_ids[None, :] < cache_len[:, None]).reshape(timelines_here, 1, 1, 1, SPAN_DEV)
    maxima, totals, weights = block_terms(scores, usable)
    partials = jnp.einsum(
        "tkgqs,tsgd->tkgqd",
        weights.astype(jnp.bfloat16),
        cached_values,
        preferred_element_type=jnp.float32,
    )
    merged = combined_all((maxima, totals, partials), "gx", combine)
    fresh_scores = (
        jnp.einsum("tkgqd,tjgd->tkgqj", grouped, fresh_keys, preferred_element_type=jnp.float32)
        * scaling
    )
    key_ids = jnp.arange(tokens_here, dtype=jnp.int32)
    allowed = (key_ids[None, :] <= key_ids[:, None]).reshape(1, tokens_here, 1, 1, tokens_here)
    fresh_maxima, fresh_totals, fresh_weights = block_terms(fresh_scores, allowed)
    fresh_partials = jnp.einsum(
        "tkgqj,tjgd->tkgqd",
        fresh_weights.astype(jnp.bfloat16),
        fresh_values,
        preferred_element_type=jnp.float32,
    )
    _, denominator, numerator = combine(merged, (fresh_maxima, fresh_totals, fresh_partials))
    attended = (
        (numerator / denominator[..., None])
        .astype(jnp.bfloat16)
        .reshape(timelines_here, tokens_here, H * HD)
    )
    heads_in = lax.all_to_all(attended, "gy", split_axis=2, concat_axis=0, tiled=True)
    return lax.psum_scatter(
        jnp.einsum("rke,ed->rkd", heads_in, w_out, preferred_element_type=jnp.float32),
        "gy",
        scatter_dimension=0,
        tiled=True,
    ).astype(jnp.bfloat16)


NX = 4
NY = 4
ROWS = 4
QKV_ROWS = (H + 2 * KVH) // NY * ROWS
OUT_HEADS = H // NY
OUT_ROWS = OUT_HEADS * ROWS
QUERIES = H * ROWS
VMEM_SPEC = pl.BlockSpec(memory_space=pltpu.VMEM)
SMEM_SPEC = pl.BlockSpec(memory_space=pltpu.SMEM)
F32 = jnp.float32
BF16 = jnp.bfloat16


def call(kernel, name, out_shape, operands, scratch=(), scalars=0, mib=8, cost=None):
    many = isinstance(out_shape, (list, tuple))
    return pl.pallas_call(
        kernel,
        in_specs=[SMEM_SPEC] * scalars + [VMEM_SPEC] * (len(operands) - scalars),
        out_specs=[VMEM_SPEC] * len(out_shape) if many else VMEM_SPEC,
        out_shape=out_shape,
        scratch_shapes=list(scratch),
        compiler_params=pltpu.CompilerParams(vmem_limit_bytes=mib << 20),
        cost_estimate=cost,
        name=name,
    )(*operands)


def high_rest(values):
    high = values.astype(BF16).astype(F32)
    return high, values - high


def pair_kernel(own, other, out):
    out[0] = own[...]
    out[1] = other[...]


def add_kernel(a, b, out):
    out[...] = a[...] + b[...]


def square_kernel(near, far, out):
    for half, pair in enumerate((near, far)):
        for k in range(4):
            wide = pair[k // 2, k % 2].astype(F32)
            total = jnp.sum(wide * wide, axis=-1, keepdims=True)
            at = 8 * half + 2 * k
            out[at : at + 2, :] = jnp.broadcast_to(total, (2, HD))


def project_kernel(near, far, s0, s1, gain, w, kept, sent, rows, sums):
    mixed = lax.axis_index("gx") ^ lax.axis_index("gy")
    for half, pair in enumerate((near, far)):
        for k in range(4):
            at = 8 * half + 2 * k
            rows[at : at + 2, :] = pair[k // 2, k % 2].astype(F32)
    squares = (s0[...] + s1[...])[:, 0:1]
    normed = rows[...] * lax.rsqrt(squares / D + EPSILON) * gain[...].astype(F32)
    normed = normed.astype(BF16)
    width = 512
    for step in range(w.shape[1] // width):
        part = jnp.dot(
            normed, w[:, width * step : width * (step + 1)], preferred_element_type=F32
        )
        for head in range(width // HD):
            at = (step * (width // HD) + head) * ROWS
            for shift in range(NY):
                sums[shift, at : at + ROWS, :] = part[
                    ROWS * shift : ROWS * (shift + 1), HD * head : HD * (head + 1)
                ]
    for k in range(2):
        kept[k] = sums[mixed ^ (2 * k)]
        sent[k] = sums[mixed ^ (2 * k + 1)]


def halve_kernel(a, b, kept, sent):
    kept[...] = a[0] + b[0].astype(F32)
    sent[...] = (a[1] + b[1].astype(F32)).astype(sent.dtype)


def round_kernel(a, b, out):
    out[...] = (a[...] + b[...]).astype(BF16)


def attend_kernel(
    lengths, near, far, cosine, sine, keys, values, kept, sent, projected, turns, spread, parts
):
    my_x = lax.axis_index("gx")
    for core, pair in enumerate((near, far)):
        for k in range(2):
            at = pl.multiple_of((my_x ^ (2 * k + core)) * QKV_ROWS, 16)
            projected[pl.ds(at, QKV_ROWS), :] = pair[k].astype(F32)
    for t in range(4):
        turns[0, 2 * t : 2 * t + 2, :] = cosine[t % 2]
        turns[1, 2 * t : 2 * t + 2, :] = sine[t % 2]
    turned = projected[: QUERIES + KVH * ROWS, :]
    swapped = pltpu.roll(turned, HD // 2, 1)
    turned = (
        turned.reshape(-1, 8, HD) * turns[0][None] + swapped.reshape(-1, 8, HD) * turns[1][None]
    ).reshape(-1, HD)
    queries = turned[:QUERIES].astype(BF16)
    new_keys = turned[QUERIES:].astype(BF16)
    new_values = projected[QUERIES + KVH * ROWS :, :].astype(BF16)

    row = lax.broadcasted_iota(jnp.int32, (QUERIES, 1), 0)
    token = row & 1
    timeline = (row >> 1) & 1
    group_rows = QUERIES // KVH
    spread[...] = jnp.zeros_like(spread)
    scores = jnp.zeros((QUERIES, SPAN_DEV), F32)
    for t in range(2):
        mine = jnp.where(timeline == t, queries, jnp.zeros_like(queries))
        for g in range(KVH):
            at = slice(group_rows * g, group_rows * (g + 1))
            spread[t, at, HD * g : HD * (g + 1)] = mine[at]
        scores += lax.dot_general(
            spread[t], keys[t], (((1,), (1,)), ((), ())), preferred_element_type=F32
        )
    scaling = HD ** (-0.5)
    scores = scores * scaling
    slot = my_x * SPAN_DEV + lax.broadcasted_iota(jnp.int32, (QUERIES, SPAN_DEV), 1)
    usable = slot < jnp.where(timeline == 0, lengths[0], lengths[1])
    maxima = jnp.max(jnp.where(usable, scores, NEGATIVE), axis=-1, keepdims=True)

    wide_queries = queries.astype(F32)
    column = lax.broadcasted_iota(jnp.int32, (QUERIES, KVH * ROWS), 1)
    fresh = []
    for j in range(2):
        pick = jnp.where(column == (row // group_rows) * ROWS + timeline * 2 + j, 1.0, 0.0)
        pick = pick.astype(BF16)
        key = jnp.dot(pick, new_keys, preferred_element_type=F32)
        value = jnp.dot(pick, new_values, preferred_element_type=F32)
        score = jnp.sum(wide_queries * key, axis=-1, keepdims=True) * scaling
        allowed = (token >= j) & (my_x == 0)
        maxima = jnp.maximum(maxima, jnp.where(allowed, score, NEGATIVE))
        fresh.append((score, allowed, value))
    weights = jnp.exp(jnp.where(usable, scores - maxima, NEGATIVE))
    totals = jnp.sum(weights, axis=-1, keepdims=True)
    rounded = weights.astype(BF16)
    added = jnp.zeros((QUERIES, HD), F32)
    for score, allowed, value in fresh:
        weight = jnp.exp(jnp.where(allowed, score - maxima, NEGATIVE))
        totals += weight
        added += weight.astype(BF16).astype(F32) * value
    sums = jnp.zeros((QUERIES, KVH * HD), F32)
    for t in range(2):
        mine = jnp.where(timeline == t, rounded, jnp.zeros_like(rounded))
        sums += jnp.dot(mine, values[t], preferred_element_type=F32)
    for g in range(KVH):
        at = slice(group_rows * g, group_rows * (g + 1))
        inside = group_rows * (g % 2)
        parts[g // 2, inside : inside + group_rows, :] = (
            sums[at, HD * g : HD * (g + 1)] + added[at]
        )

    lane = lax.broadcasted_iota(jnp.int32, (QUERIES, HD), 1)
    sheet = jnp.where(lane == 0, maxima, jnp.where(lane == 1, totals, 0.0))
    flat = jnp.transpose(sheet)[0:8]
    for q in range(NY):
        half = flat[:, HD * (q // 2) : HD * (q // 2 + 1)]
        parts[q, OUT_ROWS:, :] = half if q % 2 == 0 else pltpu.roll(half, OUT_ROWS, 1)
    for k in range(2):
        kept[k] = parts[my_x ^ (2 * k)]
        sent[k] = parts[my_x ^ (2 * k + 1)]


def columns_of(rows, sheet):
    sheet[...] = jnp.zeros_like(sheet)
    for k, row in enumerate(rows):
        sheet[k : k + 1, :] = row
    turned = jnp.transpose(sheet[...])[:OUT_ROWS]
    return [turned[:, k : k + 1] for k in range(len(rows))]


def merge_kernel(a, b, kept, sent, sheet):
    line = lax.broadcasted_iota(jnp.int32, (8, HD), 0)
    powers, stats = [], []
    for k in range(2):
        a_stats, b_stats = a[k, OUT_ROWS:, :], b[k, OUT_ROWS:, :]
        highest = jnp.maximum(a_stats[0:1], b_stats[0:1])
        power_a = jnp.exp(a_stats[0:1] - highest)
        power_b = jnp.exp(b_stats[0:1] - highest)
        powers += [power_a, power_b]
        stats.append((highest, a_stats[1:2] * power_a + b_stats[1:2] * power_b))
    factors = columns_of(powers, sheet)
    merged = [
        a[k, :OUT_ROWS, :] * factors[2 * k] + b[k, :OUT_ROWS, :] * factors[2 * k + 1]
        for k in range(2)
    ]
    kept[:OUT_ROWS, :] = merged[0]
    kept[OUT_ROWS:, :] = jnp.where(line == 0, stats[0][0], jnp.where(line == 1, stats[0][1], 0.0))
    sent[:OUT_ROWS, :] = merged[1].astype(BF16)
    high, rest = high_rest(stats[1][0])
    middle, low = high_rest(rest)
    pieces = jnp.zeros((8, HD), F32)
    for k, piece in enumerate((high, middle, low, *high_rest(stats[1][1]))):
        pieces = jnp.where(line == k, piece, pieces)
    sent[OUT_ROWS:, :] = jnp.concatenate([pieces, jnp.zeros_like(pieces)], axis=0).astype(BF16)


def settle_kernel(a, b, out, sheet):
    pieces = b[OUT_ROWS:, :].astype(F32)
    maximum = (pieces[0:1] + pieces[1:2]) + pieces[2:3]
    total = pieces[3:4] + pieces[4:5]
    own_maximum, own_total = a[OUT_ROWS : OUT_ROWS + 1, :], a[OUT_ROWS + 1 : OUT_ROWS + 2, :]
    highest = jnp.maximum(own_maximum, maximum)
    power_a = jnp.exp(own_maximum - highest)
    power_b = jnp.exp(maximum - highest)
    whole = own_total * power_a + total * power_b
    factor_a, factor_b = columns_of([power_a / whole, power_b / whole], sheet)
    out[...] = (a[:OUT_ROWS, :] * factor_a + b[:OUT_ROWS, :].astype(F32) * factor_b).astype(BF16)


def output_kernel(near, far, w, kept, sent, blocks, wide, sums):
    mixed = lax.axis_index("gx") ^ lax.axis_index("gy")
    for core, pair in enumerate((near, far)):
        for k in range(2):
            blocks[mixed ^ (2 * k + core)] = pair[k].astype(F32)
    for shift in range(NY):
        for head in range(OUT_HEADS):
            wide[ROWS * shift : ROWS * (shift + 1), HD * head : HD * (head + 1)] = blocks[
                shift, ROWS * head : ROWS * (head + 1), :
            ]
    left = wide[...].astype(BF16)
    width = 512
    for step in range(w.shape[1] // width):
        part = jnp.dot(left, w[:, width * step : width * (step + 1)], preferred_element_type=F32)
        for chunk in range(width // HD):
            at = (step * (width // HD) + chunk) * ROWS
            for shift in range(NY):
                sums[shift, at : at + ROWS, :] = part[
                    ROWS * shift : ROWS * (shift + 1), HD * chunk : HD * (chunk + 1)
                ]
    for k in range(2):
        kept[k] = sums[k]
        sent[k] = sums[2 + k].astype(BF16)


def finish_kernel(a, b, out, total):
    total[...] = a[...] + b[...].astype(F32)
    for chunk in range(out.shape[2] // HD):
        for timeline in range(2):
            at = ROWS * chunk + 2 * timeline
            out[timeline, :, HD * chunk : HD * (chunk + 1)] = total[at : at + 2, :].astype(BF16)


def rotation(positions):
    halfway = HD // 2
    frequency = ROPE_BASE ** (-2.0 * jnp.arange(halfway, dtype=F32) / HD)
    places = positions[:, None] + jnp.arange(2, dtype=jnp.int32)[None, :]
    angles = places.astype(F32)[:, :, None] * frequency[None, None, :]
    cosine, sine = jnp.cos(angles), jnp.sin(angles)
    return jnp.concatenate([cosine, cosine], axis=2), jnp.concatenate([-sine, sine], axis=2)


def partner(part, axis, distance):
    return lax.ppermute(part, axis, [(k, k ^ distance) for k in range(lax.axis_size(axis))])


def swapped(part):
    pairs = [(x * NY + y, y * NY + x) for x in range(NX) for y in range(NY)]
    return lax.ppermute(part, ("gx", "gy"), pairs)


def paired(part, axis, distance):
    return call(
        pair_kernel,
        "pair",
        jax.ShapeDtypeStruct((2, *part.shape), part.dtype),
        [part, partner(part, axis, distance)],
    )


def small_body(hidden, norm_gain, w_qkv, w_out, k_cache, v_cache, cache_len, positions):
    def shape(*dims, dtype=BF16):
        return jax.ShapeDtypeStruct(dims, dtype)

    def pinned(array):
        return pltpu.with_memory_space_constraint(array, pltpu.VMEM)

    columns = w_out.shape[1]
    features = hidden.shape[2]
    count = columns // HD * ROWS
    w_qkv, w_out, k_cache, v_cache = map(pinned, (w_qkv, w_out, k_cache, v_cache))
    cosine, sine = rotation(positions)

    near = paired(hidden, "gy", 1)
    far = partner(near, "gy", 2)
    squares = call(
        square_kernel, "square", shape(NY * ROWS, HD, dtype=F32), [near, far]
    )
    squares = call(
        add_kernel, "add", shape(NY * ROWS, HD, dtype=F32), [squares, partner(squares, "gx", 1)]
    )
    half = shape(2, QKV_ROWS, HD, dtype=F32)
    kept, sent = call(
        project_kernel,
        "project",
        [half, half],
        [near, far, squares, partner(squares, "gx", 2), norm_gain[None], w_qkv],
        [pltpu.VMEM((NY * ROWS, features), F32), pltpu.VMEM((NY, QKV_ROWS, HD), F32)],
    )
    quarter = shape(QKV_ROWS, HD, dtype=F32)
    kept, sent = call(halve_kernel, "halve", [quarter, quarter], [kept, partner(sent, "gx", 1)])
    block = call(round_kernel, "round", shape(QKV_ROWS, HD), [kept, partner(sent, "gx", 2)])
    near = paired(swapped(block), "gx", 2)
    far = partner(near, "gx", 1)

    half = shape(2, OUT_ROWS + 8, HD, dtype=F32)
    kept, sent = call(
        attend_kernel,
        "attend",
        [half, half],
        [cache_len, near, far, cosine, sine, k_cache, v_cache],
        [
            pltpu.VMEM((NY * QKV_ROWS, HD), F32),
            pltpu.VMEM((2, 8, HD), F32),
            pltpu.VMEM((2, QUERIES, KVH * HD), BF16),
            pltpu.VMEM((NY, OUT_ROWS + 8, HD), F32),
        ],
        scalars=1,
        mib=16,
    )
    kept, sent = call(
        merge_kernel,
        "merge",
        [shape(OUT_ROWS + 8, HD, dtype=F32), shape(OUT_ROWS + 16, HD)],
        [kept, partner(sent, "gx", 1)],
        [pltpu.VMEM((HD, HD), F32)],
    )
    block = call(
        settle_kernel,
        "settle",
        shape(OUT_ROWS, HD),
        [kept, partner(sent, "gx", 2)],
        [pltpu.VMEM((HD, HD), F32)],
    )
    near = paired(swapped(block), "gx", 2)
    far = partner(near, "gx", 1)

    kept, sent = call(
        output_kernel,
        "output",
        [shape(2, count, HD, dtype=F32), shape(2, count, HD)],
        [near, far, w_out],
        [
            pltpu.VMEM((NY, OUT_ROWS, HD), F32),
            pltpu.VMEM((NY * ROWS, w_out.shape[0]), F32),
            pltpu.VMEM((NY, count, HD), F32),
        ],
    )
    kept, sent = call(
        halve_kernel,
        "halve",
        [shape(count, HD, dtype=F32), shape(count, HD)],
        [kept, partner(sent, "gy", 2)],
    )
    return call(
        finish_kernel,
        "finish",
        shape(2, 2, columns),
        [kept, partner(sent, "gy", 1)],
        [pltpu.VMEM((count, HD), F32)],
    )


def solution(mesh):
    small = mesh.shape["gx"] == NX and mesh.shape["gy"] == NY
    body = small_body if small else general_body
    in_specs = (
        P(("group", "gy"), None, "gx"),
        P("gx"),
        P("gx", "gy"),
        P("gy", "gx"),
        P(("group", "gy"), "gx", None),
        P(("group", "gy"), "gx", None),
        P(("group", "gy")),
        P(("group", "gy")),
    )
    out_specs = P(("group", "gy"), None, "gx")
    return jax.shard_map(body, mesh=mesh, in_specs=in_specs, out_specs=out_specs, check_vma=False)
```

```python
import functools

import jax
import jax.numpy as jnp
from jax import lax
from jax.experimental import pallas as pl
from jax.experimental.pallas import tpu as pltpu
from jax.sharding import PartitionSpec as P

D = 8192
H = 64
KVH = 8
HD = 128
SPAN_DEV = 384


NEGATIVE = -1e30
ROPE_BASE = 500000.0
EPSILON = 1e-05


def combined_all(shard, axis, combine):
    everything = jax.tree.map(lambda part: lax.all_gather(part, axis), shard)
    first = jax.tree.map(lambda part: part[0], everything)

    def turn(k, so_far):
        return combine(so_far, jax.tree.map(lambda part: part[k], everything))

    return lax.fori_loop(1, lax.axis_size(axis), turn, first)


def rotate(inputs, positions, offset):
    halfway = HD // 2
    frequency = ROPE_BASE ** (-2.0 * jnp.arange(halfway, dtype=jnp.float32) / HD)
    places = (
        positions[:, None] + offset + jnp.arange(inputs.shape[1], dtype=jnp.int32)[None, :]
    ).astype(jnp.float32)
    angles = places[:, :, None] * frequency[None, None, :]
    cosine = jnp.cos(angles)[:, :, None, :]
    sines = jnp.sin(angles)[:, :, None, :]
    leading = inputs[..., :halfway]
    trailing = inputs[..., halfway:]
    return jnp.concatenate(
        [leading * cosine - trailing * sines, trailing * cosine + leading * sines], axis=-1
    )


def block_terms(scores, usable):
    maxima = jnp.max(jnp.where(usable, scores, NEGATIVE), axis=-1)
    weights = jnp.exp(jnp.where(usable, scores - maxima[..., None], NEGATIVE))
    return (maxima, jnp.sum(weights, axis=-1), weights)


def combine(first_part, second_part):
    maxima_a, totals_a, partials_a = first_part
    maxima_b, totals_b, partials_b = second_part
    highest = jnp.maximum(maxima_a, maxima_b)
    factor_a = jnp.exp(maxima_a - highest)
    factor_b = jnp.exp(maxima_b - highest)
    return (
        highest,
        totals_a * factor_a + totals_b * factor_b,
        partials_a * factor_a[..., None] + partials_b * factor_b[..., None],
    )


def general_body(hidden, norm_gain, w_qkv, w_out, k_cache, v_cache, cache_len, positions):
    timelines_here = hidden.shape[0]
    tokens_here = hidden.shape[1]
    floats = hidden.astype(jnp.float32)
    squares = lax.psum(jnp.sum(floats * floats, axis=-1), "gx")
    normed = (
        floats * lax.rsqrt(squares[..., None] / D + EPSILON) * norm_gain.astype(jnp.float32)
    ).astype(jnp.bfloat16)
    partial_sums = jnp.einsum(
        "rkc,ce->rke",
        lax.all_gather(normed, "gy", axis=0, tiled=True),
        w_qkv,
        preferred_element_type=jnp.float32,
    )
    summed = lax.psum(partial_sums, "gx").astype(jnp.bfloat16)
    projected = lax.all_to_all(summed, "gy", split_axis=0, concat_axis=2, tiled=True)
    widened = projected.astype(jnp.float32)
    queries = rotate(
        widened[..., : H * HD].reshape(timelines_here, tokens_here, H, HD), positions, 0
    ).astype(jnp.bfloat16)
    fresh_keys = rotate(
        widened[..., H * HD : (H + KVH) * HD].reshape(timelines_here, tokens_here, KVH, HD),
        positions,
        0,
    ).astype(jnp.bfloat16)
    fresh_values = projected[..., (H + KVH) * HD :].reshape(timelines_here, tokens_here, KVH, HD)
    grouped = queries.reshape(timelines_here, tokens_here, KVH, H // KVH, HD)
    cached_keys = k_cache.reshape(timelines_here, SPAN_DEV, KVH, HD)
    cached_values = v_cache.reshape(timelines_here, SPAN_DEV, KVH, HD)
    scaling = HD ** (-0.5)
    scores = (
        jnp.einsum("tkgqd,tsgd->tkgqs", grouped, cached_keys, preferred_element_type=jnp.float32)
        * scaling
    )
    slot_ids = lax.axis_index("gx") * SPAN_DEV + jnp.arange(SPAN_DEV, dtype=jnp.int32)
    usable = (slot_ids[None, :] < cache_len[:, None]).reshape(timelines_here, 1, 1, 1, SPAN_DEV)
    maxima, totals, weights = block_terms(scores, usable)
    partials = jnp.einsum(
        "tkgqs,tsgd->tkgqd",
        weights.astype(jnp.bfloat16),
        cached_values,
        preferred_element_type=jnp.float32,
    )
    merged = combined_all((maxima, totals, partials), "gx", combine)
    fresh_scores = (
        jnp.einsum("tkgqd,tjgd->tkgqj", grouped, fresh_keys, preferred_element_type=jnp.float32)
        * scaling
    )
    key_ids = jnp.arange(tokens_here, dtype=jnp.int32)
    allowed = (key_ids[None, :] <= key_ids[:, None]).reshape(1, tokens_here, 1, 1, tokens_here)
    fresh_maxima, fresh_totals, fresh_weights = block_terms(fresh_scores, allowed)
    fresh_partials = jnp.einsum(
        "tkgqj,tjgd->tkgqd",
        fresh_weights.astype(jnp.bfloat16),
        fresh_values,
        preferred_element_type=jnp.float32,
    )
    _, denominator, numerator = combine(merged, (fresh_maxima, fresh_totals, fresh_partials))
    attended = (
        (numerator / denominator[..., None])
        .astype(jnp.bfloat16)
        .reshape(timelines_here, tokens_here, H * HD)
    )
    heads_in = lax.all_to_all(attended, "gy", split_axis=2, concat_axis=0, tiled=True)
    return lax.psum_scatter(
        jnp.einsum("rke,ed->rkd", heads_in, w_out, preferred_element_type=jnp.float32),
        "gy",
        scatter_dimension=0,
        tiled=True,
    ).astype(jnp.bfloat16)


NX = 4
NY = 4
ROWS = 4
QKV_ROWS = (H + 2 * KVH) // NY * ROWS
OUT_HEADS = H // NY
OUT_ROWS = OUT_HEADS * ROWS
QUERIES = H * ROWS
VMEM_SPEC = pl.BlockSpec(memory_space=pltpu.VMEM)
SMEM_SPEC = pl.BlockSpec(memory_space=pltpu.SMEM)
F32 = jnp.float32
BF16 = jnp.bfloat16


def call(kernel, name, out_shape, operands, scratch=(), scalars=0, mib=8):
    many = isinstance(out_shape, (list, tuple))
    return pl.pallas_call(
        kernel,
        in_specs=[SMEM_SPEC] * scalars + [VMEM_SPEC] * (len(operands) - scalars),
        out_specs=[VMEM_SPEC] * len(out_shape) if many else VMEM_SPEC,
        out_shape=out_shape,
        scratch_shapes=list(scratch),
        compiler_params=pltpu.CompilerParams(vmem_limit_bytes=mib << 20),
        name=name,
    )(*operands)


def high_rest(values):
    high = values.astype(BF16).astype(F32)
    return high, values - high


def fetch_kernel(count, *refs):
    sources, outs, done = refs[:count], refs[count : 2 * count], refs[2 * count]
    copies = [
        pltpu.make_async_copy(source, out, done.at[k])
        for k, (source, out) in enumerate(zip(sources, outs))
    ]
    for copy in copies:
        copy.start()
    for copy in copies:
        copy.wait()


def fetch(*arrays):
    size = sum(array.size * array.dtype.itemsize for array in arrays)
    return pl.pallas_call(
        functools.partial(fetch_kernel, len(arrays)),
        in_specs=[pl.BlockSpec(memory_space=pltpu.HBM)] * len(arrays),
        out_specs=[VMEM_SPEC] * len(arrays),
        out_shape=[pltpu.VMEM(array.shape, array.dtype) for array in arrays],
        scratch_shapes=[pltpu.SemaphoreType.DMA((len(arrays),))],
        compiler_params=pltpu.CompilerParams(vmem_limit_bytes=1 << 20),
        cost_estimate=pl.CostEstimate(flops=0, bytes_accessed=size, transcendentals=0),
        name="fetch",
    )(*(pltpu.with_memory_space_constraint(array, pltpu.HBM) for array in arrays))


def square_kernel(h0, h1, h2, h3, out):
    for shift, hidden in enumerate((h0, h1, h2, h3)):
        for timeline in range(2):
            wide = hidden[timeline].astype(F32)
            total = jnp.sum(wide * wide, axis=-1, keepdims=True)
            at = ROWS * shift + 2 * timeline
            out[at : at + 2, :] = jnp.broadcast_to(total, (2, HD))


def project_kernel(h0, h1, h2, h3, s0, s1, s2, s3, gain, w, out, rows):
    for shift, hidden in enumerate((h0, h1, h2, h3)):
        for timeline in range(2):
            at = ROWS * shift + 2 * timeline
            rows[at : at + 2, :] = hidden[timeline].astype(F32)
    squares = ((s0[...] + s1[...]) + (s2[...] + s3[...]))[:, 0:1]
    normed = rows[...] * lax.rsqrt(squares / D + EPSILON) * gain[...].astype(F32)
    normed = normed.astype(BF16)
    width = 512
    for step in range(w.shape[1] // width):
        part = jnp.dot(
            normed, w[:, width * step : width * (step + 1)], preferred_element_type=F32
        )
        for head in range(width // HD):
            at = (step * (width // HD) + head) * ROWS
            for shift in range(NY):
                out[shift, at : at + ROWS, :] = part[
                    ROWS * shift : ROWS * (shift + 1), HD * head : HD * (head + 1)
                ]


def add_kernel(a, b, out):
    out[...] = a[...] + b[...]


def round_kernel(a, b, *outs):
    for shift, out in enumerate(outs):
        out[...] = (a[shift] + b[shift]).astype(BF16)


def attend_kernel(
    lengths, r0, r1, r2, r3, cosine, sine, keys, values, out, projected, turns, spread
):
    my_x = lax.axis_index("gx")
    my_y = lax.axis_index("gy")
    for shift, received in enumerate((r0, r1, r2, r3)):
        at = pl.multiple_of((my_y ^ shift) * QKV_ROWS, 16)
        projected[pl.ds(at, QKV_ROWS), :] = received[...].astype(F32)
    for t in range(4):
        turns[0, 2 * t : 2 * t + 2, :] = cosine[t % 2]
        turns[1, 2 * t : 2 * t + 2, :] = sine[t % 2]
    turned = projected[: QUERIES + KVH * ROWS, :]
    swapped = pltpu.roll(turned, HD // 2, 1)
    turned = (
        turned.reshape(-1, 8, HD) * turns[0][None] + swapped.reshape(-1, 8, HD) * turns[1][None]
    ).reshape(-1, HD)
    queries = turned[:QUERIES].astype(BF16)
    new_keys = turned[QUERIES:].astype(BF16)
    new_values = projected[QUERIES + KVH * ROWS :, :].astype(BF16)

    row = lax.broadcasted_iota(jnp.int32, (QUERIES, 1), 0)
    token = row & 1
    timeline = (row >> 1) & 1
    group_rows = QUERIES // KVH
    spread[...] = jnp.zeros_like(spread)
    scores = jnp.zeros((QUERIES, SPAN_DEV), F32)
    for t in range(2):
        mine = jnp.where(timeline == t, queries, jnp.zeros_like(queries))
        for g in range(KVH):
            at = slice(group_rows * g, group_rows * (g + 1))
            spread[t, at, HD * g : HD * (g + 1)] = mine[at]
        scores += lax.dot_general(
            spread[t], keys[t], (((1,), (1,)), ((), ())), preferred_element_type=F32
        )
    scaling = HD ** (-0.5)
    scores = scores * scaling
    slot = my_x * SPAN_DEV + lax.broadcasted_iota(jnp.int32, (QUERIES, SPAN_DEV), 1)
    usable = slot < jnp.where(timeline == 0, lengths[0], lengths[1])
    maxima = jnp.max(jnp.where(usable, scores, NEGATIVE), axis=-1, keepdims=True)

    wide_queries = queries.astype(F32)
    column = lax.broadcasted_iota(jnp.int32, (QUERIES, KVH * ROWS), 1)
    fresh = []
    for j in range(2):
        pick = jnp.where(column == (row // group_rows) * ROWS + timeline * 2 + j, 1.0, 0.0)
        pick = pick.astype(BF16)
        key = jnp.dot(pick, new_keys, preferred_element_type=F32)
        value = jnp.dot(pick, new_values, preferred_element_type=F32)
        score = jnp.sum(wide_queries * key, axis=-1, keepdims=True) * scaling
        allowed = (token >= j) & (my_x == 0)
        maxima = jnp.maximum(maxima, jnp.where(allowed, score, NEGATIVE))
        fresh.append((score, allowed, value))
    weights = jnp.exp(jnp.where(usable, scores - maxima, NEGATIVE))
    totals = jnp.sum(weights, axis=-1, keepdims=True)
    rounded = weights.astype(BF16)
    added = jnp.zeros((QUERIES, HD), F32)
    for score, allowed, value in fresh:
        weight = jnp.exp(jnp.where(allowed, score - maxima, NEGATIVE))
        totals += weight
        added += weight.astype(BF16).astype(F32) * value
    sums = jnp.zeros((QUERIES, KVH * HD), F32)
    for t in range(2):
        mine = jnp.where(timeline == t, rounded, jnp.zeros_like(rounded))
        sums += jnp.dot(mine, values[t], preferred_element_type=F32)
    for g in range(KVH):
        at = slice(group_rows * g, group_rows * (g + 1))
        out[at, :] = sums[at, HD * g : HD * (g + 1)] + added[at]

    lane = lax.broadcasted_iota(jnp.int32, (QUERIES, HD), 1)
    sheet = jnp.where(lane == 0, maxima, jnp.where(lane == 1, totals, 0.0))
    flat = jnp.transpose(sheet)[0:8]
    out[QUERIES : QUERIES + 8, :] = flat[:, :HD]
    out[QUERIES + 8 : QUERIES + 16, :] = flat[:, HD:]


def factor_columns(rows, sheets):
    columns = []
    for half in range(2):
        sheets[half] = jnp.zeros((HD, HD), F32)
        for k in range(2):
            sheets[half, k : k + 1, :] = rows[half][k]
    turned = [jnp.transpose(sheets[half]) for half in range(2)]
    for k in range(2):
        columns.append(
            jnp.concatenate([turned[half][:, k : k + 1] for half in range(2)], axis=0)
        )
    return columns


def merge_kernel(a, b, kept, sent, sheets):
    rows = []
    for half in range(2):
        at = QUERIES + 8 * half
        highest = jnp.maximum(a[at : at + 1, :], b[at : at + 1, :])
        high, rest = high_rest(highest)
        middle, low = high_rest(rest)
        power_a = jnp.exp(a[at : at + 1, :] - highest)
        power_b = jnp.exp(b[at : at + 1, :] - highest)
        total = a[at + 1 : at + 2, :] * power_a + b[at + 1 : at + 2, :] * power_b
        line = lax.broadcasted_iota(jnp.int32, (8, HD), 0)
        stats = jnp.zeros((8, HD), F32)
        for k, piece in enumerate((high, middle, low, *high_rest(total))):
            stats = jnp.where(line == k, piece, stats)
        kept[at : at + 8, :] = jnp.where(line == 0, highest, jnp.where(line == 1, total, 0.0))
        sheets[half, 0:8, :] = stats
        rows.append((power_a, power_b))
    sent[QUERIES : QUERIES + 16, :] = jnp.concatenate(
        [sheets[0, 0:8, :], sheets[1, 0:8, :]], axis=0
    ).astype(BF16)
    factor_a, factor_b = factor_columns(rows, sheets)
    merged = a[:QUERIES, :] * factor_a + b[:QUERIES, :] * factor_b
    kept[:QUERIES, :] = merged
    sent[:QUERIES, :] = merged.astype(BF16)


def settle_kernel(a, b, o0, o1, o2, o3, attended, sheets):
    my_y = lax.axis_index("gy")
    other = b[QUERIES : QUERIES + 16, :].astype(F32)
    rows = []
    for half in range(2):
        at = QUERIES + 8 * half
        stats = other[8 * half : 8 * half + 8]
        maximum = (stats[0:1] + stats[1:2]) + stats[2:3]
        total = stats[3:4] + stats[4:5]
        own_maximum, own_total = a[at : at + 1, :], a[at + 1 : at + 2, :]
        highest = jnp.maximum(own_maximum, maximum)
        power_a = jnp.exp(own_maximum - highest)
        power_b = jnp.exp(maximum - highest)
        whole = own_total * power_a + total * power_b
        rows.append((power_a / whole, power_b / whole))
    factor_a, factor_b = factor_columns(rows, sheets)
    attended[...] = a[:QUERIES, :] * factor_a + b[:QUERIES, :].astype(F32) * factor_b
    for shift, out in enumerate((o0, o1, o2, o3)):
        at = pl.multiple_of((my_y ^ shift) * OUT_ROWS, OUT_ROWS)
        out[...] = attended[pl.ds(at, OUT_ROWS), :].astype(BF16)


def output_kernel(a0, a1, a2, a3, w, o0, o1, o2, o3, wide, sums):
    for shift, attended in enumerate((a0, a1, a2, a3)):
        block = attended[...].astype(F32)
        for head in range(OUT_HEADS):
            wide[ROWS * shift : ROWS * (shift + 1), HD * head : HD * (head + 1)] = block[
                ROWS * head : ROWS * (head + 1)
            ]
    left = wide[...].astype(BF16)
    width = 512
    for step in range(w.shape[1] // width):
        part = jnp.dot(left, w[:, width * step : width * (step + 1)], preferred_element_type=F32)
        for chunk in range(width // HD):
            at = (step * (width // HD) + chunk) * ROWS
            for shift in range(NY):
                sums[shift, at : at + ROWS, :] = part[
                    ROWS * shift : ROWS * (shift + 1), HD * chunk : HD * (chunk + 1)
                ]
    o0[...] = sums[0]
    for shift, out in ((1, o1), (2, o2), (3, o3)):
        out[...] = sums[shift].astype(BF16)


def finish_kernel(a, b, c, d, out, total):
    total[...] = (a[...] + b[...].astype(F32)) + (c[...].astype(F32) + d[...].astype(F32))
    for chunk in range(out.shape[2] // HD):
        for timeline in range(2):
            at = ROWS * chunk + 2 * timeline
            out[timeline, :, HD * chunk : HD * (chunk + 1)] = total[at : at + 2, :].astype(BF16)


def rotation(positions):
    halfway = HD // 2
    frequency = ROPE_BASE ** (-2.0 * jnp.arange(halfway, dtype=F32) / HD)
    places = positions[:, None] + jnp.arange(2, dtype=jnp.int32)[None, :]
    angles = places.astype(F32)[:, :, None] * frequency[None, None, :]
    cosine, sine = jnp.cos(angles), jnp.sin(angles)
    return jnp.concatenate([cosine, cosine], axis=2), jnp.concatenate([-sine, sine], axis=2)


def partner(part, axis, distance):
    if distance == 0:
        return part
    return lax.ppermute(part, axis, [(k, k ^ distance) for k in range(lax.axis_size(axis))])


def small_body(hidden, norm_gain, w_qkv, w_out, k_cache, v_cache, cache_len, positions):
    def shape(*dims, dtype=BF16):
        return jax.ShapeDtypeStruct(dims, dtype)

    columns = w_out.shape[1]
    features = hidden.shape[2]
    w_qkv, own = fetch(w_qkv, hidden)
    k_cache = pltpu.with_memory_space_constraint(k_cache, pltpu.VMEM)
    v_cache = pltpu.with_memory_space_constraint(v_cache, pltpu.VMEM)
    w_out = pltpu.with_memory_space_constraint(w_out, pltpu.VMEM)
    cosine, sine = rotation(positions)
    hiddens = [own] + [partner(hidden, "gy", y) for y in range(1, NY)]
    squares = call(square_kernel, "square", shape(NY * ROWS, HD, dtype=F32), hiddens)
    squares = [partner(squares, "gx", x) for x in range(NX)]
    sums = call(
        project_kernel,
        "project",
        shape(NY, QKV_ROWS, HD, dtype=F32),
        [*hiddens, *squares, norm_gain[None], w_qkv],
        [pltpu.VMEM((NY * ROWS, features), F32)],
    )
    sums = call(
        add_kernel, "add", shape(NY, QKV_ROWS, HD, dtype=F32), [sums, partner(sums, "gx", 1)]
    )
    blocks = call(
        round_kernel, "round", [shape(QKV_ROWS, HD)] * NY, [sums, partner(sums, "gx", 2)]
    )
    blocks = [partner(block, "gy", y) for y, block in enumerate(blocks)]
    partial = call(
        attend_kernel,
        "attend",
        shape(QUERIES + 16, HD, dtype=F32),
        [cache_len, *blocks, cosine, sine, k_cache, v_cache],
        [
            pltpu.VMEM((NY * QKV_ROWS, HD), F32),
            pltpu.VMEM((2, 8, HD), F32),
            pltpu.VMEM((2, QUERIES, KVH * HD), BF16),
        ],
        scalars=1,
        mib=16,
    )
    kept, sent = call(
        merge_kernel,
        "merge",
        [shape(QUERIES + 16, HD, dtype=F32), shape(QUERIES + 16, HD)],
        [partial, partner(partial, "gx", 1)],
        [pltpu.VMEM((2, HD, HD), F32)],
    )
    blocks = call(
        settle_kernel,
        "settle",
        [shape(OUT_ROWS, HD)] * NY,
        [kept, partner(sent, "gx", 2)],
        [pltpu.VMEM((QUERIES, HD), F32), pltpu.VMEM((2, HD, HD), F32)],
    )
    blocks = [partner(block, "gy", y) for y, block in enumerate(blocks)]
    count = columns // HD * ROWS
    blocks = call(
        output_kernel,
        "output",
        [shape(count, HD, dtype=F32)] + [shape(count, HD)] * (NY - 1),
        [*blocks, w_out],
        [
            pltpu.VMEM((NY * ROWS, w_out.shape[0]), F32),
            pltpu.VMEM((NY, count, HD), F32),
        ],
    )
    blocks = [partner(block, "gy", y) for y, block in enumerate(blocks)]
    return call(
        finish_kernel,
        "finish",
        shape(2, 2, columns),
        blocks,
        [pltpu.VMEM((count, HD), F32)],
    )


def solution(mesh):
    small = mesh.shape["gx"] == NX and mesh.shape["gy"] == NY
    body = small_body if small else general_body
    in_specs = (
        P(("group", "gy"), None, "gx"),
        P("gx"),
        P("gx", "gy"),
        P("gy", "gx"),
        P(("group", "gy"), "gx", None),
        P(("group", "gy"), "gx", None),
        P(("group", "gy")),
        P(("group", "gy")),
    )
    out_specs = P(("group", "gy"), None, "gx")
    return jax.shard_map(body, mesh=mesh, in_specs=in_specs, out_specs=out_specs, check_vma=False)
```

```python
import functools

import jax
import jax.numpy as jnp
from jax import lax
from jax.experimental import pallas as pl
from jax.experimental.pallas import tpu as pltpu
from jax.sharding import PartitionSpec as P

D = 8192
H = 64
KVH = 8
HD = 128
SPAN_DEV = 384


NEGATIVE = -1e30
ROPE_BASE = 500000.0
EPSILON = 1e-05


def combined_all(shard, axis, combine):
    everything = jax.tree.map(lambda part: lax.all_gather(part, axis), shard)
    first = jax.tree.map(lambda part: part[0], everything)

    def turn(k, so_far):
        return combine(so_far, jax.tree.map(lambda part: part[k], everything))

    return lax.fori_loop(1, lax.axis_size(axis), turn, first)


def rotate(inputs, positions, offset):
    halfway = HD // 2
    frequency = ROPE_BASE ** (-2.0 * jnp.arange(halfway, dtype=jnp.float32) / HD)
    places = (
        positions[:, None] + offset + jnp.arange(inputs.shape[1], dtype=jnp.int32)[None, :]
    ).astype(jnp.float32)
    angles = places[:, :, None] * frequency[None, None, :]
    cosine = jnp.cos(angles)[:, :, None, :]
    sines = jnp.sin(angles)[:, :, None, :]
    leading = inputs[..., :halfway]
    trailing = inputs[..., halfway:]
    return jnp.concatenate(
        [leading * cosine - trailing * sines, trailing * cosine + leading * sines], axis=-1
    )


def block_terms(scores, usable):
    maxima = jnp.max(jnp.where(usable, scores, NEGATIVE), axis=-1)
    weights = jnp.exp(jnp.where(usable, scores - maxima[..., None], NEGATIVE))
    return (maxima, jnp.sum(weights, axis=-1), weights)


def combine(first_part, second_part):
    maxima_a, totals_a, partials_a = first_part
    maxima_b, totals_b, partials_b = second_part
    highest = jnp.maximum(maxima_a, maxima_b)
    factor_a = jnp.exp(maxima_a - highest)
    factor_b = jnp.exp(maxima_b - highest)
    return (
        highest,
        totals_a * factor_a + totals_b * factor_b,
        partials_a * factor_a[..., None] + partials_b * factor_b[..., None],
    )


def general_body(hidden, norm_gain, w_qkv, w_out, k_cache, v_cache, cache_len, positions):
    timelines_here = hidden.shape[0]
    tokens_here = hidden.shape[1]
    floats = hidden.astype(jnp.float32)
    squares = lax.psum(jnp.sum(floats * floats, axis=-1), "gx")
    normed = (
        floats * lax.rsqrt(squares[..., None] / D + EPSILON) * norm_gain.astype(jnp.float32)
    ).astype(jnp.bfloat16)
    partial_sums = jnp.einsum(
        "rkc,ce->rke",
        lax.all_gather(normed, "gy", axis=0, tiled=True),
        w_qkv,
        preferred_element_type=jnp.float32,
    )
    summed = lax.psum(partial_sums, "gx").astype(jnp.bfloat16)
    projected = lax.all_to_all(summed, "gy", split_axis=0, concat_axis=2, tiled=True)
    widened = projected.astype(jnp.float32)
    queries = rotate(
        widened[..., : H * HD].reshape(timelines_here, tokens_here, H, HD), positions, 0
    ).astype(jnp.bfloat16)
    fresh_keys = rotate(
        widened[..., H * HD : (H + KVH) * HD].reshape(timelines_here, tokens_here, KVH, HD),
        positions,
        0,
    ).astype(jnp.bfloat16)
    fresh_values = projected[..., (H + KVH) * HD :].reshape(timelines_here, tokens_here, KVH, HD)
    grouped = queries.reshape(timelines_here, tokens_here, KVH, H // KVH, HD)
    cached_keys = k_cache.reshape(timelines_here, SPAN_DEV, KVH, HD)
    cached_values = v_cache.reshape(timelines_here, SPAN_DEV, KVH, HD)
    scaling = HD ** (-0.5)
    scores = (
        jnp.einsum("tkgqd,tsgd->tkgqs", grouped, cached_keys, preferred_element_type=jnp.float32)
        * scaling
    )
    slot_ids = lax.axis_index("gx") * SPAN_DEV + jnp.arange(SPAN_DEV, dtype=jnp.int32)
    usable = (slot_ids[None, :] < cache_len[:, None]).reshape(timelines_here, 1, 1, 1, SPAN_DEV)
    maxima, totals, weights = block_terms(scores, usable)
    partials = jnp.einsum(
        "tkgqs,tsgd->tkgqd",
        weights.astype(jnp.bfloat16),
        cached_values,
        preferred_element_type=jnp.float32,
    )
    merged = combined_all((maxima, totals, partials), "gx", combine)
    fresh_scores = (
        jnp.einsum("tkgqd,tjgd->tkgqj", grouped, fresh_keys, preferred_element_type=jnp.float32)
        * scaling
    )
    key_ids = jnp.arange(tokens_here, dtype=jnp.int32)
    allowed = (key_ids[None, :] <= key_ids[:, None]).reshape(1, tokens_here, 1, 1, tokens_here)
    fresh_maxima, fresh_totals, fresh_weights = block_terms(fresh_scores, allowed)
    fresh_partials = jnp.einsum(
        "tkgqj,tjgd->tkgqd",
        fresh_weights.astype(jnp.bfloat16),
        fresh_values,
        preferred_element_type=jnp.float32,
    )
    _, denominator, numerator = combine(merged, (fresh_maxima, fresh_totals, fresh_partials))
    attended = (
        (numerator / denominator[..., None])
        .astype(jnp.bfloat16)
        .reshape(timelines_here, tokens_here, H * HD)
    )
    heads_in = lax.all_to_all(attended, "gy", split_axis=2, concat_axis=0, tiled=True)
    return lax.psum_scatter(
        jnp.einsum("rke,ed->rkd", heads_in, w_out, preferred_element_type=jnp.float32),
        "gy",
        scatter_dimension=0,
        tiled=True,
    ).astype(jnp.bfloat16)


NX = 4
NY = 4
ROWS = 4
QKV_ROWS = (H + 2 * KVH) // NY * ROWS
OUT_HEADS = H // NY
OUT_ROWS = OUT_HEADS * ROWS
QUERIES = H * ROWS
GROUP_ROWS = QUERIES // KVH
VMEM_SPEC = pl.BlockSpec(memory_space=pltpu.VMEM)
SMEM_SPEC = pl.BlockSpec(memory_space=pltpu.SMEM)
F32 = jnp.float32
BF16 = jnp.bfloat16


def call(kernel, name, out_shape, operands, scratch=(), scalars=0, mib=8):
    many = isinstance(out_shape, (list, tuple))
    return pl.pallas_call(
        kernel,
        in_specs=[SMEM_SPEC] * scalars + [VMEM_SPEC] * (len(operands) - scalars),
        out_specs=[VMEM_SPEC] * len(out_shape) if many else VMEM_SPEC,
        out_shape=out_shape,
        scratch_shapes=list(scratch),
        compiler_params=pltpu.CompilerParams(vmem_limit_bytes=mib << 20),
        name=name,
    )(*operands)


def high_rest(values):
    high = values.astype(BF16).astype(F32)
    return high, values - high


def fetch_kernel(pieces, source, out, done):
    rows = source.shape[0] // pieces
    copies = [
        pltpu.make_async_copy(
            source.at[pl.ds(rows * k, rows)], out.at[pl.ds(rows * k, rows)], done.at[k]
        )
        for k in range(pieces)
    ]
    for copy in copies:
        copy.start()
    for copy in copies:
        copy.wait()


def fetch(array, pieces=8):
    size = array.size * array.dtype.itemsize
    return pl.pallas_call(
        functools.partial(fetch_kernel, pieces),
        in_specs=[pl.BlockSpec(memory_space=pltpu.HBM)],
        out_specs=VMEM_SPEC,
        out_shape=pltpu.VMEM(array.shape, array.dtype),
        scratch_shapes=[pltpu.SemaphoreType.DMA((pieces,))],
        compiler_params=pltpu.CompilerParams(vmem_limit_bytes=1 << 20),
        cost_estimate=pl.CostEstimate(flops=0, bytes_accessed=size, transcendentals=0),
        name="fetch",
    )(pltpu.with_memory_space_constraint(array, pltpu.HBM))


def square_kernel(hidden, out, held):
    out[...] = jnp.zeros_like(out)
    held[...] = hidden[...]
    for timeline in range(2):
        wide = hidden[timeline].astype(F32)
        total = jnp.sum(wide * wide, axis=-1, keepdims=True)
        out[2 * timeline : 2 * timeline + 2, :] = jnp.broadcast_to(total, (2, HD))


def add_kernel(a, b, out):
    out[...] = a[...] + b[...]


def norm_kernel(hidden, a, b, gain, out):
    squares = (a[...] + b[...])[:, 0:1]
    wide_gain = gain[...].astype(F32)
    for timeline in range(2):
        scale = lax.rsqrt(squares[2 * timeline : 2 * timeline + 2] / D + EPSILON)
        out[timeline] = (hidden[timeline].astype(F32) * scale * wide_gain).astype(BF16)


def project_kernel(n0, n1, n2, n3, w, kept, sent, rows, sums):
    core = lax.axis_index("gx") & 1
    for shift, normed in enumerate((n0, n1, n2, n3)):
        for timeline in range(2):
            at = ROWS * shift + 2 * timeline
            rows[at : at + 2, :] = normed[timeline].astype(F32)
    left = rows[...].astype(BF16)
    width = 512
    for step in range(w.shape[1] // width):
        part = jnp.dot(left, w[:, width * step : width * (step + 1)], preferred_element_type=F32)
        for head in range(width // HD):
            at = (step * (width // HD) + head) * ROWS
            for shift in range(NY):
                sums[shift, at : at + ROWS, :] = part[
                    ROWS * shift : ROWS * (shift + 1), HD * head : HD * (head + 1)
                ]
    for k in range(2):
        kept[k] = sums[(3 * k) ^ core]
        sent[k] = sums[(3 * k) ^ core ^ 1]


def chip_kernel(a, b, *outs):
    for k, out in enumerate(outs):
        out[...] = a[k] + b[k]


def round_kernel(a0, b0, a1, b1, out):
    out[0] = (a0[...] + b0[...]).astype(BF16)
    out[1] = (a1[...] + b1[...]).astype(BF16)


def attend_kernel(
    lengths, near, far, cosine, sine, keys, values, kept, sent, projected, turns, table, parts
):
    my_x = lax.axis_index("gx")
    my_y = lax.axis_index("gy")
    core = my_x & 1
    for other, pair in enumerate((near, far)):
        for k in range(2):
            at = pl.multiple_of((my_y ^ (3 * k) ^ core ^ other) * QKV_ROWS, 16)
            projected[pl.ds(at, QKV_ROWS), :] = pair[k].astype(F32)
    for t in range(4):
        turns[0, 2 * t : 2 * t + 2, :] = cosine[t % 2]
        turns[1, 2 * t : 2 * t + 2, :] = sine[t % 2]
    turned = projected[: QUERIES + KVH * ROWS, :]
    swapped = pltpu.roll(turned, HD // 2, 1)
    turned = (
        turned.reshape(-1, 8, HD) * turns[0][None] + swapped.reshape(-1, 8, HD) * turns[1][None]
    ).reshape(-1, HD)
    queries = turned[:QUERIES].astype(BF16)
    new_keys = turned[QUERIES:].astype(BF16)
    new_values = projected[QUERIES + KVH * ROWS :, :].astype(BF16)

    row = lax.broadcasted_iota(jnp.int32, (QUERIES, 1), 0)
    token = row & 1
    timeline = (row >> 1) & 1
    group_rows = GROUP_ROWS
    first = timeline[:GROUP_ROWS] == 0
    for g in range(KVH):
        at = slice(GROUP_ROWS * g, GROUP_ROWS * (g + 1))
        both = [
            lax.dot_general(
                queries[at],
                keys[t, :, HD * g : HD * (g + 1)],
                (((1,), (1,)), ((), ())),
                preferred_element_type=F32,
            )
            for t in range(2)
        ]
        table[at, :] = jnp.where(first, both[0], both[1])
    scaling = HD ** (-0.5)
    scores = table[...] * scaling
    slot = my_x * SPAN_DEV + lax.broadcasted_iota(jnp.int32, (QUERIES, SPAN_DEV), 1)
    usable = slot < jnp.where(timeline == 0, lengths[0], lengths[1])
    maxima = jnp.max(jnp.where(usable, scores, NEGATIVE), axis=-1, keepdims=True)

    wide_queries = queries.astype(F32)
    column = lax.broadcasted_iota(jnp.int32, (QUERIES, KVH * ROWS), 1)
    fresh = []
    for j in range(2):
        pick = jnp.where(column == (row // group_rows) * ROWS + timeline * 2 + j, 1.0, 0.0)
        pick = pick.astype(BF16)
        key = jnp.dot(pick, new_keys, preferred_element_type=F32)
        value = jnp.dot(pick, new_values, preferred_element_type=F32)
        score = jnp.sum(wide_queries * key, axis=-1, keepdims=True) * scaling
        allowed = (token >= j) & (my_x == 0)
        maxima = jnp.maximum(maxima, jnp.where(allowed, score, NEGATIVE))
        fresh.append((score, allowed, value))
    weights = jnp.exp(jnp.where(usable, scores - maxima, NEGATIVE))
    totals = jnp.sum(weights, axis=-1, keepdims=True)
    rounded = weights.astype(BF16)
    added = jnp.zeros((QUERIES, HD), F32)
    for score, allowed, value in fresh:
        weight = jnp.exp(jnp.where(allowed, score - maxima, NEGATIVE))
        totals += weight
        added += weight.astype(BF16).astype(F32) * value
    mine = [jnp.where(timeline == t, rounded, jnp.zeros_like(rounded)) for t in range(2)]
    for g in range(KVH):
        at = slice(GROUP_ROWS * g, GROUP_ROWS * (g + 1))
        total = added[at]
        for t in range(2):
            total += jnp.dot(
                mine[t][at], values[t, :, HD * g : HD * (g + 1)], preferred_element_type=F32
            )
        inside = GROUP_ROWS * (g % 2)
        parts[g // 2, inside : inside + GROUP_ROWS, :] = total

    lane = lax.broadcasted_iota(jnp.int32, (QUERIES, HD), 1)
    sheet = jnp.where(lane == 0, maxima, jnp.where(lane == 1, totals, 0.0))
    flat = jnp.transpose(sheet)[0:8]
    for q in range(NY):
        half = flat[:, HD * (q // 2) : HD * (q // 2 + 1)]
        parts[q, OUT_ROWS:, :] = half if q % 2 == 0 else pltpu.roll(half, OUT_ROWS, 1)
    for k in range(2):
        kept[k] = parts[my_y ^ (3 * k) ^ core]
        sent[k] = parts[my_y ^ (3 * k) ^ core ^ 1]


def columns_of(rows, sheet):
    sheet[...] = jnp.zeros_like(sheet)
    for k, row in enumerate(rows):
        sheet[k : k + 1, :] = row
    turned = jnp.transpose(sheet[...])[:OUT_ROWS]
    return [turned[:, k : k + 1] for k in range(len(rows))]


def merge_kernel(a, b, o0, o1, sheet):
    line = lax.broadcasted_iota(jnp.int32, (8, HD), 0)
    powers, stats = [], []
    for k in range(2):
        a_stats, b_stats = a[k, OUT_ROWS:, :], b[k, OUT_ROWS:, :]
        highest = jnp.maximum(a_stats[0:1], b_stats[0:1])
        power_a = jnp.exp(a_stats[0:1] - highest)
        power_b = jnp.exp(b_stats[0:1] - highest)
        powers += [power_a, power_b]
        stats.append((highest, a_stats[1:2] * power_a + b_stats[1:2] * power_b))
    factors = columns_of(powers, sheet)
    for k, out in enumerate((o0, o1)):
        merged = a[k, :OUT_ROWS, :] * factors[2 * k] + b[k, :OUT_ROWS, :] * factors[2 * k + 1]
        out[:OUT_ROWS, :] = merged.astype(BF16)
        high, rest = high_rest(stats[k][0])
        middle, low = high_rest(rest)
        pieces = jnp.zeros((8, HD), F32)
        for m, piece in enumerate((high, middle, low, *high_rest(stats[k][1]))):
            pieces = jnp.where(line == m, piece, pieces)
        out[OUT_ROWS:, :] = jnp.concatenate([pieces, jnp.zeros_like(pieces)], axis=0).astype(BF16)


def settle_kernel(a0, b0, a1, b1, out, sheet):
    factors = []
    for pair in ((a0, b0), (a1, b1)):
        maxima, totals = [], []
        for part in pair:
            pieces = part[OUT_ROWS:, :].astype(F32)
            maxima.append((pieces[0:1] + pieces[1:2]) + pieces[2:3])
            totals.append(pieces[3:4] + pieces[4:5])
        highest = jnp.maximum(*maxima)
        powers = [jnp.exp(maximum - highest) for maximum in maxima]
        whole = totals[0] * powers[0] + totals[1] * powers[1]
        factors += [power / whole for power in powers]
    columns = columns_of(factors, sheet)
    for k, (a, b) in enumerate(((a0, b0), (a1, b1))):
        attended = a[:OUT_ROWS, :].astype(F32) * columns[2 * k]
        attended += b[:OUT_ROWS, :].astype(F32) * columns[2 * k + 1]
        out[k] = attended.astype(BF16)


def output_kernel(near, far, w, o0, o1, o2, o3, blocks, wide, sums):
    core = lax.axis_index("gx") & 1
    for other, pair in enumerate((near, far)):
        for k in range(2):
            blocks[(3 * k) ^ core ^ other] = pair[k].astype(F32)
    for shift in range(NY):
        for head in range(OUT_HEADS):
            wide[ROWS * shift : ROWS * (shift + 1), HD * head : HD * (head + 1)] = blocks[
                shift, ROWS * head : ROWS * (head + 1), :
            ]
    left = wide[...].astype(BF16)
    width = 512
    for step in range(w.shape[1] // width):
        part = jnp.dot(left, w[:, width * step : width * (step + 1)], preferred_element_type=F32)
        for chunk in range(width // HD):
            at = (step * (width // HD) + chunk) * ROWS
            for shift in range(NY):
                sums[shift, at : at + ROWS, :] = part[
                    ROWS * shift : ROWS * (shift + 1), HD * chunk : HD * (chunk + 1)
                ]
    o0[...] = sums[0]
    for shift, out in ((1, o1), (2, o2), (3, o3)):
        out[...] = sums[shift].astype(BF16)


def finish_kernel(a, b, c, d, out, total):
    total[...] = (a[...] + b[...].astype(F32)) + (c[...].astype(F32) + d[...].astype(F32))
    for chunk in range(out.shape[2] // HD):
        for timeline in range(2):
            at = ROWS * chunk + 2 * timeline
            out[timeline, :, HD * chunk : HD * (chunk + 1)] = total[at : at + 2, :].astype(BF16)


def rotation(positions):
    halfway = HD // 2
    frequency = ROPE_BASE ** (-2.0 * jnp.arange(halfway, dtype=F32) / HD)
    places = positions[:, None] + jnp.arange(2, dtype=jnp.int32)[None, :]
    angles = places.astype(F32)[:, :, None] * frequency[None, None, :]
    cosine, sine = jnp.cos(angles), jnp.sin(angles)
    return jnp.concatenate([cosine, cosine], axis=2), jnp.concatenate([-sine, sine], axis=2)


def partner(part, axis, distance):
    return lax.ppermute(part, axis, [(k, k ^ distance) for k in range(lax.axis_size(axis))])


def on_gy(parts):
    far = {y: partner(parts[y], "gy", y) for y in (3, 2, 1)}
    return [parts[0], far[1], far[2], far[3]]


def on_chips(parts):
    received = {}
    for k in (1, 0):
        for far_x in (1, 0):
            pairs = [
                (x * NY + y, (x ^ (2 * far_x)) * NY + (y ^ (3 * k) ^ (x & 1)))
                for x in range(NX)
                for y in range(NY)
            ]
            received[k, far_x] = lax.ppermute(parts[k], ("gx", "gy"), pairs)
    return [received[k, far_x] for k in range(2) for far_x in range(2)]


def small_body(hidden, norm_gain, w_qkv, w_out, k_cache, v_cache, cache_len, positions):
    def shape(*dims, dtype=BF16):
        return jax.ShapeDtypeStruct(dims, dtype)

    def pinned(array):
        return pltpu.with_memory_space_constraint(array, pltpu.VMEM)

    columns = w_out.shape[1]
    features = hidden.shape[2]
    count = columns // HD * ROWS
    hidden, w_out, k_cache, v_cache = map(pinned, (hidden, w_out, k_cache, v_cache))
    w_qkv = fetch(w_qkv)
    cosine, sine = rotation(positions)

    line = shape(8, HD, dtype=F32)
    squares, hidden = call(square_kernel, "square", [line, shape(*hidden.shape)], [hidden])
    squares = call(add_kernel, "add", line, [squares, partner(squares, "gx", 1)])
    normed = call(
        norm_kernel,
        "norm",
        shape(*hidden.shape),
        [hidden, squares, partner(squares, "gx", 2), norm_gain[None]],
    )
    half = shape(2, QKV_ROWS, HD, dtype=F32)
    kept, sent = call(
        project_kernel,
        "project",
        [half, half],
        [*on_gy([normed] * NY), w_qkv],
        [pltpu.VMEM((NY * ROWS, features), F32), pltpu.VMEM((NY, QKV_ROWS, HD), F32)],
    )
    block = shape(QKV_ROWS, HD, dtype=F32)
    sums = call(chip_kernel, "chip", [block, block], [kept, partner(sent, "gx", 1)])
    near = call(round_kernel, "round", shape(2, QKV_ROWS, HD), on_chips(sums))

    half = shape(2, OUT_ROWS + 8, HD, dtype=F32)
    kept, sent = call(
        attend_kernel,
        "attend",
        [half, half],
        [cache_len, near, partner(near, "gx", 1), cosine, sine, k_cache, v_cache],
        [
            pltpu.VMEM((NY * QKV_ROWS, HD), F32),
            pltpu.VMEM((2, 8, HD), F32),
            pltpu.VMEM((QUERIES, SPAN_DEV), F32),
            pltpu.VMEM((NY, OUT_ROWS + 8, HD), F32),
        ],
        scalars=1,
        mib=16,
    )
    block = shape(OUT_ROWS + 16, HD)
    merged = call(
        merge_kernel,
        "merge",
        [block, block],
        [kept, partner(sent, "gx", 1)],
        [pltpu.VMEM((HD, HD), F32)],
    )
    near = call(
        settle_kernel,
        "settle",
        shape(2, OUT_ROWS, HD),
        on_chips(merged),
        [pltpu.VMEM((HD, HD), F32)],
    )
    blocks = call(
        output_kernel,
        "output",
        [shape(count, HD, dtype=F32)] + [shape(count, HD)] * (NY - 1),
        [near, partner(near, "gx", 1), w_out],
        [
            pltpu.VMEM((NY, OUT_ROWS, HD), F32),
            pltpu.VMEM((NY * ROWS, w_out.shape[0]), F32),
            pltpu.VMEM((NY, count, HD), F32),
        ],
    )
    return call(
        finish_kernel,
        "finish",
        shape(2, 2, columns),
        on_gy(blocks),
        [pltpu.VMEM((count, HD), F32)],
    )


def solution(mesh):
    small = mesh.shape["gx"] == NX and mesh.shape["gy"] == NY
    body = small_body if small else general_body
    in_specs = (
        P(("group", "gy"), None, "gx"),
        P("gx"),
        P("gx", "gy"),
        P("gy", "gx"),
        P(("group", "gy"), "gx", None),
        P(("group", "gy"), "gx", None),
        P(("group", "gy")),
        P(("group", "gy")),
    )
    out_specs = P(("group", "gy"), None, "gx")
    return jax.shard_map(body, mesh=mesh, in_specs=in_specs, out_specs=out_specs, check_vma=False)
```

```python
import jax
import jax.numpy as jnp
from jax import lax
from jax.experimental import pallas as pl
from jax.experimental.pallas import tpu as pltpu
from jax.sharding import PartitionSpec as P

D = 8192
H = 64
KVH = 8
HD = 128
SPAN_DEV = 384


NEGATIVE = -1e30
ROPE_BASE = 500000.0
EPSILON = 1e-05


def combined_all(shard, axis, combine):
    everything = jax.tree.map(lambda part: lax.all_gather(part, axis), shard)
    first = jax.tree.map(lambda part: part[0], everything)

    def turn(k, so_far):
        return combine(so_far, jax.tree.map(lambda part: part[k], everything))

    return lax.fori_loop(1, lax.axis_size(axis), turn, first)


def rotate(inputs, positions, offset):
    halfway = HD // 2
    frequency = ROPE_BASE ** (-2.0 * jnp.arange(halfway, dtype=jnp.float32) / HD)
    places = (
        positions[:, None] + offset + jnp.arange(inputs.shape[1], dtype=jnp.int32)[None, :]
    ).astype(jnp.float32)
    angles = places[:, :, None] * frequency[None, None, :]
    cosine = jnp.cos(angles)[:, :, None, :]
    sines = jnp.sin(angles)[:, :, None, :]
    leading = inputs[..., :halfway]
    trailing = inputs[..., halfway:]
    return jnp.concatenate(
        [leading * cosine - trailing * sines, trailing * cosine + leading * sines], axis=-1
    )


def block_terms(scores, usable):
    maxima = jnp.max(jnp.where(usable, scores, NEGATIVE), axis=-1)
    weights = jnp.exp(jnp.where(usable, scores - maxima[..., None], NEGATIVE))
    return (maxima, jnp.sum(weights, axis=-1), weights)


def combine(first_part, second_part):
    maxima_a, totals_a, partials_a = first_part
    maxima_b, totals_b, partials_b = second_part
    highest = jnp.maximum(maxima_a, maxima_b)
    factor_a = jnp.exp(maxima_a - highest)
    factor_b = jnp.exp(maxima_b - highest)
    return (
        highest,
        totals_a * factor_a + totals_b * factor_b,
        partials_a * factor_a[..., None] + partials_b * factor_b[..., None],
    )


def general_body(hidden, norm_gain, w_qkv, w_out, k_cache, v_cache, cache_len, positions):
    timelines_here = hidden.shape[0]
    tokens_here = hidden.shape[1]
    floats = hidden.astype(jnp.float32)
    squares = lax.psum(jnp.sum(floats * floats, axis=-1), "gx")
    normed = (
        floats * lax.rsqrt(squares[..., None] / D + EPSILON) * norm_gain.astype(jnp.float32)
    ).astype(jnp.bfloat16)
    partial_sums = jnp.einsum(
        "rkc,ce->rke",
        lax.all_gather(normed, "gy", axis=0, tiled=True),
        w_qkv,
        preferred_element_type=jnp.float32,
    )
    summed = lax.psum(partial_sums, "gx").astype(jnp.bfloat16)
    projected = lax.all_to_all(summed, "gy", split_axis=0, concat_axis=2, tiled=True)
    widened = projected.astype(jnp.float32)
    queries = rotate(
        widened[..., : H * HD].reshape(timelines_here, tokens_here, H, HD), positions, 0
    ).astype(jnp.bfloat16)
    fresh_keys = rotate(
        widened[..., H * HD : (H + KVH) * HD].reshape(timelines_here, tokens_here, KVH, HD),
        positions,
        0,
    ).astype(jnp.bfloat16)
    fresh_values = projected[..., (H + KVH) * HD :].reshape(timelines_here, tokens_here, KVH, HD)
    grouped = queries.reshape(timelines_here, tokens_here, KVH, H // KVH, HD)
    cached_keys = k_cache.reshape(timelines_here, SPAN_DEV, KVH, HD)
    cached_values = v_cache.reshape(timelines_here, SPAN_DEV, KVH, HD)
    scaling = HD ** (-0.5)
    scores = (
        jnp.einsum("tkgqd,tsgd->tkgqs", grouped, cached_keys, preferred_element_type=jnp.float32)
        * scaling
    )
    slot_ids = lax.axis_index("gx") * SPAN_DEV + jnp.arange(SPAN_DEV, dtype=jnp.int32)
    usable = (slot_ids[None, :] < cache_len[:, None]).reshape(timelines_here, 1, 1, 1, SPAN_DEV)
    maxima, totals, weights = block_terms(scores, usable)
    partials = jnp.einsum(
        "tkgqs,tsgd->tkgqd",
        weights.astype(jnp.bfloat16),
        cached_values,
        preferred_element_type=jnp.float32,
    )
    merged = combined_all((maxima, totals, partials), "gx", combine)
    fresh_scores = (
        jnp.einsum("tkgqd,tjgd->tkgqj", grouped, fresh_keys, preferred_element_type=jnp.float32)
        * scaling
    )
    key_ids = jnp.arange(tokens_here, dtype=jnp.int32)
    allowed = (key_ids[None, :] <= key_ids[:, None]).reshape(1, tokens_here, 1, 1, tokens_here)
    fresh_maxima, fresh_totals, fresh_weights = block_terms(fresh_scores, allowed)
    fresh_partials = jnp.einsum(
        "tkgqj,tjgd->tkgqd",
        fresh_weights.astype(jnp.bfloat16),
        fresh_values,
        preferred_element_type=jnp.float32,
    )
    _, denominator, numerator = combine(merged, (fresh_maxima, fresh_totals, fresh_partials))
    attended = (
        (numerator / denominator[..., None])
        .astype(jnp.bfloat16)
        .reshape(timelines_here, tokens_here, H * HD)
    )
    heads_in = lax.all_to_all(attended, "gy", split_axis=2, concat_axis=0, tiled=True)
    return lax.psum_scatter(
        jnp.einsum("rke,ed->rkd", heads_in, w_out, preferred_element_type=jnp.float32),
        "gy",
        scatter_dimension=0,
        tiled=True,
    ).astype(jnp.bfloat16)


NX = 4
NY = 4
ROWS = 4
QKV_ROWS = (H + 2 * KVH) // NY * ROWS
OUT_HEADS = H // NY
OUT_ROWS = OUT_HEADS * ROWS
QUERIES = H * ROWS
GROUP_ROWS = QUERIES // KVH
VMEM_SPEC = pl.BlockSpec(memory_space=pltpu.VMEM)
HBM_SPEC = pl.BlockSpec(memory_space=pltpu.HBM)
SMEM_SPEC = pl.BlockSpec(memory_space=pltpu.SMEM)
F32 = jnp.float32
BF16 = jnp.bfloat16


def call(kernel, name, out_shape, operands, scratch=(), scalars=0, mib=8, later=()):
    many = isinstance(out_shape, (list, tuple))
    return pl.pallas_call(
        kernel,
        in_specs=[SMEM_SPEC] * scalars
        + [VMEM_SPEC] * (len(operands) - scalars)
        + [HBM_SPEC] * len(later),
        out_specs=[VMEM_SPEC] * len(out_shape) if many else VMEM_SPEC,
        out_shape=out_shape,
        scratch_shapes=list(scratch),
        compiler_params=pltpu.CompilerParams(vmem_limit_bytes=mib << 20),
        name=name,
    )(*operands, *(pltpu.with_memory_space_constraint(array, pltpu.HBM) for array in later))


def high_rest(values):
    high = values.astype(BF16).astype(F32)
    return high, values - high


def square_kernel(hidden, later, out, held):
    out[...] = jnp.zeros_like(out)
    held[...] = hidden[...]
    for timeline in range(2):
        wide = hidden[timeline].astype(F32)
        total = jnp.sum(wide * wide, axis=-1, keepdims=True)
        out[2 * timeline : 2 * timeline + 2, :] = jnp.broadcast_to(total, (2, HD))


def add_kernel(a, b, out):
    out[...] = a[...] + b[...]


def norm_kernel(hidden, a, b, gain, out):
    squares = (a[...] + b[...])[:, 0:1]
    wide_gain = gain[...].astype(F32)
    for timeline in range(2):
        scale = lax.rsqrt(squares[2 * timeline : 2 * timeline + 2] / D + EPSILON)
        out[timeline] = (hidden[timeline].astype(F32) * scale * wide_gain).astype(BF16)


def project_kernel(n3, n2, n1, n0, w, kept, sent, rows, sums):
    core = lax.axis_index("gx") & 1
    for shift, normed in enumerate((n0, n1, n2, n3)):
        for timeline in range(2):
            at = ROWS * shift + 2 * timeline
            rows[at : at + 2, :] = normed[timeline].astype(F32)
    left = rows[...].astype(BF16)
    width = 512
    for step in range(w.shape[1] // width):
        part = jnp.dot(left, w[:, width * step : width * (step + 1)], preferred_element_type=F32)
        for head in range(width // HD):
            at = (step * (width // HD) + head) * ROWS
            for shift in range(NY):
                sums[shift, at : at + ROWS, :] = part[
                    ROWS * shift : ROWS * (shift + 1), HD * head : HD * (head + 1)
                ]
    for k in range(2):
        kept[k] = sums[(3 * k) ^ core]
        sent[k] = sums[(3 * k) ^ core ^ 1]


def chip_kernel(a, b, *outs):
    for k, out in enumerate(outs):
        out[...] = a[k] + b[k]


def round_kernel(b1, a1, b0, a0, out):
    out[0] = (a0[...] + b0[...]).astype(BF16)
    out[1] = (a1[...] + b1[...]).astype(BF16)


def attend_kernel(
    lengths, near, far, cosine, sine, keys, values, kept, sent, projected, turns, table, parts
):
    my_x = lax.axis_index("gx")
    my_y = lax.axis_index("gy")
    core = my_x & 1
    for other, pair in enumerate((near, far)):
        for k in range(2):
            at = pl.multiple_of((my_y ^ (3 * k) ^ core ^ other) * QKV_ROWS, 16)
            projected[pl.ds(at, QKV_ROWS), :] = pair[k].astype(F32)
    for t in range(4):
        turns[0, 2 * t : 2 * t + 2, :] = cosine[t % 2]
        turns[1, 2 * t : 2 * t + 2, :] = sine[t % 2]
    turned = projected[: QUERIES + KVH * ROWS, :]
    swapped = pltpu.roll(turned, HD // 2, 1)
    turned = (
        turned.reshape(-1, 8, HD) * turns[0][None] + swapped.reshape(-1, 8, HD) * turns[1][None]
    ).reshape(-1, HD)
    queries = turned[:QUERIES].astype(BF16)
    new_keys = turned[QUERIES:].astype(BF16)
    new_values = projected[QUERIES + KVH * ROWS :, :].astype(BF16)

    row = lax.broadcasted_iota(jnp.int32, (QUERIES, 1), 0)
    token = row & 1
    timeline = (row >> 1) & 1
    group_rows = GROUP_ROWS
    first = timeline[:GROUP_ROWS] == 0
    for g in range(KVH):
        at = slice(GROUP_ROWS * g, GROUP_ROWS * (g + 1))
        both = [
            lax.dot_general(
                queries[at],
                keys[t, :, HD * g : HD * (g + 1)],
                (((1,), (1,)), ((), ())),
                preferred_element_type=F32,
            )
            for t in range(2)
        ]
        table[at, :] = jnp.where(first, both[0], both[1])
    scaling = HD ** (-0.5)
    scores = table[...] * scaling
    slot = my_x * SPAN_DEV + lax.broadcasted_iota(jnp.int32, (QUERIES, SPAN_DEV), 1)
    usable = slot < jnp.where(timeline == 0, lengths[0], lengths[1])
    maxima = jnp.max(jnp.where(usable, scores, NEGATIVE), axis=-1, keepdims=True)

    wide_queries = queries.astype(F32)
    column = lax.broadcasted_iota(jnp.int32, (QUERIES, KVH * ROWS), 1)
    fresh = []
    for j in range(2):
        pick = jnp.where(column == (row // group_rows) * ROWS + timeline * 2 + j, 1.0, 0.0)
        pick = pick.astype(BF16)
        key = jnp.dot(pick, new_keys, preferred_element_type=F32)
        value = jnp.dot(pick, new_values, preferred_element_type=F32)
        score = jnp.sum(wide_queries * key, axis=-1, keepdims=True) * scaling
        allowed = (token >= j) & (my_x == 0)
        maxima = jnp.maximum(maxima, jnp.where(allowed, score, NEGATIVE))
        fresh.append((score, allowed, value))
    weights = jnp.exp(jnp.where(usable, scores - maxima, NEGATIVE))
    totals = jnp.sum(weights, axis=-1, keepdims=True)
    rounded = weights.astype(BF16)
    added = jnp.zeros((QUERIES, HD), F32)
    for score, allowed, value in fresh:
        weight = jnp.exp(jnp.where(allowed, score - maxima, NEGATIVE))
        totals += weight
        added += weight.astype(BF16).astype(F32) * value
    mine = [jnp.where(timeline == t, rounded, jnp.zeros_like(rounded)) for t in range(2)]
    for g in range(KVH):
        at = slice(GROUP_ROWS * g, GROUP_ROWS * (g + 1))
        total = added[at]
        for t in range(2):
            total += jnp.dot(
                mine[t][at], values[t, :, HD * g : HD * (g + 1)], preferred_element_type=F32
            )
        inside = GROUP_ROWS * (g % 2)
        parts[g // 2, inside : inside + GROUP_ROWS, :] = total

    lane = lax.broadcasted_iota(jnp.int32, (QUERIES, HD), 1)
    sheet = jnp.where(lane == 0, maxima, jnp.where(lane == 1, totals, 0.0))
    flat = jnp.transpose(sheet)[0:8]
    for q in range(NY):
        half = flat[:, HD * (q // 2) : HD * (q // 2 + 1)]
        parts[q, OUT_ROWS:, :] = half if q % 2 == 0 else pltpu.roll(half, OUT_ROWS, 1)
    for k in range(2):
        kept[k] = parts[my_y ^ (3 * k) ^ core]
        sent[k] = parts[my_y ^ (3 * k) ^ core ^ 1]


def columns_of(rows, sheet):
    sheet[...] = jnp.zeros_like(sheet)
    for k, row in enumerate(rows):
        sheet[k : k + 1, :] = row
    turned = jnp.transpose(sheet[...])[:OUT_ROWS]
    return [turned[:, k : k + 1] for k in range(len(rows))]


def merge_kernel(a, b, o0, o1, sheet):
    line = lax.broadcasted_iota(jnp.int32, (8, HD), 0)
    powers, stats = [], []
    for k in range(2):
        a_stats, b_stats = a[k, OUT_ROWS:, :], b[k, OUT_ROWS:, :]
        highest = jnp.maximum(a_stats[0:1], b_stats[0:1])
        power_a = jnp.exp(a_stats[0:1] - highest)
        power_b = jnp.exp(b_stats[0:1] - highest)
        powers += [power_a, power_b]
        stats.append((highest, a_stats[1:2] * power_a + b_stats[1:2] * power_b))
    factors = columns_of(powers, sheet)
    for k, out in enumerate((o0, o1)):
        merged = a[k, :OUT_ROWS, :] * factors[2 * k] + b[k, :OUT_ROWS, :] * factors[2 * k + 1]
        out[:OUT_ROWS, :] = merged.astype(BF16)
        high, rest = high_rest(stats[k][0])
        middle, low = high_rest(rest)
        pieces = jnp.zeros((8, HD), F32)
        for m, piece in enumerate((high, middle, low, *high_rest(stats[k][1]))):
            pieces = jnp.where(line == m, piece, pieces)
        out[OUT_ROWS:, :] = jnp.concatenate([pieces, jnp.zeros_like(pieces)], axis=0).astype(BF16)


def settle_kernel(b1, a1, b0, a0, out, sheet):
    factors = []
    for pair in ((a0, b0), (a1, b1)):
        maxima, totals = [], []
        for part in pair:
            pieces = part[OUT_ROWS:, :].astype(F32)
            maxima.append((pieces[0:1] + pieces[1:2]) + pieces[2:3])
            totals.append(pieces[3:4] + pieces[4:5])
        highest = jnp.maximum(*maxima)
        powers = [jnp.exp(maximum - highest) for maximum in maxima]
        whole = totals[0] * powers[0] + totals[1] * powers[1]
        factors += [power / whole for power in powers]
    columns = columns_of(factors, sheet)
    for k, (a, b) in enumerate(((a0, b0), (a1, b1))):
        attended = a[:OUT_ROWS, :].astype(F32) * columns[2 * k]
        attended += b[:OUT_ROWS, :].astype(F32) * columns[2 * k + 1]
        out[k] = attended.astype(BF16)


def output_kernel(near, far, w, o0, o1, o2, o3, blocks, wide, sums):
    core = lax.axis_index("gx") & 1
    for other, pair in enumerate((near, far)):
        for k in range(2):
            blocks[(3 * k) ^ core ^ other] = pair[k].astype(F32)
    for shift in range(NY):
        for head in range(OUT_HEADS):
            wide[ROWS * shift : ROWS * (shift + 1), HD * head : HD * (head + 1)] = blocks[
                shift, ROWS * head : ROWS * (head + 1), :
            ]
    left = wide[...].astype(BF16)
    width = 512
    for step in range(w.shape[1] // width):
        part = jnp.dot(left, w[:, width * step : width * (step + 1)], preferred_element_type=F32)
        for chunk in range(width // HD):
            at = (step * (width // HD) + chunk) * ROWS
            for shift in range(NY):
                sums[shift, at : at + ROWS, :] = part[
                    ROWS * shift : ROWS * (shift + 1), HD * chunk : HD * (chunk + 1)
                ]
    o0[...] = sums[0]
    for shift, out in ((1, o1), (2, o2), (3, o3)):
        out[...] = sums[shift].astype(BF16)


def finish_kernel(d, c, b, a, out, total):
    total[...] = (a[...] + b[...].astype(F32)) + (c[...].astype(F32) + d[...].astype(F32))
    for chunk in range(out.shape[2] // HD):
        for timeline in range(2):
            at = ROWS * chunk + 2 * timeline
            out[timeline, :, HD * chunk : HD * (chunk + 1)] = total[at : at + 2, :].astype(BF16)


def rotation(positions):
    halfway = HD // 2
    frequency = ROPE_BASE ** (-2.0 * jnp.arange(halfway, dtype=F32) / HD)
    places = positions[:, None] + jnp.arange(2, dtype=jnp.int32)[None, :]
    angles = places.astype(F32)[:, :, None] * frequency[None, None, :]
    cosine, sine = jnp.cos(angles), jnp.sin(angles)
    return jnp.concatenate([cosine, cosine], axis=2), jnp.concatenate([-sine, sine], axis=2)


def partner(part, axis, distance):
    return lax.ppermute(part, axis, [(k, k ^ distance) for k in range(lax.axis_size(axis))])


def on_gy(parts):
    return [partner(parts[y], "gy", y) if y else parts[y] for y in (3, 2, 1, 0)]


def on_chips(parts):
    received = {}
    for k in (1, 0):
        for far_x in (1, 0):
            pairs = [
                (x * NY + y, (x ^ (2 * far_x)) * NY + (y ^ (3 * k) ^ (x & 1)))
                for x in range(NX)
                for y in range(NY)
            ]
            received[k, far_x] = lax.ppermute(parts[k], ("gx", "gy"), pairs)
    return [received[k, far_x] for k in (1, 0) for far_x in (1, 0)]


def small_body(hidden, norm_gain, w_qkv, w_out, k_cache, v_cache, cache_len, positions):
    def shape(*dims, dtype=BF16):
        return jax.ShapeDtypeStruct(dims, dtype)

    def pinned(array):
        return pltpu.with_memory_space_constraint(array, pltpu.VMEM)

    columns = w_out.shape[1]
    features = hidden.shape[2]
    count = columns // HD * ROWS
    pinned_w_qkv = pinned(w_qkv)
    hidden, w_out, k_cache, v_cache = map(pinned, (hidden, w_out, k_cache, v_cache))
    cosine, sine = rotation(positions)

    line = shape(8, HD, dtype=F32)
    squares, hidden = call(
        square_kernel, "square", [line, shape(*hidden.shape)], [hidden], later=[w_qkv]
    )
    squares = call(add_kernel, "add", line, [squares, partner(squares, "gx", 1)])
    normed = call(
        norm_kernel,
        "norm",
        shape(*hidden.shape),
        [hidden, squares, partner(squares, "gx", 2), norm_gain[None]],
    )
    half = shape(2, QKV_ROWS, HD, dtype=F32)
    kept, sent = call(
        project_kernel,
        "project",
        [half, half],
        [*on_gy([normed] * NY), pinned_w_qkv],
        [pltpu.VMEM((NY * ROWS, features), F32), pltpu.VMEM((NY, QKV_ROWS, HD), F32)],
    )
    block = shape(QKV_ROWS, HD, dtype=F32)
    sums = call(chip_kernel, "chip", [block, block], [kept, partner(sent, "gx", 1)])
    near = call(round_kernel, "round", shape(2, QKV_ROWS, HD), on_chips(sums))

    half = shape(2, OUT_ROWS + 8, HD, dtype=F32)
    kept, sent = call(
        attend_kernel,
        "attend",
        [half, half],
        [cache_len, near, partner(near, "gx", 1), cosine, sine, k_cache, v_cache],
        [
            pltpu.VMEM((NY * QKV_ROWS, HD), F32),
            pltpu.VMEM((2, 8, HD), F32),
            pltpu.VMEM((QUERIES, SPAN_DEV), F32),
            pltpu.VMEM((NY, OUT_ROWS + 8, HD), F32),
        ],
        scalars=1,
        mib=16,
    )
    block = shape(OUT_ROWS + 16, HD)
    merged = call(
        merge_kernel,
        "merge",
        [block, block],
        [kept, partner(sent, "gx", 1)],
        [pltpu.VMEM((HD, HD), F32)],
    )
    near = call(
        settle_kernel,
        "settle",
        shape(2, OUT_ROWS, HD),
        on_chips(merged),
        [pltpu.VMEM((HD, HD), F32)],
    )
    blocks = call(
        output_kernel,
        "output",
        [shape(count, HD, dtype=F32)] + [shape(count, HD)] * (NY - 1),
        [near, partner(near, "gx", 1), w_out],
        [
            pltpu.VMEM((NY, OUT_ROWS, HD), F32),
            pltpu.VMEM((NY * ROWS, w_out.shape[0]), F32),
            pltpu.VMEM((NY, count, HD), F32),
        ],
    )
    return call(
        finish_kernel,
        "finish",
        shape(2, 2, columns),
        on_gy(blocks),
        [pltpu.VMEM((count, HD), F32)],
    )


def solution(mesh):
    small = mesh.shape["gx"] == NX and mesh.shape["gy"] == NY
    body = small_body if small else general_body
    in_specs = (
        P(("group", "gy"), None, "gx"),
        P("gx"),
        P("gx", "gy"),
        P("gy", "gx"),
        P(("group", "gy"), "gx", None),
        P(("group", "gy"), "gx", None),
        P(("group", "gy")),
        P(("group", "gy")),
    )
    out_specs = P(("group", "gy"), None, "gx")
    return jax.shard_map(body, mesh=mesh, in_specs=in_specs, out_specs=out_specs, check_vma=False)
```

```python
import jax
import jax.numpy as jnp
from jax import lax
from jax.experimental import pallas as pl
from jax.experimental.pallas import tpu as pltpu
from jax.sharding import PartitionSpec as P

D = 8192
H = 64
KVH = 8
HD = 128
SPAN_DEV = 384


NEGATIVE = -1e30
ROPE_BASE = 500000.0
EPSILON = 1e-05


def combined_all(shard, axis, combine):
    everything = jax.tree.map(lambda part: lax.all_gather(part, axis), shard)
    first = jax.tree.map(lambda part: part[0], everything)

    def turn(k, so_far):
        return combine(so_far, jax.tree.map(lambda part: part[k], everything))

    return lax.fori_loop(1, lax.axis_size(axis), turn, first)


def rotate(inputs, positions, offset):
    halfway = HD // 2
    frequency = ROPE_BASE ** (-2.0 * jnp.arange(halfway, dtype=jnp.float32) / HD)
    places = (
        positions[:, None] + offset + jnp.arange(inputs.shape[1], dtype=jnp.int32)[None, :]
    ).astype(jnp.float32)
    angles = places[:, :, None] * frequency[None, None, :]
    cosine = jnp.cos(angles)[:, :, None, :]
    sines = jnp.sin(angles)[:, :, None, :]
    leading = inputs[..., :halfway]
    trailing = inputs[..., halfway:]
    return jnp.concatenate(
        [leading * cosine - trailing * sines, trailing * cosine + leading * sines], axis=-1
    )


def block_terms(scores, usable):
    maxima = jnp.max(jnp.where(usable, scores, NEGATIVE), axis=-1)
    weights = jnp.exp(jnp.where(usable, scores - maxima[..., None], NEGATIVE))
    return (maxima, jnp.sum(weights, axis=-1), weights)


def combine(first_part, second_part):
    maxima_a, totals_a, partials_a = first_part
    maxima_b, totals_b, partials_b = second_part
    highest = jnp.maximum(maxima_a, maxima_b)
    factor_a = jnp.exp(maxima_a - highest)
    factor_b = jnp.exp(maxima_b - highest)
    return (
        highest,
        totals_a * factor_a + totals_b * factor_b,
        partials_a * factor_a[..., None] + partials_b * factor_b[..., None],
    )


def general_body(hidden, norm_gain, w_qkv, w_out, k_cache, v_cache, cache_len, positions):
    timelines_here = hidden.shape[0]
    tokens_here = hidden.shape[1]
    floats = hidden.astype(jnp.float32)
    squares = lax.psum(jnp.sum(floats * floats, axis=-1), "gx")
    normed = (
        floats * lax.rsqrt(squares[..., None] / D + EPSILON) * norm_gain.astype(jnp.float32)
    ).astype(jnp.bfloat16)
    partial_sums = jnp.einsum(
        "rkc,ce->rke",
        lax.all_gather(normed, "gy", axis=0, tiled=True),
        w_qkv,
        preferred_element_type=jnp.float32,
    )
    summed = lax.psum(partial_sums, "gx").astype(jnp.bfloat16)
    projected = lax.all_to_all(summed, "gy", split_axis=0, concat_axis=2, tiled=True)
    widened = projected.astype(jnp.float32)
    queries = rotate(
        widened[..., : H * HD].reshape(timelines_here, tokens_here, H, HD), positions, 0
    ).astype(jnp.bfloat16)
    fresh_keys = rotate(
        widened[..., H * HD : (H + KVH) * HD].reshape(timelines_here, tokens_here, KVH, HD),
        positions,
        0,
    ).astype(jnp.bfloat16)
    fresh_values = projected[..., (H + KVH) * HD :].reshape(timelines_here, tokens_here, KVH, HD)
    grouped = queries.reshape(timelines_here, tokens_here, KVH, H // KVH, HD)
    cached_keys = k_cache.reshape(timelines_here, SPAN_DEV, KVH, HD)
    cached_values = v_cache.reshape(timelines_here, SPAN_DEV, KVH, HD)
    scaling = HD ** (-0.5)
    scores = (
        jnp.einsum("tkgqd,tsgd->tkgqs", grouped, cached_keys, preferred_element_type=jnp.float32)
        * scaling
    )
    slot_ids = lax.axis_index("gx") * SPAN_DEV + jnp.arange(SPAN_DEV, dtype=jnp.int32)
    usable = (slot_ids[None, :] < cache_len[:, None]).reshape(timelines_here, 1, 1, 1, SPAN_DEV)
    maxima, totals, weights = block_terms(scores, usable)
    partials = jnp.einsum(
        "tkgqs,tsgd->tkgqd",
        weights.astype(jnp.bfloat16),
        cached_values,
        preferred_element_type=jnp.float32,
    )
    merged = combined_all((maxima, totals, partials), "gx", combine)
    fresh_scores = (
        jnp.einsum("tkgqd,tjgd->tkgqj", grouped, fresh_keys, preferred_element_type=jnp.float32)
        * scaling
    )
    key_ids = jnp.arange(tokens_here, dtype=jnp.int32)
    allowed = (key_ids[None, :] <= key_ids[:, None]).reshape(1, tokens_here, 1, 1, tokens_here)
    fresh_maxima, fresh_totals, fresh_weights = block_terms(fresh_scores, allowed)
    fresh_partials = jnp.einsum(
        "tkgqj,tjgd->tkgqd",
        fresh_weights.astype(jnp.bfloat16),
        fresh_values,
        preferred_element_type=jnp.float32,
    )
    _, denominator, numerator = combine(merged, (fresh_maxima, fresh_totals, fresh_partials))
    attended = (
        (numerator / denominator[..., None])
        .astype(jnp.bfloat16)
        .reshape(timelines_here, tokens_here, H * HD)
    )
    heads_in = lax.all_to_all(attended, "gy", split_axis=2, concat_axis=0, tiled=True)
    return lax.psum_scatter(
        jnp.einsum("rke,ed->rkd", heads_in, w_out, preferred_element_type=jnp.float32),
        "gy",
        scatter_dimension=0,
        tiled=True,
    ).astype(jnp.bfloat16)


NX = 4
NY = 4
ROWS = 4
QKV_ROWS = (H + 2 * KVH) // NY * ROWS
OUT_HEADS = H // NY
OUT_ROWS = OUT_HEADS * ROWS
QUERIES = H * ROWS
GROUP_ROWS = QUERIES // KVH
VMEM_SPEC = pl.BlockSpec(memory_space=pltpu.VMEM)
HBM_SPEC = pl.BlockSpec(memory_space=pltpu.HBM)
SMEM_SPEC = pl.BlockSpec(memory_space=pltpu.SMEM)
F32 = jnp.float32
BF16 = jnp.bfloat16


def call(kernel, name, out_shape, operands, scratch=(), scalars=0, mib=8, later=()):
    many = isinstance(out_shape, (list, tuple))
    return pl.pallas_call(
        kernel,
        in_specs=[SMEM_SPEC] * scalars
        + [VMEM_SPEC] * (len(operands) - scalars)
        + [HBM_SPEC] * len(later),
        out_specs=[VMEM_SPEC] * len(out_shape) if many else VMEM_SPEC,
        out_shape=out_shape,
        scratch_shapes=list(scratch),
        compiler_params=pltpu.CompilerParams(vmem_limit_bytes=mib << 20),
        name=name,
    )(*operands, *(pltpu.with_memory_space_constraint(array, pltpu.HBM) for array in later))


def high_rest(values):
    high = values.astype(BF16).astype(F32)
    return high, values - high


def square_kernel(hidden, other, later, out, held):
    out[...] = jnp.zeros_like(out)
    held[...] = hidden[...]
    for timeline in range(2):
        total = jnp.zeros((2, 1), F32)
        for part in (hidden, other):
            wide = part[timeline].astype(F32)
            total += jnp.sum(wide * wide, axis=-1, keepdims=True)
        out[2 * timeline : 2 * timeline + 2, :] = jnp.broadcast_to(total, (2, HD))


def norm_kernel(hidden, a, b, gain, out):
    squares = (a[...] + b[...])[:, 0:1]
    wide_gain = gain[...].astype(F32)
    for timeline in range(2):
        scale = lax.rsqrt(squares[2 * timeline : 2 * timeline + 2] / D + EPSILON)
        out[timeline] = (hidden[timeline].astype(F32) * scale * wide_gain).astype(BF16)


def project_kernel(n3, n2, n1, n0, w, kept, sent, rows, sums):
    core = lax.axis_index("gx") & 1
    for shift, normed in enumerate((n0, n1, n2, n3)):
        for timeline in range(2):
            at = ROWS * shift + 2 * timeline
            rows[at : at + 2, :] = normed[timeline].astype(F32)
    left = rows[...].astype(BF16)
    width = 512
    for step in range(w.shape[1] // width):
        part = jnp.dot(left, w[:, width * step : width * (step + 1)], preferred_element_type=F32)
        for head in range(width // HD):
            at = (step * (width // HD) + head) * ROWS
            for shift in range(NY):
                sums[shift, at : at + ROWS, :] = part[
                    ROWS * shift : ROWS * (shift + 1), HD * head : HD * (head + 1)
                ]
    for k in range(2):
        kept[k] = sums[(3 * k) ^ core]
        sent[k] = sums[(3 * k) ^ core ^ 1]


def chip_kernel(a, b, *outs):
    for k, out in enumerate(outs):
        out[...] = a[k] + b[k]


def round_kernel(b1, a1, b0, a0, out):
    out[0] = (a0[...] + b0[...]).astype(BF16)
    out[1] = (a1[...] + b1[...]).astype(BF16)


def attend_kernel(
    lengths,
    near,
    far,
    cosine,
    sine,
    keys,
    far_keys,
    values,
    far_values,
    o0,
    o1,
    projected,
    turns,
    table,
    parts,
):
    my_x = lax.axis_index("gx")
    my_y = lax.axis_index("gy")
    core = my_x & 1
    for other, pair in enumerate((near, far)):
        for k in range(2):
            at = pl.multiple_of((my_y ^ (3 * k) ^ core ^ other) * QKV_ROWS, 16)
            projected[pl.ds(at, QKV_ROWS), :] = pair[k].astype(F32)
    for t in range(4):
        turns[0, 2 * t : 2 * t + 2, :] = cosine[t % 2]
        turns[1, 2 * t : 2 * t + 2, :] = sine[t % 2]

    def mine(start, count):
        return projected[pl.ds(pl.multiple_of(start + core * count, 16), count), :]

    def turned(wide):
        swapped = pltpu.roll(wide, HD // 2, 1)
        wide, swapped = wide.reshape(-1, 8, HD), swapped.reshape(-1, 8, HD)
        return (wide * turns[0][None] + swapped * turns[1][None]).reshape(-1, HD).astype(BF16)

    count = QUERIES // 2
    fresh_count = KVH * ROWS // 2
    queries = turned(mine(0, count))
    new_keys = turned(mine(QUERIES, fresh_count))
    new_values = mine(QUERIES + KVH * ROWS, fresh_count).astype(BF16)
    row = lax.broadcasted_iota(jnp.int32, (count, 1), 0)
    token = row & 1
    timeline = (row >> 1) & 1
    first = timeline[:GROUP_ROWS] == 0
    groups = [
        (
            slice(GROUP_ROWS * g, GROUP_ROWS * (g + 1)),
            pl.ds(pl.multiple_of(core * (KVH // 2 * HD) + HD * g, HD), HD),
        )
        for g in range(KVH // 2)
    ]
    for at, lanes in groups:
        for block, cache in enumerate((keys, far_keys)):
            both = [
                lax.dot_general(
                    queries[at],
                    cache[t, :, lanes],
                    (((1,), (1,)), ((), ())),
                    preferred_element_type=F32,
                )
                for t in range(2)
            ]
            table[at, SPAN_DEV * block : SPAN_DEV * (block + 1)] = jnp.where(first, *both)
    scaling = HD ** (-0.5)
    lane = lax.broadcasted_iota(jnp.int32, (1, 2 * SPAN_DEV), 1)
    slot = jnp.where(
        lane < SPAN_DEV, my_x * SPAN_DEV + lane, (my_x ^ 1) * SPAN_DEV + lane - SPAN_DEV
    )
    usable = slot < jnp.where(timeline == 0, lengths[0], lengths[1])
    scores = jnp.where(usable, table[...] * scaling, NEGATIVE)
    maxima = jnp.maximum(jnp.max(scores, axis=-1, keepdims=True), NEGATIVE / 10)

    wide_queries = queries.astype(F32)
    column = lax.broadcasted_iota(jnp.int32, (count, fresh_count), 1)
    fresh = []
    for j in range(2):
        pick = jnp.where(column == (row // GROUP_ROWS) * ROWS + timeline * 2 + j, 1.0, 0.0)
        pick = pick.astype(BF16)
        key = jnp.dot(pick, new_keys, preferred_element_type=F32)
        value = jnp.dot(pick, new_values, preferred_element_type=F32)
        score = jnp.sum(wide_queries * key, axis=-1, keepdims=True) * scaling
        score = jnp.where((token >= j) & (my_x < 2), score, NEGATIVE)
        maxima = jnp.maximum(maxima, score)
        fresh.append((score, value))
    weights = jnp.exp(scores - maxima)
    totals = jnp.sum(weights, axis=-1, keepdims=True)
    rounded = weights.astype(BF16)
    added = jnp.zeros((count, HD), F32)
    for score, value in fresh:
        weight = jnp.exp(score - maxima)
        totals += weight
        added += weight.astype(BF16).astype(F32) * value
    for g, (at, lanes) in enumerate(groups):
        both = [
            sum(
                jnp.dot(
                    rounded[at, SPAN_DEV * block : SPAN_DEV * (block + 1)],
                    cache[t, :, lanes],
                    preferred_element_type=F32,
                )
                for block, cache in enumerate((values, far_values))
            )
            for t in range(2)
        ]
        inside = GROUP_ROWS * (g % 2)
        parts[g // 2, inside : inside + GROUP_ROWS, :] = added[at] + jnp.where(first, *both)

    lane = lax.broadcasted_iota(jnp.int32, (count, HD), 1)
    sheet = jnp.where(lane == 0, maxima, jnp.where(lane == 1, totals, 0.0))
    flat = jnp.transpose(sheet)
    high, rest = high_rest(flat[0:1])
    middle, low = high_rest(rest)
    line = lax.broadcasted_iota(jnp.int32, (16, HD), 0)
    pieces = jnp.zeros((16, HD), F32)
    for m, piece in enumerate((high, middle, low, *high_rest(flat[1:2]))):
        pieces = jnp.where(line == m, piece, pieces)
    parts[0, OUT_ROWS:, :] = pieces
    parts[1, OUT_ROWS:, :] = pltpu.roll(pieces, OUT_ROWS, 1)
    o0[...] = parts[my_y & 1].astype(BF16)
    o1[...] = parts[(my_y & 1) ^ 1].astype(BF16)


def columns_of(rows, sheet):
    sheet[...] = jnp.zeros_like(sheet)
    for k, row in enumerate(rows):
        sheet[k : k + 1, :] = row
    turned = jnp.transpose(sheet[...])[:OUT_ROWS]
    return [turned[:, k : k + 1] for k in range(len(rows))]


def settle_kernel(b1, a1, b0, a0, out, sheet):
    factors = []
    for pair in ((a0, b0), (a1, b1)):
        maxima, totals = [], []
        for part in pair:
            pieces = part[OUT_ROWS:, :].astype(F32)
            maxima.append((pieces[0:1] + pieces[1:2]) + pieces[2:3])
            totals.append(pieces[3:4] + pieces[4:5])
        highest = jnp.maximum(*maxima)
        powers = [jnp.exp(maximum - highest) for maximum in maxima]
        whole = totals[0] * powers[0] + totals[1] * powers[1]
        factors += [power / whole for power in powers]
    columns = columns_of(factors, sheet)
    for k, (a, b) in enumerate(((a0, b0), (a1, b1))):
        attended = a[:OUT_ROWS, :].astype(F32) * columns[2 * k]
        attended += b[:OUT_ROWS, :].astype(F32) * columns[2 * k + 1]
        out[k] = attended.astype(BF16)


def output_kernel(near, far, w, o0, o1, o2, o3, blocks, wide, sums):
    my_y = lax.axis_index("gy")
    core = lax.axis_index("gx") & 1
    for other, pair in enumerate((near, far)):
        for k in range(2):
            source = 2 * (core ^ other) + ((my_y & 1) ^ k)
            blocks[source ^ my_y] = pair[k].astype(F32)
    for shift in range(NY):
        for head in range(OUT_HEADS):
            wide[ROWS * shift : ROWS * (shift + 1), HD * head : HD * (head + 1)] = blocks[
                shift, ROWS * head : ROWS * (head + 1), :
            ]
    left = wide[...].astype(BF16)
    width = 512
    for step in range(w.shape[1] // width):
        part = jnp.dot(left, w[:, width * step : width * (step + 1)], preferred_element_type=F32)
        for chunk in range(width // HD):
            at = (step * (width // HD) + chunk) * ROWS
            for shift in range(NY):
                sums[shift, at : at + ROWS, :] = part[
                    ROWS * shift : ROWS * (shift + 1), HD * chunk : HD * (chunk + 1)
                ]
    o0[...] = sums[0]
    for shift, out in ((1, o1), (2, o2), (3, o3)):
        out[...] = sums[shift].astype(BF16)


def finish_kernel(d, c, b, a, out, total):
    total[...] = (a[...] + b[...].astype(F32)) + (c[...].astype(F32) + d[...].astype(F32))
    for chunk in range(out.shape[2] // HD):
        for timeline in range(2):
            at = ROWS * chunk + 2 * timeline
            out[timeline, :, HD * chunk : HD * (chunk + 1)] = total[at : at + 2, :].astype(BF16)


def rotation(positions):
    halfway = HD // 2
    frequency = ROPE_BASE ** (-2.0 * jnp.arange(halfway, dtype=F32) / HD)
    places = positions[:, None] + jnp.arange(2, dtype=jnp.int32)[None, :]
    angles = places.astype(F32)[:, :, None] * frequency[None, None, :]
    cosine, sine = jnp.cos(angles), jnp.sin(angles)
    return jnp.concatenate([cosine, cosine], axis=2), jnp.concatenate([-sine, sine], axis=2)


def partner(part, axis, distance):
    return lax.ppermute(part, axis, [(k, k ^ distance) for k in range(lax.axis_size(axis))])


def on_gy(parts):
    return [partner(parts[y], "gy", y) if y else parts[y] for y in (3, 2, 1, 0)]


def on_chips(parts, target):
    received = []
    for k in (1, 0):
        for far_x in (2, 0):
            pairs = []
            for x in range(NX):
                for y in range(NY):
                    core, there = target(x & 1, y, k)
                    pairs.append((x * NY + y, ((x & 2 ^ far_x) + core) * NY + there))
            received.append(lax.ppermute(parts[k], ("gx", "gy"), pairs))
    return received


def by_distance(core, y, k):
    return core, y ^ (3 * k) ^ core


def by_heads(core, y, k):
    return y >> 1, 2 * core + ((y & 1) ^ k)


def small_body(hidden, norm_gain, w_qkv, w_out, k_cache, v_cache, cache_len, positions):
    def shape(*dims, dtype=BF16):
        return jax.ShapeDtypeStruct(dims, dtype)

    def pinned(array):
        return pltpu.with_memory_space_constraint(array, pltpu.VMEM)

    columns = w_out.shape[1]
    features = hidden.shape[2]
    count = columns // HD * ROWS
    pinned_w_qkv = pinned(w_qkv)
    w_out = pinned(w_out)
    caches = [(pinned(cache), pinned(partner(cache, "gx", 1))) for cache in (k_cache, v_cache)]
    cosine, sine = rotation(positions)

    line = shape(8, HD, dtype=F32)
    squares, hidden = call(
        square_kernel,
        "square",
        [line, shape(*hidden.shape)],
        [pinned(hidden), partner(hidden, "gx", 1)],
        later=[w_qkv],
    )
    normed = call(
        norm_kernel,
        "norm",
        shape(*hidden.shape),
        [hidden, squares, partner(squares, "gx", 2), norm_gain[None]],
    )
    half = shape(2, QKV_ROWS, HD, dtype=F32)
    kept, sent = call(
        project_kernel,
        "project",
        [half, half],
        [*on_gy([normed] * NY), pinned_w_qkv],
        [pltpu.VMEM((NY * ROWS, features), F32), pltpu.VMEM((NY, QKV_ROWS, HD), F32)],
    )
    block = shape(QKV_ROWS, HD, dtype=F32)
    sums = call(chip_kernel, "chip", [block, block], [kept, partner(sent, "gx", 1)])
    near = call(round_kernel, "round", shape(2, QKV_ROWS, HD), on_chips(sums, by_distance))

    block = shape(OUT_ROWS + 16, HD)
    partials = call(
        attend_kernel,
        "attend",
        [block, block],
        [cache_len, near, partner(near, "gx", 1), cosine, sine, *caches[0], *caches[1]],
        [
            pltpu.VMEM((NY * QKV_ROWS, HD), F32),
            pltpu.VMEM((2, 8, HD), F32),
            pltpu.VMEM((QUERIES // 2, 2 * SPAN_DEV), F32),
            pltpu.VMEM((2, OUT_ROWS + 16, HD), F32),
        ],
        scalars=1,
        mib=16,
    )
    near = call(
        settle_kernel,
        "settle",
        shape(2, OUT_ROWS, HD),
        on_chips(partials, by_heads),
        [pltpu.VMEM((HD, HD), F32)],
    )
    blocks = call(
        output_kernel,
        "output",
        [shape(count, HD, dtype=F32)] + [shape(count, HD)] * (NY - 1),
        [near, partner(near, "gx", 1), w_out],
        [
            pltpu.VMEM((NY, OUT_ROWS, HD), F32),
            pltpu.VMEM((NY * ROWS, w_out.shape[0]), F32),
            pltpu.VMEM((NY, count, HD), F32),
        ],
    )
    return call(
        finish_kernel,
        "finish",
        shape(2, 2, columns),
        on_gy(blocks),
        [pltpu.VMEM((count, HD), F32)],
    )


def solution(mesh):
    small = mesh.shape["gx"] == NX and mesh.shape["gy"] == NY
    body = small_body if small else general_body
    in_specs = (
        P(("group", "gy"), None, "gx"),
        P("gx"),
        P("gx", "gy"),
        P("gy", "gx"),
        P(("group", "gy"), "gx", None),
        P(("group", "gy"), "gx", None),
        P(("group", "gy")),
        P(("group", "gy")),
    )
    out_specs = P(("group", "gy"), None, "gx")
    return jax.shard_map(body, mesh=mesh, in_specs=in_specs, out_specs=out_specs, check_vma=False)
```

```python
import jax
import jax.numpy as jnp
from jax import lax
from jax.experimental import pallas as pl
from jax.experimental.pallas import tpu as pltpu
from jax.sharding import PartitionSpec as P

D = 8192
H = 64
KVH = 8
HD = 128
SPAN_DEV = 384


NEGATIVE = -1e30
ROPE_BASE = 500000.0
EPSILON = 1e-05


def combined_all(shard, axis, combine):
    everything = jax.tree.map(lambda part: lax.all_gather(part, axis), shard)
    first = jax.tree.map(lambda part: part[0], everything)

    def turn(k, so_far):
        return combine(so_far, jax.tree.map(lambda part: part[k], everything))

    return lax.fori_loop(1, lax.axis_size(axis), turn, first)


def rotate(inputs, positions, offset):
    halfway = HD // 2
    frequency = ROPE_BASE ** (-2.0 * jnp.arange(halfway, dtype=jnp.float32) / HD)
    places = (
        positions[:, None] + offset + jnp.arange(inputs.shape[1], dtype=jnp.int32)[None, :]
    ).astype(jnp.float32)
    angles = places[:, :, None] * frequency[None, None, :]
    cosine = jnp.cos(angles)[:, :, None, :]
    sines = jnp.sin(angles)[:, :, None, :]
    leading = inputs[..., :halfway]
    trailing = inputs[..., halfway:]
    return jnp.concatenate(
        [leading * cosine - trailing * sines, trailing * cosine + leading * sines], axis=-1
    )


def block_terms(scores, usable):
    maxima = jnp.max(jnp.where(usable, scores, NEGATIVE), axis=-1)
    weights = jnp.exp(jnp.where(usable, scores - maxima[..., None], NEGATIVE))
    return (maxima, jnp.sum(weights, axis=-1), weights)


def combine(first_part, second_part):
    maxima_a, totals_a, partials_a = first_part
    maxima_b, totals_b, partials_b = second_part
    highest = jnp.maximum(maxima_a, maxima_b)
    factor_a = jnp.exp(maxima_a - highest)
    factor_b = jnp.exp(maxima_b - highest)
    return (
        highest,
        totals_a * factor_a + totals_b * factor_b,
        partials_a * factor_a[..., None] + partials_b * factor_b[..., None],
    )


def general_body(hidden, norm_gain, w_qkv, w_out, k_cache, v_cache, cache_len, positions):
    timelines_here = hidden.shape[0]
    tokens_here = hidden.shape[1]
    floats = hidden.astype(jnp.float32)
    squares = lax.psum(jnp.sum(floats * floats, axis=-1), "gx")
    normed = (
        floats * lax.rsqrt(squares[..., None] / D + EPSILON) * norm_gain.astype(jnp.float32)
    ).astype(jnp.bfloat16)
    partial_sums = jnp.einsum(
        "rkc,ce->rke",
        lax.all_gather(normed, "gy", axis=0, tiled=True),
        w_qkv,
        preferred_element_type=jnp.float32,
    )
    summed = lax.psum(partial_sums, "gx").astype(jnp.bfloat16)
    projected = lax.all_to_all(summed, "gy", split_axis=0, concat_axis=2, tiled=True)
    widened = projected.astype(jnp.float32)
    queries = rotate(
        widened[..., : H * HD].reshape(timelines_here, tokens_here, H, HD), positions, 0
    ).astype(jnp.bfloat16)
    fresh_keys = rotate(
        widened[..., H * HD : (H + KVH) * HD].reshape(timelines_here, tokens_here, KVH, HD),
        positions,
        0,
    ).astype(jnp.bfloat16)
    fresh_values = projected[..., (H + KVH) * HD :].reshape(timelines_here, tokens_here, KVH, HD)
    grouped = queries.reshape(timelines_here, tokens_here, KVH, H // KVH, HD)
    cached_keys = k_cache.reshape(timelines_here, SPAN_DEV, KVH, HD)
    cached_values = v_cache.reshape(timelines_here, SPAN_DEV, KVH, HD)
    scaling = HD ** (-0.5)
    scores = (
        jnp.einsum("tkgqd,tsgd->tkgqs", grouped, cached_keys, preferred_element_type=jnp.float32)
        * scaling
    )
    slot_ids = lax.axis_index("gx") * SPAN_DEV + jnp.arange(SPAN_DEV, dtype=jnp.int32)
    usable = (slot_ids[None, :] < cache_len[:, None]).reshape(timelines_here, 1, 1, 1, SPAN_DEV)
    maxima, totals, weights = block_terms(scores, usable)
    partials = jnp.einsum(
        "tkgqs,tsgd->tkgqd",
        weights.astype(jnp.bfloat16),
        cached_values,
        preferred_element_type=jnp.float32,
    )
    merged = combined_all((maxima, totals, partials), "gx", combine)
    fresh_scores = (
        jnp.einsum("tkgqd,tjgd->tkgqj", grouped, fresh_keys, preferred_element_type=jnp.float32)
        * scaling
    )
    key_ids = jnp.arange(tokens_here, dtype=jnp.int32)
    allowed = (key_ids[None, :] <= key_ids[:, None]).reshape(1, tokens_here, 1, 1, tokens_here)
    fresh_maxima, fresh_totals, fresh_weights = block_terms(fresh_scores, allowed)
    fresh_partials = jnp.einsum(
        "tkgqj,tjgd->tkgqd",
        fresh_weights.astype(jnp.bfloat16),
        fresh_values,
        preferred_element_type=jnp.float32,
    )
    _, denominator, numerator = combine(merged, (fresh_maxima, fresh_totals, fresh_partials))
    attended = (
        (numerator / denominator[..., None])
        .astype(jnp.bfloat16)
        .reshape(timelines_here, tokens_here, H * HD)
    )
    heads_in = lax.all_to_all(attended, "gy", split_axis=2, concat_axis=0, tiled=True)
    return lax.psum_scatter(
        jnp.einsum("rke,ed->rkd", heads_in, w_out, preferred_element_type=jnp.float32),
        "gy",
        scatter_dimension=0,
        tiled=True,
    ).astype(jnp.bfloat16)


NX = 4
NY = 4
ROWS = 4
QKV_ROWS = (H + 2 * KVH) // NY * ROWS
OUT_HEADS = H // NY
OUT_ROWS = OUT_HEADS * ROWS
QUERIES = H * ROWS
GROUP_ROWS = QUERIES // KVH
VMEM_SPEC = pl.BlockSpec(memory_space=pltpu.VMEM)
HBM_SPEC = pl.BlockSpec(memory_space=pltpu.HBM)
SMEM_SPEC = pl.BlockSpec(memory_space=pltpu.SMEM)
F32 = jnp.float32
BF16 = jnp.bfloat16


def call(kernel, name, out_shape, operands, scratch=(), scalars=0, mib=8, later=()):
    many = isinstance(out_shape, (list, tuple))
    return pl.pallas_call(
        kernel,
        in_specs=[SMEM_SPEC] * scalars
        + [VMEM_SPEC] * (len(operands) - scalars)
        + [HBM_SPEC] * len(later),
        out_specs=[VMEM_SPEC] * len(out_shape) if many else VMEM_SPEC,
        out_shape=out_shape,
        scratch_shapes=list(scratch),
        compiler_params=pltpu.CompilerParams(vmem_limit_bytes=mib << 20),
        name=name,
    )(*operands, *(pltpu.with_memory_space_constraint(array, pltpu.HBM) for array in later))


def high_rest(values):
    high = values.astype(BF16).astype(F32)
    return high, values - high


def square_kernel(hidden, other, later, out, held):
    out[...] = jnp.zeros_like(out)
    held[...] = hidden[...]
    for timeline in range(2):
        total = jnp.zeros((2, 1), F32)
        for part in (hidden, other):
            wide = part[timeline].astype(F32)
            total += jnp.sum(wide * wide, axis=-1, keepdims=True)
        out[2 * timeline : 2 * timeline + 2, :] = jnp.broadcast_to(total, (2, HD))


def cut_kernel(squares, keys, values, out, done):
    width = KVH // 2 * HD
    lanes = pl.ds(pl.multiple_of((1 - (lax.axis_index("gx") & 1)) * width, width), width)
    copies = [
        pltpu.make_async_copy(cache.at[t, :, lanes], out.at[k, t], done.at[k, t])
        for k, cache in enumerate((keys, values))
        for t in range(2)
    ]
    for copy in copies:
        copy.start()
    for copy in copies:
        copy.wait()


def norm_kernel(hidden, a, b, gain, out):
    squares = (a[...] + b[...])[:, 0:1]
    wide_gain = gain[...].astype(F32)
    for timeline in range(2):
        scale = lax.rsqrt(squares[2 * timeline : 2 * timeline + 2] / D + EPSILON)
        out[timeline] = (hidden[timeline].astype(F32) * scale * wide_gain).astype(BF16)


def project_kernel(n3, n2, n1, n0, w, later, kept, sent, rows, sums):
    core = lax.axis_index("gx") & 1
    for shift, normed in enumerate((n0, n1, n2, n3)):
        for timeline in range(2):
            at = ROWS * shift + 2 * timeline
            rows[at : at + 2, :] = normed[timeline].astype(F32)
    left = rows[...].astype(BF16)
    width = 512
    for step in range(w.shape[1] // width):
        part = jnp.dot(left, w[:, width * step : width * (step + 1)], preferred_element_type=F32)
        for head in range(width // HD):
            at = (step * (width // HD) + head) * ROWS
            for shift in range(NY):
                sums[shift, at : at + ROWS, :] = part[
                    ROWS * shift : ROWS * (shift + 1), HD * head : HD * (head + 1)
                ]
    for k in range(2):
        kept[k] = sums[(3 * k) ^ core]
        sent[k] = sums[(3 * k) ^ core ^ 1]


def chip_kernel(a, b, *outs):
    for k, out in enumerate(outs):
        out[...] = a[k] + b[k]


def round_kernel(b1, a1, b0, a0, out):
    out[0] = (a0[...] + b0[...]).astype(BF16)
    out[1] = (a1[...] + b1[...]).astype(BF16)


def attend_kernel(
    lengths,
    near,
    far,
    cosine,
    sine,
    keys,
    values,
    far_caches,
    o0,
    o1,
    projected,
    turns,
    table,
    parts,
):
    my_x = lax.axis_index("gx")
    my_y = lax.axis_index("gy")
    core = my_x & 1
    for other, pair in enumerate((near, far)):
        for k in range(2):
            at = pl.multiple_of((my_y ^ (3 * k) ^ core ^ other) * QKV_ROWS, 16)
            projected[pl.ds(at, QKV_ROWS), :] = pair[k].astype(F32)
    for t in range(4):
        turns[0, 2 * t : 2 * t + 2, :] = cosine[t % 2]
        turns[1, 2 * t : 2 * t + 2, :] = sine[t % 2]

    def mine(start, count):
        return projected[pl.ds(pl.multiple_of(start + core * count, 16), count), :]

    def turned(wide):
        swapped = pltpu.roll(wide, HD // 2, 1)
        wide, swapped = wide.reshape(-1, 8, HD), swapped.reshape(-1, 8, HD)
        return (wide * turns[0][None] + swapped * turns[1][None]).reshape(-1, HD).astype(BF16)

    count = QUERIES // 2
    fresh_count = KVH * ROWS // 2
    queries = turned(mine(0, count))
    new_keys = turned(mine(QUERIES, fresh_count))
    new_values = mine(QUERIES + KVH * ROWS, fresh_count).astype(BF16)
    row = lax.broadcasted_iota(jnp.int32, (count, 1), 0)
    token = row & 1
    timeline = (row >> 1) & 1
    first = timeline[:GROUP_ROWS] == 0
    groups = [slice(GROUP_ROWS * g, GROUP_ROWS * (g + 1)) for g in range(KVH // 2)]

    def block_of(g, which, t):
        lanes = pl.ds(pl.multiple_of(core * (KVH // 2 * HD) + HD * g, HD), HD)
        own = (keys, values)[which][t, :, lanes]
        return own, far_caches[which, t, :, HD * g : HD * (g + 1)]

    for g, at in enumerate(groups):
        blocks = [block_of(g, 0, t) for t in range(2)]
        for block in range(2):
            both = [
                lax.dot_general(
                    queries[at],
                    blocks[t][block],
                    (((1,), (1,)), ((), ())),
                    preferred_element_type=F32,
                )
                for t in range(2)
            ]
            table[at, SPAN_DEV * block : SPAN_DEV * (block + 1)] = jnp.where(first, *both)
    scaling = HD ** (-0.5)
    lane = lax.broadcasted_iota(jnp.int32, (1, 2 * SPAN_DEV), 1)
    slot = jnp.where(
        lane < SPAN_DEV, my_x * SPAN_DEV + lane, (my_x ^ 1) * SPAN_DEV + lane - SPAN_DEV
    )
    usable = slot < jnp.where(timeline == 0, lengths[0], lengths[1])
    scores = jnp.where(usable, table[...] * scaling, NEGATIVE)
    maxima = jnp.maximum(jnp.max(scores, axis=-1, keepdims=True), NEGATIVE / 10)

    wide_queries = queries.astype(F32)
    column = lax.broadcasted_iota(jnp.int32, (count, fresh_count), 1)
    fresh = []
    for j in range(2):
        pick = jnp.where(column == (row // GROUP_ROWS) * ROWS + timeline * 2 + j, 1.0, 0.0)
        pick = pick.astype(BF16)
        key = jnp.dot(pick, new_keys, preferred_element_type=F32)
        value = jnp.dot(pick, new_values, preferred_element_type=F32)
        score = jnp.sum(wide_queries * key, axis=-1, keepdims=True) * scaling
        score = jnp.where((token >= j) & (my_x < 2), score, NEGATIVE)
        maxima = jnp.maximum(maxima, score)
        fresh.append((score, value))
    weights = jnp.exp(scores - maxima)
    totals = jnp.sum(weights, axis=-1, keepdims=True)
    rounded = weights.astype(BF16)
    added = jnp.zeros((count, HD), F32)
    for score, value in fresh:
        weight = jnp.exp(score - maxima)
        totals += weight
        added += weight.astype(BF16).astype(F32) * value
    for g, at in enumerate(groups):
        both = [
            sum(
                jnp.dot(
                    rounded[at, SPAN_DEV * block : SPAN_DEV * (block + 1)],
                    part,
                    preferred_element_type=F32,
                )
                for block, part in enumerate(block_of(g, 1, t))
            )
            for t in range(2)
        ]
        inside = GROUP_ROWS * (g % 2)
        parts[g // 2, inside : inside + GROUP_ROWS, :] = added[at] + jnp.where(first, *both)

    lane = lax.broadcasted_iota(jnp.int32, (count, HD), 1)
    sheet = jnp.where(lane == 0, maxima, jnp.where(lane == 1, totals, 0.0))
    flat = jnp.transpose(sheet)
    high, rest = high_rest(flat[0:1])
    middle, low = high_rest(rest)
    line = lax.broadcasted_iota(jnp.int32, (16, HD), 0)
    pieces = jnp.zeros((16, HD), F32)
    for m, piece in enumerate((high, middle, low, *high_rest(flat[1:2]))):
        pieces = jnp.where(line == m, piece, pieces)
    parts[0, OUT_ROWS:, :] = pieces
    parts[1, OUT_ROWS:, :] = pltpu.roll(pieces, OUT_ROWS, 1)
    o0[...] = parts[my_y & 1].astype(BF16)
    o1[...] = parts[(my_y & 1) ^ 1].astype(BF16)


def columns_of(rows, sheet):
    sheet[...] = jnp.zeros_like(sheet)
    for k, row in enumerate(rows):
        sheet[k : k + 1, :] = row
    turned = jnp.transpose(sheet[...])[:OUT_ROWS]
    return [turned[:, k : k + 1] for k in range(len(rows))]


def settle_kernel(b1, a1, b0, a0, out, sheet):
    factors = []
    for pair in ((a0, b0), (a1, b1)):
        maxima, totals = [], []
        for part in pair:
            pieces = part[OUT_ROWS:, :].astype(F32)
            maxima.append((pieces[0:1] + pieces[1:2]) + pieces[2:3])
            totals.append(pieces[3:4] + pieces[4:5])
        highest = jnp.maximum(*maxima)
        powers = [jnp.exp(maximum - highest) for maximum in maxima]
        whole = totals[0] * powers[0] + totals[1] * powers[1]
        factors += [power / whole for power in powers]
    columns = columns_of(factors, sheet)
    for k, (a, b) in enumerate(((a0, b0), (a1, b1))):
        attended = a[:OUT_ROWS, :].astype(F32) * columns[2 * k]
        attended += b[:OUT_ROWS, :].astype(F32) * columns[2 * k + 1]
        out[k] = attended.astype(BF16)


def output_kernel(near, far, w, o0, o1, o2, o3, blocks, wide, sums):
    my_y = lax.axis_index("gy")
    core = lax.axis_index("gx") & 1
    for other, pair in enumerate((near, far)):
        for k in range(2):
            source = 2 * (core ^ other) + ((my_y & 1) ^ k)
            blocks[source ^ my_y] = pair[k].astype(F32)
    for shift in range(NY):
        for head in range(OUT_HEADS):
            wide[ROWS * shift : ROWS * (shift + 1), HD * head : HD * (head + 1)] = blocks[
                shift, ROWS * head : ROWS * (head + 1), :
            ]
    left = wide[...].astype(BF16)
    width = 512
    for step in range(w.shape[1] // width):
        part = jnp.dot(left, w[:, width * step : width * (step + 1)], preferred_element_type=F32)
        for chunk in range(width // HD):
            at = (step * (width // HD) + chunk) * ROWS
            for shift in range(NY):
                sums[shift, at : at + ROWS, :] = part[
                    ROWS * shift : ROWS * (shift + 1), HD * chunk : HD * (chunk + 1)
                ]
    o0[...] = sums[0]
    for shift, out in ((1, o1), (2, o2), (3, o3)):
        out[...] = sums[shift].astype(BF16)


def finish_kernel(d, c, b, a, out, total):
    total[...] = (a[...] + b[...].astype(F32)) + (c[...].astype(F32) + d[...].astype(F32))
    for chunk in range(out.shape[2] // HD):
        for timeline in range(2):
            at = ROWS * chunk + 2 * timeline
            out[timeline, :, HD * chunk : HD * (chunk + 1)] = total[at : at + 2, :].astype(BF16)


def rotation(positions):
    halfway = HD // 2
    frequency = ROPE_BASE ** (-2.0 * jnp.arange(halfway, dtype=F32) / HD)
    places = positions[:, None] + jnp.arange(2, dtype=jnp.int32)[None, :]
    angles = places.astype(F32)[:, :, None] * frequency[None, None, :]
    cosine, sine = jnp.cos(angles), jnp.sin(angles)
    return jnp.concatenate([cosine, cosine], axis=2), jnp.concatenate([-sine, sine], axis=2)


def partner(part, axis, distance):
    return lax.ppermute(part, axis, [(k, k ^ distance) for k in range(lax.axis_size(axis))])


def on_gy(parts):
    return [partner(parts[y], "gy", y) if y else parts[y] for y in (3, 2, 1, 0)]


def on_chips(parts, target):
    received = []
    for k in (1, 0):
        for far_x in (2, 0):
            pairs = []
            for x in range(NX):
                for y in range(NY):
                    core, there = target(x & 1, y, k)
                    pairs.append((x * NY + y, ((x & 2 ^ far_x) + core) * NY + there))
            received.append(lax.ppermute(parts[k], ("gx", "gy"), pairs))
    return received


def by_distance(core, y, k):
    return core, y ^ (3 * k) ^ core


def by_heads(core, y, k):
    return y >> 1, 2 * core + ((y & 1) ^ k)


def small_body(hidden, norm_gain, w_qkv, w_out, k_cache, v_cache, cache_len, positions):
    def shape(*dims, dtype=BF16):
        return jax.ShapeDtypeStruct(dims, dtype)

    def pinned(array):
        return pltpu.with_memory_space_constraint(array, pltpu.VMEM)

    columns = w_out.shape[1]
    features = hidden.shape[2]
    count = columns // HD * ROWS
    pinned_w_qkv = pinned(w_qkv)
    w_out = pinned(w_out)
    pinned_caches = [pinned(k_cache), pinned(v_cache)]
    cosine, sine = rotation(positions)

    line = shape(8, HD, dtype=F32)
    squares, hidden = call(
        square_kernel,
        "square",
        [line, shape(*hidden.shape)],
        [pinned(hidden), partner(hidden, "gx", 1)],
        later=[w_qkv],
    )
    slots = k_cache.shape[1]
    cut = call(
        cut_kernel,
        "cut",
        shape(2, 2, slots, KVH // 2 * HD),
        [squares],
        [pltpu.SemaphoreType.DMA((2, 2))],
        later=[k_cache, v_cache],
    )
    far_caches = pinned(partner(cut, "gx", 1))
    normed = call(
        norm_kernel,
        "norm",
        shape(*hidden.shape),
        [hidden, squares, partner(squares, "gx", 2), norm_gain[None]],
    )
    half = shape(2, QKV_ROWS, HD, dtype=F32)
    kept, sent = call(
        project_kernel,
        "project",
        [half, half],
        [*on_gy([normed] * NY), pinned_w_qkv, far_caches],
        [pltpu.VMEM((NY * ROWS, features), F32), pltpu.VMEM((NY, QKV_ROWS, HD), F32)],
    )
    block = shape(QKV_ROWS, HD, dtype=F32)
    sums = call(chip_kernel, "chip", [block, block], [kept, partner(sent, "gx", 1)])
    near = call(round_kernel, "round", shape(2, QKV_ROWS, HD), on_chips(sums, by_distance))

    block = shape(OUT_ROWS + 16, HD)
    partials = call(
        attend_kernel,
        "attend",
        [block, block],
        [cache_len, near, partner(near, "gx", 1), cosine, sine, *pinned_caches, far_caches],
        [
            pltpu.VMEM((NY * QKV_ROWS, HD), F32),
            pltpu.VMEM((2, 8, HD), F32),
            pltpu.VMEM((QUERIES // 2, 2 * SPAN_DEV), F32),
            pltpu.VMEM((2, OUT_ROWS + 16, HD), F32),
        ],
        scalars=1,
        mib=16,
    )
    near = call(
        settle_kernel,
        "settle",
        shape(2, OUT_ROWS, HD),
        on_chips(partials, by_heads),
        [pltpu.VMEM((HD, HD), F32)],
    )
    blocks = call(
        output_kernel,
        "output",
        [shape(count, HD, dtype=F32)] + [shape(count, HD)] * (NY - 1),
        [near, partner(near, "gx", 1), w_out],
        [
            pltpu.VMEM((NY, OUT_ROWS, HD), F32),
            pltpu.VMEM((NY * ROWS, w_out.shape[0]), F32),
            pltpu.VMEM((NY, count, HD), F32),
        ],
    )
    return call(
        finish_kernel,
        "finish",
        shape(2, 2, columns),
        on_gy(blocks),
        [pltpu.VMEM((count, HD), F32)],
    )


def solution(mesh):
    small = mesh.shape["gx"] == NX and mesh.shape["gy"] == NY
    body = small_body if small else general_body
    in_specs = (
        P(("group", "gy"), None, "gx"),
        P("gx"),
        P("gx", "gy"),
        P("gy", "gx"),
        P(("group", "gy"), "gx", None),
        P(("group", "gy"), "gx", None),
        P(("group", "gy")),
        P(("group", "gy")),
    )
    out_specs = P(("group", "gy"), None, "gx")
    return jax.shard_map(body, mesh=mesh, in_specs=in_specs, out_specs=out_specs, check_vma=False)
```

```python
import jax
import jax.numpy as jnp
from jax import lax
from jax.experimental import pallas as pl
from jax.experimental.pallas import tpu as pltpu
from jax.sharding import PartitionSpec as P

D = 8192
H = 64
KVH = 8
HD = 128
SPAN_DEV = 384


NEGATIVE = -1e30
ROPE_BASE = 500000.0
EPSILON = 1e-05


def combined_all(shard, axis, combine):
    everything = jax.tree.map(lambda part: lax.all_gather(part, axis), shard)
    first = jax.tree.map(lambda part: part[0], everything)

    def turn(k, so_far):
        return combine(so_far, jax.tree.map(lambda part: part[k], everything))

    return lax.fori_loop(1, lax.axis_size(axis), turn, first)


def rotate(inputs, positions, offset):
    halfway = HD // 2
    frequency = ROPE_BASE ** (-2.0 * jnp.arange(halfway, dtype=jnp.float32) / HD)
    places = (
        positions[:, None] + offset + jnp.arange(inputs.shape[1], dtype=jnp.int32)[None, :]
    ).astype(jnp.float32)
    angles = places[:, :, None] * frequency[None, None, :]
    cosine = jnp.cos(angles)[:, :, None, :]
    sines = jnp.sin(angles)[:, :, None, :]
    leading = inputs[..., :halfway]
    trailing = inputs[..., halfway:]
    return jnp.concatenate(
        [leading * cosine - trailing * sines, trailing * cosine + leading * sines], axis=-1
    )


def block_terms(scores, usable):
    maxima = jnp.max(jnp.where(usable, scores, NEGATIVE), axis=-1)
    weights = jnp.exp(jnp.where(usable, scores - maxima[..., None], NEGATIVE))
    return (maxima, jnp.sum(weights, axis=-1), weights)


def combine(first_part, second_part):
    maxima_a, totals_a, partials_a = first_part
    maxima_b, totals_b, partials_b = second_part
    highest = jnp.maximum(maxima_a, maxima_b)
    factor_a = jnp.exp(maxima_a - highest)
    factor_b = jnp.exp(maxima_b - highest)
    return (
        highest,
        totals_a * factor_a + totals_b * factor_b,
        partials_a * factor_a[..., None] + partials_b * factor_b[..., None],
    )


def general_body(hidden, norm_gain, w_qkv, w_out, k_cache, v_cache, cache_len, positions):
    timelines_here = hidden.shape[0]
    tokens_here = hidden.shape[1]
    floats = hidden.astype(jnp.float32)
    squares = lax.psum(jnp.sum(floats * floats, axis=-1), "gx")
    normed = (
        floats * lax.rsqrt(squares[..., None] / D + EPSILON) * norm_gain.astype(jnp.float32)
    ).astype(jnp.bfloat16)
    partial_sums = jnp.einsum(
        "rkc,ce->rke",
        lax.all_gather(normed, "gy", axis=0, tiled=True),
        w_qkv,
        preferred_element_type=jnp.float32,
    )
    summed = lax.psum(partial_sums, "gx").astype(jnp.bfloat16)
    projected = lax.all_to_all(summed, "gy", split_axis=0, concat_axis=2, tiled=True)
    widened = projected.astype(jnp.float32)
    queries = rotate(
        widened[..., : H * HD].reshape(timelines_here, tokens_here, H, HD), positions, 0
    ).astype(jnp.bfloat16)
    fresh_keys = rotate(
        widened[..., H * HD : (H + KVH) * HD].reshape(timelines_here, tokens_here, KVH, HD),
        positions,
        0,
    ).astype(jnp.bfloat16)
    fresh_values = projected[..., (H + KVH) * HD :].reshape(timelines_here, tokens_here, KVH, HD)
    grouped = queries.reshape(timelines_here, tokens_here, KVH, H // KVH, HD)
    cached_keys = k_cache.reshape(timelines_here, SPAN_DEV, KVH, HD)
    cached_values = v_cache.reshape(timelines_here, SPAN_DEV, KVH, HD)
    scaling = HD ** (-0.5)
    scores = (
        jnp.einsum("tkgqd,tsgd->tkgqs", grouped, cached_keys, preferred_element_type=jnp.float32)
        * scaling
    )
    slot_ids = lax.axis_index("gx") * SPAN_DEV + jnp.arange(SPAN_DEV, dtype=jnp.int32)
    usable = (slot_ids[None, :] < cache_len[:, None]).reshape(timelines_here, 1, 1, 1, SPAN_DEV)
    maxima, totals, weights = block_terms(scores, usable)
    partials = jnp.einsum(
        "tkgqs,tsgd->tkgqd",
        weights.astype(jnp.bfloat16),
        cached_values,
        preferred_element_type=jnp.float32,
    )
    merged = combined_all((maxima, totals, partials), "gx", combine)
    fresh_scores = (
        jnp.einsum("tkgqd,tjgd->tkgqj", grouped, fresh_keys, preferred_element_type=jnp.float32)
        * scaling
    )
    key_ids = jnp.arange(tokens_here, dtype=jnp.int32)
    allowed = (key_ids[None, :] <= key_ids[:, None]).reshape(1, tokens_here, 1, 1, tokens_here)
    fresh_maxima, fresh_totals, fresh_weights = block_terms(fresh_scores, allowed)
    fresh_partials = jnp.einsum(
        "tkgqj,tjgd->tkgqd",
        fresh_weights.astype(jnp.bfloat16),
        fresh_values,
        preferred_element_type=jnp.float32,
    )
    _, denominator, numerator = combine(merged, (fresh_maxima, fresh_totals, fresh_partials))
    attended = (
        (numerator / denominator[..., None])
        .astype(jnp.bfloat16)
        .reshape(timelines_here, tokens_here, H * HD)
    )
    heads_in = lax.all_to_all(attended, "gy", split_axis=2, concat_axis=0, tiled=True)
    return lax.psum_scatter(
        jnp.einsum("rke,ed->rkd", heads_in, w_out, preferred_element_type=jnp.float32),
        "gy",
        scatter_dimension=0,
        tiled=True,
    ).astype(jnp.bfloat16)


NX = 4
NY = 4
ROWS = 4
QKV_ROWS = (H + 2 * KVH) // NY * ROWS
OUT_HEADS = H // NY
OUT_ROWS = OUT_HEADS * ROWS
QUERIES = H * ROWS
GROUP_ROWS = QUERIES // KVH
VMEM_SPEC = pl.BlockSpec(memory_space=pltpu.VMEM)
HBM_SPEC = pl.BlockSpec(memory_space=pltpu.HBM)
SMEM_SPEC = pl.BlockSpec(memory_space=pltpu.SMEM)
F32 = jnp.float32
BF16 = jnp.bfloat16


def call(kernel, name, out_shape, operands, scratch=(), scalars=0, mib=8, later=()):
    many = isinstance(out_shape, (list, tuple))
    return pl.pallas_call(
        kernel,
        in_specs=[SMEM_SPEC] * scalars
        + [VMEM_SPEC] * (len(operands) - scalars)
        + [HBM_SPEC] * len(later),
        out_specs=[VMEM_SPEC] * len(out_shape) if many else VMEM_SPEC,
        out_shape=out_shape,
        scratch_shapes=list(scratch),
        compiler_params=pltpu.CompilerParams(vmem_limit_bytes=mib << 20),
        name=name,
    )(*operands, *(pltpu.with_memory_space_constraint(array, pltpu.HBM) for array in later))


def high_rest(values):
    high = values.astype(BF16).astype(F32)
    return high, values - high


def squares_of(hidden, timeline):
    wide = hidden[timeline].astype(F32)
    return jnp.sum(wide * wide, axis=-1, keepdims=True)


def square_kernel(hidden, later, out, held):
    held[...] = hidden[...]
    out[...] = jnp.zeros_like(out)
    for timeline in range(2):
        total = jnp.broadcast_to(squares_of(hidden, timeline), (2, HD))
        out[2 * timeline : 2 * timeline + 2, :] = total


def norm_kernel(h3, h2, h1, h0, squares, gain, out):
    wide_gain = gain[...].astype(F32)
    for timeline in range(2):
        total = squares[2 * timeline : 2 * timeline + 2, 0:1] + squares_of(h1, timeline)
        total += squares_of(h2, timeline) + squares_of(h3, timeline)
        scale = lax.rsqrt(total / D + EPSILON)
        out[timeline] = (h0[timeline].astype(F32) * scale * wide_gain).astype(BF16)


def project_kernel(n3, n2, n1, n0, w, kept, sent, rows, sums):
    core = lax.axis_index("gx") & 1
    for shift, normed in enumerate((n0, n1, n2, n3)):
        for timeline in range(2):
            at = ROWS * shift + 2 * timeline
            rows[at : at + 2, :] = normed[timeline].astype(F32)
    left = rows[...].astype(BF16)
    width = 512
    for step in range(w.shape[1] // width):
        part = jnp.dot(left, w[:, width * step : width * (step + 1)], preferred_element_type=F32)
        for head in range(width // HD):
            at = (step * (width // HD) + head) * ROWS
            for shift in range(NY):
                sums[shift, at : at + ROWS, :] = part[
                    ROWS * shift : ROWS * (shift + 1), HD * head : HD * (head + 1)
                ]
    for k in range(2):
        kept[k] = sums[(3 * k) ^ core]
        sent[k] = sums[(3 * k) ^ core ^ 1]


def chip_kernel(a, b, *outs):
    for k, out in enumerate(outs):
        out[...] = a[k] + b[k]


def round_kernel(b1, a1, b0, a0, out):
    out[0] = (a0[...] + b0[...]).astype(BF16)
    out[1] = (a1[...] + b1[...]).astype(BF16)


def attend_kernel(
    lengths, near, far, cosine, sine, keys, values, kept, sent, projected, turns, table, parts
):
    my_x = lax.axis_index("gx")
    my_y = lax.axis_index("gy")
    core = my_x & 1
    for other, pair in enumerate((near, far)):
        for k in range(2):
            at = pl.multiple_of((my_y ^ (3 * k) ^ core ^ other) * QKV_ROWS, 16)
            projected[pl.ds(at, QKV_ROWS), :] = pair[k].astype(F32)
    for t in range(4):
        turns[0, 2 * t : 2 * t + 2, :] = cosine[t % 2]
        turns[1, 2 * t : 2 * t + 2, :] = sine[t % 2]
    turned = projected[: QUERIES + KVH * ROWS, :]
    swapped = pltpu.roll(turned, HD // 2, 1)
    turned = (
        turned.reshape(-1, 8, HD) * turns[0][None] + swapped.reshape(-1, 8, HD) * turns[1][None]
    ).reshape(-1, HD)
    queries = turned[:QUERIES].astype(BF16)
    new_keys = turned[QUERIES:].astype(BF16)
    new_values = projected[QUERIES + KVH * ROWS :, :].astype(BF16)

    row = lax.broadcasted_iota(jnp.int32, (QUERIES, 1), 0)
    token = row & 1
    timeline = (row >> 1) & 1
    group_rows = GROUP_ROWS
    first = timeline[:GROUP_ROWS] == 0
    for g in range(KVH):
        at = slice(GROUP_ROWS * g, GROUP_ROWS * (g + 1))
        both = [
            lax.dot_general(
                queries[at],
                keys[t, :, HD * g : HD * (g + 1)],
                (((1,), (1,)), ((), ())),
                preferred_element_type=F32,
            )
            for t in range(2)
        ]
        table[at, :] = jnp.where(first, both[0], both[1])
    scaling = HD ** (-0.5)
    slot = my_x * SPAN_DEV + lax.broadcasted_iota(jnp.int32, (QUERIES, SPAN_DEV), 1)
    usable = slot < jnp.where(timeline == 0, lengths[0], lengths[1])
    scores = jnp.where(usable, table[...] * scaling, NEGATIVE)
    maxima = jnp.maximum(jnp.max(scores, axis=-1, keepdims=True), NEGATIVE / 10)

    wide_queries = queries.astype(F32)
    column = lax.broadcasted_iota(jnp.int32, (QUERIES, KVH * ROWS), 1)
    fresh = []
    for j in range(2):
        pick = jnp.where(column == (row // group_rows) * ROWS + timeline * 2 + j, 1.0, 0.0)
        pick = pick.astype(BF16)
        key = jnp.dot(pick, new_keys, preferred_element_type=F32)
        value = jnp.dot(pick, new_values, preferred_element_type=F32)
        score = jnp.sum(wide_queries * key, axis=-1, keepdims=True) * scaling
        allowed = (token >= j) & (my_x == 0)
        maxima = jnp.maximum(maxima, jnp.where(allowed, score, NEGATIVE))
        fresh.append((score, allowed, value))
    weights = jnp.exp(scores - maxima)
    totals = jnp.sum(weights, axis=-1, keepdims=True)
    rounded = weights.astype(BF16)
    added = jnp.zeros((QUERIES, HD), F32)
    for score, allowed, value in fresh:
        weight = jnp.exp(jnp.where(allowed, score - maxima, NEGATIVE))
        totals += weight
        added += weight.astype(BF16).astype(F32) * value
    for g in range(KVH):
        at = slice(GROUP_ROWS * g, GROUP_ROWS * (g + 1))
        both = [
            jnp.dot(rounded[at], values[t, :, HD * g : HD * (g + 1)], preferred_element_type=F32)
            for t in range(2)
        ]
        inside = GROUP_ROWS * (g % 2)
        parts[g // 2, inside : inside + GROUP_ROWS, :] = added[at] + jnp.where(first, *both)

    lane = lax.broadcasted_iota(jnp.int32, (QUERIES, HD), 1)
    sheet = jnp.where(lane == 0, maxima, jnp.where(lane == 1, totals, 0.0))
    flat = jnp.transpose(sheet)[0:8]
    for q in range(NY):
        half = flat[:, HD * (q // 2) : HD * (q // 2 + 1)]
        parts[q, OUT_ROWS:, :] = half if q % 2 == 0 else pltpu.roll(half, OUT_ROWS, 1)
    for k in range(2):
        kept[k] = parts[my_y ^ (3 * k) ^ core]
        sent[k] = parts[my_y ^ (3 * k) ^ core ^ 1]


def columns_of(rows, sheet):
    sheet[...] = jnp.zeros_like(sheet)
    for k, row in enumerate(rows):
        sheet[k : k + 1, :] = row
    turned = jnp.transpose(sheet[...])[:OUT_ROWS]
    return [turned[:, k : k + 1] for k in range(len(rows))]


def merge_kernel(a, b, o0, o1, sheet):
    line = lax.broadcasted_iota(jnp.int32, (8, HD), 0)
    powers, stats = [], []
    for k in range(2):
        a_stats, b_stats = a[k, OUT_ROWS:, :], b[k, OUT_ROWS:, :]
        highest = jnp.maximum(a_stats[0:1], b_stats[0:1])
        power_a = jnp.exp(a_stats[0:1] - highest)
        power_b = jnp.exp(b_stats[0:1] - highest)
        powers += [power_a, power_b]
        stats.append((highest, a_stats[1:2] * power_a + b_stats[1:2] * power_b))
    factors = columns_of(powers, sheet)
    for k, out in enumerate((o0, o1)):
        merged = a[k, :OUT_ROWS, :] * factors[2 * k] + b[k, :OUT_ROWS, :] * factors[2 * k + 1]
        out[:OUT_ROWS, :] = merged.astype(BF16)
        high, rest = high_rest(stats[k][0])
        middle, low = high_rest(rest)
        pieces = jnp.zeros((8, HD), F32)
        for m, piece in enumerate((high, middle, low, *high_rest(stats[k][1]))):
            pieces = jnp.where(line == m, piece, pieces)
        out[OUT_ROWS:, :] = jnp.concatenate([pieces, jnp.zeros_like(pieces)], axis=0).astype(BF16)


def settle_kernel(b1, a1, b0, a0, out, sheet):
    factors = []
    for pair in ((a0, b0), (a1, b1)):
        maxima, totals = [], []
        for part in pair:
            pieces = part[OUT_ROWS:, :].astype(F32)
            maxima.append((pieces[0:1] + pieces[1:2]) + pieces[2:3])
            totals.append(pieces[3:4] + pieces[4:5])
        highest = jnp.maximum(*maxima)
        powers = [jnp.exp(maximum - highest) for maximum in maxima]
        whole = totals[0] * powers[0] + totals[1] * powers[1]
        factors += [power / whole for power in powers]
    columns = columns_of(factors, sheet)
    for k, (a, b) in enumerate(((a0, b0), (a1, b1))):
        attended = a[:OUT_ROWS, :].astype(F32) * columns[2 * k]
        attended += b[:OUT_ROWS, :].astype(F32) * columns[2 * k + 1]
        out[k] = attended.astype(BF16)


def output_kernel(near, far, w, o0, o1, o2, o3, blocks, wide, sums):
    core = lax.axis_index("gx") & 1
    for other, pair in enumerate((near, far)):
        for k in range(2):
            blocks[(3 * k) ^ core ^ other] = pair[k].astype(F32)
    for shift in range(NY):
        for head in range(OUT_HEADS):
            wide[ROWS * shift : ROWS * (shift + 1), HD * head : HD * (head + 1)] = blocks[
                shift, ROWS * head : ROWS * (head + 1), :
            ]
    left = wide[...].astype(BF16)
    width = 512
    for step in range(w.shape[1] // width):
        part = jnp.dot(left, w[:, width * step : width * (step + 1)], preferred_element_type=F32)
        for chunk in range(width // HD):
            at = (step * (width // HD) + chunk) * ROWS
            for shift in range(NY):
                sums[shift, at : at + ROWS, :] = part[
                    ROWS * shift : ROWS * (shift + 1), HD * chunk : HD * (chunk + 1)
                ]
    o0[...] = sums[0]
    for shift, out in ((1, o1), (2, o2), (3, o3)):
        out[...] = sums[shift].astype(BF16)


def finish_kernel(d, c, b, a, out, total):
    total[...] = (a[...] + b[...].astype(F32)) + (c[...].astype(F32) + d[...].astype(F32))
    for chunk in range(out.shape[2] // HD):
        for timeline in range(2):
            at = ROWS * chunk + 2 * timeline
            out[timeline, :, HD * chunk : HD * (chunk + 1)] = total[at : at + 2, :].astype(BF16)


def rotation(positions):
    halfway = HD // 2
    frequency = ROPE_BASE ** (-2.0 * jnp.arange(halfway, dtype=F32) / HD)
    places = positions[:, None] + jnp.arange(2, dtype=jnp.int32)[None, :]
    angles = places.astype(F32)[:, :, None] * frequency[None, None, :]
    cosine, sine = jnp.cos(angles), jnp.sin(angles)
    return jnp.concatenate([cosine, cosine], axis=2), jnp.concatenate([-sine, sine], axis=2)


def partner(part, axis, distance):
    return lax.ppermute(part, axis, [(k, k ^ distance) for k in range(lax.axis_size(axis))])


def on_gy(parts):
    return [partner(parts[y], "gy", y) if y else parts[y] for y in (3, 2, 1, 0)]


def on_chips(parts):
    received = {}
    for k in (1, 0):
        for far_x in (1, 0):
            pairs = [
                (x * NY + y, (x ^ (2 * far_x)) * NY + (y ^ (3 * k) ^ (x & 1)))
                for x in range(NX)
                for y in range(NY)
            ]
            received[k, far_x] = lax.ppermute(parts[k], ("gx", "gy"), pairs)
    return [received[k, far_x] for k in (1, 0) for far_x in (1, 0)]


def small_body(hidden, norm_gain, w_qkv, w_out, k_cache, v_cache, cache_len, positions):
    def shape(*dims, dtype=BF16):
        return jax.ShapeDtypeStruct(dims, dtype)

    def pinned(array):
        return pltpu.with_memory_space_constraint(array, pltpu.VMEM)

    columns = w_out.shape[1]
    features = hidden.shape[2]
    count = columns // HD * ROWS
    pinned_w_qkv = pinned(w_qkv)
    w_out, k_cache, v_cache = map(pinned, (w_out, k_cache, v_cache))
    cosine, sine = rotation(positions)

    others = [partner(hidden, "gx", x) for x in (3, 2, 1)]
    squares, held = call(
        square_kernel,
        "square",
        [shape(8, HD, dtype=F32), shape(*hidden.shape)],
        [pinned(hidden)],
        later=[w_qkv],
    )
    normed = call(
        norm_kernel,
        "norm",
        shape(*hidden.shape),
        [*others, held, squares, norm_gain[None]],
    )
    half = shape(2, QKV_ROWS, HD, dtype=F32)
    kept, sent = call(
        project_kernel,
        "project",
        [half, half],
        [*on_gy([normed] * NY), pinned_w_qkv],
        [pltpu.VMEM((NY * ROWS, features), F32), pltpu.VMEM((NY, QKV_ROWS, HD), F32)],
    )
    block = shape(QKV_ROWS, HD, dtype=F32)
    sums = call(chip_kernel, "chip", [block, block], [kept, partner(sent, "gx", 1)])
    near = call(round_kernel, "round", shape(2, QKV_ROWS, HD), on_chips(sums))

    half = shape(2, OUT_ROWS + 8, HD, dtype=F32)
    kept, sent = call(
        attend_kernel,
        "attend",
        [half, half],
        [cache_len, near, partner(near, "gx", 1), cosine, sine, k_cache, v_cache],
        [
            pltpu.VMEM((NY * QKV_ROWS, HD), F32),
            pltpu.VMEM((2, 8, HD), F32),
            pltpu.VMEM((QUERIES, SPAN_DEV), F32),
            pltpu.VMEM((NY, OUT_ROWS + 8, HD), F32),
        ],
        scalars=1,
        mib=16,
    )
    block = shape(OUT_ROWS + 16, HD)
    merged = call(
        merge_kernel,
        "merge",
        [block, block],
        [kept, partner(sent, "gx", 1)],
        [pltpu.VMEM((HD, HD), F32)],
    )
    near = call(
        settle_kernel,
        "settle",
        shape(2, OUT_ROWS, HD),
        on_chips(merged),
        [pltpu.VMEM((HD, HD), F32)],
    )
    blocks = call(
        output_kernel,
        "output",
        [shape(count, HD, dtype=F32)] + [shape(count, HD)] * (NY - 1),
        [near, partner(near, "gx", 1), w_out],
        [
            pltpu.VMEM((NY, OUT_ROWS, HD), F32),
            pltpu.VMEM((NY * ROWS, w_out.shape[0]), F32),
            pltpu.VMEM((NY, count, HD), F32),
        ],
    )
    return call(
        finish_kernel,
        "finish",
        shape(2, 2, columns),
        on_gy(blocks),
        [pltpu.VMEM((count, HD), F32)],
    )


def solution(mesh):
    small = mesh.shape["gx"] == NX and mesh.shape["gy"] == NY
    body = small_body if small else general_body
    in_specs = (
        P(("group", "gy"), None, "gx"),
        P("gx"),
        P("gx", "gy"),
        P("gy", "gx"),
        P(("group", "gy"), "gx", None),
        P(("group", "gy"), "gx", None),
        P(("group", "gy")),
        P(("group", "gy")),
    )
    out_specs = P(("group", "gy"), None, "gx")
    return jax.shard_map(body, mesh=mesh, in_specs=in_specs, out_specs=out_specs, check_vma=False)
```

```python
import jax
import jax.numpy as jnp
from jax import lax
from jax.experimental import pallas as pl
from jax.experimental.pallas import tpu as pltpu
from jax.sharding import PartitionSpec as P

D = 8192
H = 64
KVH = 8
HD = 128
SPAN_DEV = 384


NEGATIVE = -1e30
ROPE_BASE = 500000.0
EPSILON = 1e-05


def combined_all(shard, axis, combine):
    everything = jax.tree.map(lambda part: lax.all_gather(part, axis), shard)
    first = jax.tree.map(lambda part: part[0], everything)

    def turn(k, so_far):
        return combine(so_far, jax.tree.map(lambda part: part[k], everything))

    return lax.fori_loop(1, lax.axis_size(axis), turn, first)


def rotate(inputs, positions, offset):
    halfway = HD // 2
    frequency = ROPE_BASE ** (-2.0 * jnp.arange(halfway, dtype=jnp.float32) / HD)
    places = (
        positions[:, None] + offset + jnp.arange(inputs.shape[1], dtype=jnp.int32)[None, :]
    ).astype(jnp.float32)
    angles = places[:, :, None] * frequency[None, None, :]
    cosine = jnp.cos(angles)[:, :, None, :]
    sines = jnp.sin(angles)[:, :, None, :]
    leading = inputs[..., :halfway]
    trailing = inputs[..., halfway:]
    return jnp.concatenate(
        [leading * cosine - trailing * sines, trailing * cosine + leading * sines], axis=-1
    )


def block_terms(scores, usable):
    maxima = jnp.max(jnp.where(usable, scores, NEGATIVE), axis=-1)
    weights = jnp.exp(jnp.where(usable, scores - maxima[..., None], NEGATIVE))
    return (maxima, jnp.sum(weights, axis=-1), weights)


def combine(first_part, second_part):
    maxima_a, totals_a, partials_a = first_part
    maxima_b, totals_b, partials_b = second_part
    highest = jnp.maximum(maxima_a, maxima_b)
    factor_a = jnp.exp(maxima_a - highest)
    factor_b = jnp.exp(maxima_b - highest)
    return (
        highest,
        totals_a * factor_a + totals_b * factor_b,
        partials_a * factor_a[..., None] + partials_b * factor_b[..., None],
    )


def general_body(hidden, norm_gain, w_qkv, w_out, k_cache, v_cache, cache_len, positions):
    timelines_here = hidden.shape[0]
    tokens_here = hidden.shape[1]
    floats = hidden.astype(jnp.float32)
    squares = lax.psum(jnp.sum(floats * floats, axis=-1), "gx")
    normed = (
        floats * lax.rsqrt(squares[..., None] / D + EPSILON) * norm_gain.astype(jnp.float32)
    ).astype(jnp.bfloat16)
    partial_sums = jnp.einsum(
        "rkc,ce->rke",
        lax.all_gather(normed, "gy", axis=0, tiled=True),
        w_qkv,
        preferred_element_type=jnp.float32,
    )
    summed = lax.psum(partial_sums, "gx").astype(jnp.bfloat16)
    projected = lax.all_to_all(summed, "gy", split_axis=0, concat_axis=2, tiled=True)
    widened = projected.astype(jnp.float32)
    queries = rotate(
        widened[..., : H * HD].reshape(timelines_here, tokens_here, H, HD), positions, 0
    ).astype(jnp.bfloat16)
    fresh_keys = rotate(
        widened[..., H * HD : (H + KVH) * HD].reshape(timelines_here, tokens_here, KVH, HD),
        positions,
        0,
    ).astype(jnp.bfloat16)
    fresh_values = projected[..., (H + KVH) * HD :].reshape(timelines_here, tokens_here, KVH, HD)
    grouped = queries.reshape(timelines_here, tokens_here, KVH, H // KVH, HD)
    cached_keys = k_cache.reshape(timelines_here, SPAN_DEV, KVH, HD)
    cached_values = v_cache.reshape(timelines_here, SPAN_DEV, KVH, HD)
    scaling = HD ** (-0.5)
    scores = (
        jnp.einsum("tkgqd,tsgd->tkgqs", grouped, cached_keys, preferred_element_type=jnp.float32)
        * scaling
    )
    slot_ids = lax.axis_index("gx") * SPAN_DEV + jnp.arange(SPAN_DEV, dtype=jnp.int32)
    usable = (slot_ids[None, :] < cache_len[:, None]).reshape(timelines_here, 1, 1, 1, SPAN_DEV)
    maxima, totals, weights = block_terms(scores, usable)
    partials = jnp.einsum(
        "tkgqs,tsgd->tkgqd",
        weights.astype(jnp.bfloat16),
        cached_values,
        preferred_element_type=jnp.float32,
    )
    merged = combined_all((maxima, totals, partials), "gx", combine)
    fresh_scores = (
        jnp.einsum("tkgqd,tjgd->tkgqj", grouped, fresh_keys, preferred_element_type=jnp.float32)
        * scaling
    )
    key_ids = jnp.arange(tokens_here, dtype=jnp.int32)
    allowed = (key_ids[None, :] <= key_ids[:, None]).reshape(1, tokens_here, 1, 1, tokens_here)
    fresh_maxima, fresh_totals, fresh_weights = block_terms(fresh_scores, allowed)
    fresh_partials = jnp.einsum(
        "tkgqj,tjgd->tkgqd",
        fresh_weights.astype(jnp.bfloat16),
        fresh_values,
        preferred_element_type=jnp.float32,
    )
    _, denominator, numerator = combine(merged, (fresh_maxima, fresh_totals, fresh_partials))
    attended = (
        (numerator / denominator[..., None])
        .astype(jnp.bfloat16)
        .reshape(timelines_here, tokens_here, H * HD)
    )
    heads_in = lax.all_to_all(attended, "gy", split_axis=2, concat_axis=0, tiled=True)
    return lax.psum_scatter(
        jnp.einsum("rke,ed->rkd", heads_in, w_out, preferred_element_type=jnp.float32),
        "gy",
        scatter_dimension=0,
        tiled=True,
    ).astype(jnp.bfloat16)


NX = 4
NY = 4
ROWS = 4
QKV_ROWS = (H + 2 * KVH) // NY * ROWS
OUT_HEADS = H // NY
OUT_ROWS = OUT_HEADS * ROWS
QUERIES = H * ROWS
GROUP_ROWS = QUERIES // KVH
VMEM_SPEC = pl.BlockSpec(memory_space=pltpu.VMEM)
HBM_SPEC = pl.BlockSpec(memory_space=pltpu.HBM)
F32 = jnp.float32
BF16 = jnp.bfloat16


def call(kernel, name, out_shape, operands, scratch=(), mib=8, later=()):
    many = isinstance(out_shape, (list, tuple))
    return pl.pallas_call(
        kernel,
        in_specs=[VMEM_SPEC] * len(operands) + [HBM_SPEC] * len(later),
        out_specs=[VMEM_SPEC] * len(out_shape) if many else VMEM_SPEC,
        out_shape=out_shape,
        scratch_shapes=list(scratch),
        compiler_params=pltpu.CompilerParams(vmem_limit_bytes=mib << 20),
        name=name,
    )(*operands, *(pltpu.with_memory_space_constraint(array, pltpu.HBM) for array in later))


def high_rest(values):
    high = values.astype(BF16).astype(F32)
    return high, values - high


def squares_of(hidden, timeline):
    wide = hidden[timeline].astype(F32)
    return jnp.sum(wide * wide, axis=-1, keepdims=True)


def square_kernel(hidden, out, held):
    held[...] = hidden[...]
    out[...] = jnp.zeros_like(out)
    for timeline in range(2):
        total = jnp.broadcast_to(squares_of(hidden, timeline), (2, HD))
        out[2 * timeline : 2 * timeline + 2, :] = total


def norm_kernel(h3, h2, h1, h0, squares, gain, later, out):
    wide_gain = gain[...].astype(F32)
    for timeline in range(2):
        total = squares[2 * timeline : 2 * timeline + 2, 0:1] + squares_of(h1, timeline)
        total += squares_of(h2, timeline) + squares_of(h3, timeline)
        scale = lax.rsqrt(total / D + EPSILON)
        out[timeline] = (h0[timeline].astype(F32) * scale * wide_gain).astype(BF16)


def project_kernel(n3, n2, n1, n0, w, kept, sent, rows, sums):
    core = lax.axis_index("gx") & 1
    for shift, normed in enumerate((n0, n1, n2, n3)):
        for timeline in range(2):
            at = ROWS * shift + 2 * timeline
            rows[at : at + 2, :] = normed[timeline].astype(F32)
    left = rows[...].astype(BF16)
    width = 1280
    for step in range(w.shape[1] // width):
        part = jnp.dot(left, w[:, width * step : width * (step + 1)], preferred_element_type=F32)
        for head in range(width // HD):
            at = (step * (width // HD) + head) * ROWS
            for shift in range(NY):
                sums[shift, at : at + ROWS, :] = part[
                    ROWS * shift : ROWS * (shift + 1), HD * head : HD * (head + 1)
                ]
    for k in range(2):
        kept[k] = sums[(3 * k) ^ core]
        sent[k] = sums[(3 * k) ^ core ^ 1]


def chip_kernel(a, b, *outs):
    for k, out in enumerate(outs):
        out[...] = a[k] + b[k]


def round_kernel(b1, a1, b0, a0, out):
    out[0] = (a0[...] + b0[...]).astype(BF16)
    out[1] = (a1[...] + b1[...]).astype(BF16)


def attend_kernel(
    near, far, cosine, sine, lengths, keys, values, kept, sent, projected, turns, live, table, parts
):
    my_x = lax.axis_index("gx")
    my_y = lax.axis_index("gy")
    core = my_x & 1
    for other, pair in enumerate((near, far)):
        for k in range(2):
            at = pl.multiple_of((my_y ^ (3 * k) ^ core ^ other) * QKV_ROWS, 16)
            projected[pl.ds(at, QKV_ROWS), :] = pair[k].astype(F32)
    for t in range(4):
        turns[0, 2 * t : 2 * t + 2, :] = cosine[t % 2]
        turns[1, 2 * t : 2 * t + 2, :] = sine[t % 2]
        live[2 * t : 2 * t + 2, :] = lengths[t % 2]
    turned = projected[: QUERIES + KVH * ROWS, :]
    swapped = pltpu.roll(turned, HD // 2, 1)
    turned = (
        turned.reshape(-1, 8, HD) * turns[0][None] + swapped.reshape(-1, 8, HD) * turns[1][None]
    ).reshape(-1, HD)
    queries = turned[:QUERIES].astype(BF16)
    new_keys = turned[QUERIES:].astype(BF16)
    new_values = projected[QUERIES + KVH * ROWS :, :].astype(BF16)

    row = lax.broadcasted_iota(jnp.int32, (QUERIES, 1), 0)
    token = row & 1
    timeline = (row >> 1) & 1
    group_rows = GROUP_ROWS
    first = timeline[:GROUP_ROWS] == 0
    for g in range(KVH):
        at = slice(GROUP_ROWS * g, GROUP_ROWS * (g + 1))
        both = [
            lax.dot_general(
                queries[at],
                keys[t, :, HD * g : HD * (g + 1)],
                (((1,), (1,)), ((), ())),
                preferred_element_type=F32,
            )
            for t in range(2)
        ]
        table[at, :] = jnp.where(first, both[0], both[1])
    scaling = HD ** (-0.5)
    scores = []
    for start in range(0, SPAN_DEV, HD):
        slot = my_x * SPAN_DEV + start + lax.broadcasted_iota(jnp.int32, (8, HD), 1)
        usable = (slot < live[...])[None]
        part = table[:, start : start + HD].reshape(-1, 8, HD) * scaling
        scores.append(jnp.where(usable, part, NEGATIVE).reshape(QUERIES, HD))
    scores = jnp.concatenate(scores, axis=1)
    maxima = jnp.maximum(jnp.max(scores, axis=-1, keepdims=True), NEGATIVE / 10)

    wide_queries = queries.astype(F32)
    column = lax.broadcasted_iota(jnp.int32, (QUERIES, KVH * ROWS), 1)
    fresh = []
    for j in range(2):
        pick = jnp.where(column == (row // group_rows) * ROWS + timeline * 2 + j, 1.0, 0.0)
        pick = pick.astype(BF16)
        key = jnp.dot(pick, new_keys, preferred_element_type=F32)
        value = jnp.dot(pick, new_values, preferred_element_type=F32)
        score = jnp.sum(wide_queries * key, axis=-1, keepdims=True) * scaling
        allowed = (token >= j) & (my_x == 0)
        maxima = jnp.maximum(maxima, jnp.where(allowed, score, NEGATIVE))
        fresh.append((score, allowed, value))
    weights = jnp.exp(scores - maxima)
    totals = jnp.sum(weights, axis=-1, keepdims=True)
    rounded = weights.astype(BF16)
    added = jnp.zeros((QUERIES, HD), F32)
    for score, allowed, value in fresh:
        weight = jnp.exp(jnp.where(allowed, score - maxima, NEGATIVE))
        totals += weight
        added += weight.astype(BF16).astype(F32) * value
    for g in range(KVH):
        at = slice(GROUP_ROWS * g, GROUP_ROWS * (g + 1))
        both = [
            jnp.dot(rounded[at], values[t, :, HD * g : HD * (g + 1)], preferred_element_type=F32)
            for t in range(2)
        ]
        inside = GROUP_ROWS * (g % 2)
        parts[g // 2, inside : inside + GROUP_ROWS, :] = added[at] + jnp.where(first, *both)

    lane = lax.broadcasted_iota(jnp.int32, (QUERIES, HD), 1)
    sheet = jnp.where(lane == 0, maxima, jnp.where(lane == 1, totals, 0.0))
    flat = jnp.transpose(sheet)[0:8]
    for q in range(NY):
        half = flat[:, HD * (q // 2) : HD * (q // 2 + 1)]
        parts[q, OUT_ROWS:, :] = half if q % 2 == 0 else pltpu.roll(half, OUT_ROWS, 1)
    for k in range(2):
        kept[k] = parts[my_y ^ (3 * k) ^ core]
        sent[k] = parts[my_y ^ (3 * k) ^ core ^ 1]


def columns_of(rows, sheet):
    sheet[...] = jnp.zeros_like(sheet)
    for k, row in enumerate(rows):
        sheet[k : k + 1, :] = row
    turned = jnp.transpose(sheet[...])[:OUT_ROWS]
    return [turned[:, k : k + 1] for k in range(len(rows))]


def merge_kernel(a, b, o0, o1, sheet):
    line = lax.broadcasted_iota(jnp.int32, (8, HD), 0)
    powers, stats = [], []
    for k in range(2):
        a_stats, b_stats = a[k, OUT_ROWS:, :], b[k, OUT_ROWS:, :]
        highest = jnp.maximum(a_stats[0:1], b_stats[0:1])
        power_a = jnp.exp(a_stats[0:1] - highest)
        power_b = jnp.exp(b_stats[0:1] - highest)
        powers += [power_a, power_b]
        stats.append((highest, a_stats[1:2] * power_a + b_stats[1:2] * power_b))
    factors = columns_of(powers, sheet)
    for k, out in enumerate((o0, o1)):
        merged = a[k, :OUT_ROWS, :] * factors[2 * k] + b[k, :OUT_ROWS, :] * factors[2 * k + 1]
        out[:OUT_ROWS, :] = merged.astype(BF16)
        high, rest = high_rest(stats[k][0])
        middle, low = high_rest(rest)
        pieces = jnp.zeros((8, HD), F32)
        for m, piece in enumerate((high, middle, low, *high_rest(stats[k][1]))):
            pieces = jnp.where(line == m, piece, pieces)
        out[OUT_ROWS:, :] = jnp.concatenate([pieces, jnp.zeros_like(pieces)], axis=0).astype(BF16)


def settle_kernel(b1, a1, b0, a0, out, sheet):
    factors = []
    for pair in ((a0, b0), (a1, b1)):
        maxima, totals = [], []
        for part in pair:
            pieces = part[OUT_ROWS:, :].astype(F32)
            maxima.append((pieces[0:1] + pieces[1:2]) + pieces[2:3])
            totals.append(pieces[3:4] + pieces[4:5])
        highest = jnp.maximum(*maxima)
        powers = [jnp.exp(maximum - highest) for maximum in maxima]
        whole = totals[0] * powers[0] + totals[1] * powers[1]
        factors += [power / whole for power in powers]
    columns = columns_of(factors, sheet)
    for k, (a, b) in enumerate(((a0, b0), (a1, b1))):
        attended = a[:OUT_ROWS, :].astype(F32) * columns[2 * k]
        attended += b[:OUT_ROWS, :].astype(F32) * columns[2 * k + 1]
        out[k] = attended.astype(BF16)


def output_kernel(near, far, w, o0, o1, o2, o3, blocks, wide, sums):
    core = lax.axis_index("gx") & 1
    for other, pair in enumerate((near, far)):
        for k in range(2):
            blocks[(3 * k) ^ core ^ other] = pair[k].astype(F32)
    for shift in range(NY):
        for head in range(OUT_HEADS):
            wide[ROWS * shift : ROWS * (shift + 1), HD * head : HD * (head + 1)] = blocks[
                shift, ROWS * head : ROWS * (head + 1), :
            ]
    left = wide[...].astype(BF16)
    width = 1024
    for step in range(w.shape[1] // width):
        part = jnp.dot(left, w[:, width * step : width * (step + 1)], preferred_element_type=F32)
        for chunk in range(width // HD):
            at = (step * (width // HD) + chunk) * ROWS
            for shift in range(NY):
                sums[shift, at : at + ROWS, :] = part[
                    ROWS * shift : ROWS * (shift + 1), HD * chunk : HD * (chunk + 1)
                ]
    o0[...] = sums[0]
    for shift, out in ((1, o1), (2, o2), (3, o3)):
        out[...] = sums[shift].astype(BF16)


def finish_kernel(d, c, b, a, out, total):
    total[...] = (a[...] + b[...].astype(F32)) + (c[...].astype(F32) + d[...].astype(F32))
    for chunk in range(out.shape[2] // HD):
        for timeline in range(2):
            at = ROWS * chunk + 2 * timeline
            out[timeline, :, HD * chunk : HD * (chunk + 1)] = total[at : at + 2, :].astype(BF16)


def rotation(positions):
    halfway = HD // 2
    frequency = ROPE_BASE ** (-2.0 * jnp.arange(halfway, dtype=F32) / HD)
    places = positions[:, None] + jnp.arange(2, dtype=jnp.int32)[None, :]
    angles = places.astype(F32)[:, :, None] * frequency[None, None, :]
    cosine, sine = jnp.cos(angles), jnp.sin(angles)
    return jnp.concatenate([cosine, cosine], axis=2), jnp.concatenate([-sine, sine], axis=2)


def partner(part, axis, distance):
    return lax.ppermute(part, axis, [(k, k ^ distance) for k in range(lax.axis_size(axis))])


def on_gy(parts):
    return [partner(parts[y], "gy", y) if y else parts[y] for y in (3, 2, 1, 0)]


def on_chips(parts):
    received = {}
    for k in (1, 0):
        for far_x in (1, 0):
            pairs = [
                (x * NY + y, (x ^ (2 * far_x)) * NY + (y ^ (3 * k) ^ (x & 1)))
                for x in range(NX)
                for y in range(NY)
            ]
            received[k, far_x] = lax.ppermute(parts[k], ("gx", "gy"), pairs)
    return [received[k, far_x] for k in (1, 0) for far_x in (1, 0)]


def small_body(hidden, norm_gain, w_qkv, w_out, k_cache, v_cache, cache_len, positions):
    def shape(*dims, dtype=BF16):
        return jax.ShapeDtypeStruct(dims, dtype)

    def pinned(array):
        return pltpu.with_memory_space_constraint(array, pltpu.VMEM)

    columns = w_out.shape[1]
    features = hidden.shape[2]
    count = columns // HD * ROWS
    pinned_w_qkv = pinned(w_qkv)
    w_out, k_cache, v_cache = map(pinned, (w_out, k_cache, v_cache))
    cosine, sine = rotation(positions)
    lengths = jnp.broadcast_to(cache_len[:, None, None], (2, 2, HD))

    others = [partner(hidden, "gx", x) for x in (3, 2, 1)]
    squares, held = call(
        square_kernel,
        "square",
        [shape(8, HD, dtype=F32), shape(*hidden.shape)],
        [pinned(hidden)],
    )
    normed = call(
        norm_kernel,
        "norm",
        shape(*hidden.shape),
        [*others, held, squares, norm_gain[None]],
        later=[w_qkv],
    )
    half = shape(2, QKV_ROWS, HD, dtype=F32)
    kept, sent = call(
        project_kernel,
        "project",
        [half, half],
        [*on_gy([normed] * NY), pinned_w_qkv],
        [pltpu.VMEM((NY * ROWS, features), F32), pltpu.VMEM((NY, QKV_ROWS, HD), F32)],
    )
    block = shape(QKV_ROWS, HD, dtype=F32)
    sums = call(chip_kernel, "chip", [block, block], [kept, partner(sent, "gx", 1)])
    near = call(round_kernel, "round", shape(2, QKV_ROWS, HD), on_chips(sums))

    half = shape(2, OUT_ROWS + 8, HD, dtype=F32)
    kept, sent = call(
        attend_kernel,
        "attend",
        [half, half],
        [near, partner(near, "gx", 1), cosine, sine, lengths, k_cache, v_cache],
        [
            pltpu.VMEM((NY * QKV_ROWS, HD), F32),
            pltpu.VMEM((2, 8, HD), F32),
            pltpu.VMEM((8, HD), jnp.int32),
            pltpu.VMEM((QUERIES, SPAN_DEV), F32),
            pltpu.VMEM((NY, OUT_ROWS + 8, HD), F32),
        ],
        mib=16,
    )
    block = shape(OUT_ROWS + 16, HD)
    merged = call(
        merge_kernel,
        "merge",
        [block, block],
        [kept, partner(sent, "gx", 1)],
        [pltpu.VMEM((HD, HD), F32)],
    )
    near = call(
        settle_kernel,
        "settle",
        shape(2, OUT_ROWS, HD),
        on_chips(merged),
        [pltpu.VMEM((HD, HD), F32)],
    )
    blocks = call(
        output_kernel,
        "output",
        [shape(count, HD, dtype=F32)] + [shape(count, HD)] * (NY - 1),
        [near, partner(near, "gx", 1), w_out],
        [
            pltpu.VMEM((NY, OUT_ROWS, HD), F32),
            pltpu.VMEM((NY * ROWS, w_out.shape[0]), F32),
            pltpu.VMEM((NY, count, HD), F32),
        ],
    )
    return call(
        finish_kernel,
        "finish",
        shape(2, 2, columns),
        on_gy(blocks),
        [pltpu.VMEM((count, HD), F32)],
    )


def solution(mesh):
    small = mesh.shape["gx"] == NX and mesh.shape["gy"] == NY
    body = small_body if small else general_body
    in_specs = (
        P(("group", "gy"), None, "gx"),
        P("gx"),
        P("gx", "gy"),
        P("gy", "gx"),
        P(("group", "gy"), "gx", None),
        P(("group", "gy"), "gx", None),
        P(("group", "gy")),
        P(("group", "gy")),
    )
    out_specs = P(("group", "gy"), None, "gx")
    return jax.shard_map(body, mesh=mesh, in_specs=in_specs, out_specs=out_specs, check_vma=False)
```

```python
import jax
import jax.numpy as jnp
from jax import lax
from jax.experimental import pallas as pl
from jax.experimental.pallas import tpu as pltpu
from jax.sharding import PartitionSpec as P

D = 8192
H = 64
KVH = 8
HD = 128
SPAN_DEV = 384


NEGATIVE = -1e30
ROPE_BASE = 500000.0
EPSILON = 1e-05


def combined_all(shard, axis, combine):
    everything = jax.tree.map(lambda part: lax.all_gather(part, axis), shard)
    first = jax.tree.map(lambda part: part[0], everything)

    def turn(k, so_far):
        return combine(so_far, jax.tree.map(lambda part: part[k], everything))

    return lax.fori_loop(1, lax.axis_size(axis), turn, first)


def rotate(inputs, positions, offset):
    halfway = HD // 2
    frequency = ROPE_BASE ** (-2.0 * jnp.arange(halfway, dtype=jnp.float32) / HD)
    places = (
        positions[:, None] + offset + jnp.arange(inputs.shape[1], dtype=jnp.int32)[None, :]
    ).astype(jnp.float32)
    angles = places[:, :, None] * frequency[None, None, :]
    cosine = jnp.cos(angles)[:, :, None, :]
    sines = jnp.sin(angles)[:, :, None, :]
    leading = inputs[..., :halfway]
    trailing = inputs[..., halfway:]
    return jnp.concatenate(
        [leading * cosine - trailing * sines, trailing * cosine + leading * sines], axis=-1
    )


def block_terms(scores, usable):
    maxima = jnp.max(jnp.where(usable, scores, NEGATIVE), axis=-1)
    weights = jnp.exp(jnp.where(usable, scores - maxima[..., None], NEGATIVE))
    return (maxima, jnp.sum(weights, axis=-1), weights)


def combine(first_part, second_part):
    maxima_a, totals_a, partials_a = first_part
    maxima_b, totals_b, partials_b = second_part
    highest = jnp.maximum(maxima_a, maxima_b)
    factor_a = jnp.exp(maxima_a - highest)
    factor_b = jnp.exp(maxima_b - highest)
    return (
        highest,
        totals_a * factor_a + totals_b * factor_b,
        partials_a * factor_a[..., None] + partials_b * factor_b[..., None],
    )


def general_body(hidden, norm_gain, w_qkv, w_out, k_cache, v_cache, cache_len, positions):
    timelines_here = hidden.shape[0]
    tokens_here = hidden.shape[1]
    floats = hidden.astype(jnp.float32)
    squares = lax.psum(jnp.sum(floats * floats, axis=-1), "gx")
    normed = (
        floats * lax.rsqrt(squares[..., None] / D + EPSILON) * norm_gain.astype(jnp.float32)
    ).astype(jnp.bfloat16)
    partial_sums = jnp.einsum(
        "rkc,ce->rke",
        lax.all_gather(normed, "gy", axis=0, tiled=True),
        w_qkv,
        preferred_element_type=jnp.float32,
    )
    summed = lax.psum(partial_sums, "gx").astype(jnp.bfloat16)
    projected = lax.all_to_all(summed, "gy", split_axis=0, concat_axis=2, tiled=True)
    widened = projected.astype(jnp.float32)
    queries = rotate(
        widened[..., : H * HD].reshape(timelines_here, tokens_here, H, HD), positions, 0
    ).astype(jnp.bfloat16)
    fresh_keys = rotate(
        widened[..., H * HD : (H + KVH) * HD].reshape(timelines_here, tokens_here, KVH, HD),
        positions,
        0,
    ).astype(jnp.bfloat16)
    fresh_values = projected[..., (H + KVH) * HD :].reshape(timelines_here, tokens_here, KVH, HD)
    grouped = queries.reshape(timelines_here, tokens_here, KVH, H // KVH, HD)
    cached_keys = k_cache.reshape(timelines_here, SPAN_DEV, KVH, HD)
    cached_values = v_cache.reshape(timelines_here, SPAN_DEV, KVH, HD)
    scaling = HD ** (-0.5)
    scores = (
        jnp.einsum("tkgqd,tsgd->tkgqs", grouped, cached_keys, preferred_element_type=jnp.float32)
        * scaling
    )
    slot_ids = lax.axis_index("gx") * SPAN_DEV + jnp.arange(SPAN_DEV, dtype=jnp.int32)
    usable = (slot_ids[None, :] < cache_len[:, None]).reshape(timelines_here, 1, 1, 1, SPAN_DEV)
    maxima, totals, weights = block_terms(scores, usable)
    partials = jnp.einsum(
        "tkgqs,tsgd->tkgqd",
        weights.astype(jnp.bfloat16),
        cached_values,
        preferred_element_type=jnp.float32,
    )
    merged = combined_all((maxima, totals, partials), "gx", combine)
    fresh_scores = (
        jnp.einsum("tkgqd,tjgd->tkgqj", grouped, fresh_keys, preferred_element_type=jnp.float32)
        * scaling
    )
    key_ids = jnp.arange(tokens_here, dtype=jnp.int32)
    allowed = (key_ids[None, :] <= key_ids[:, None]).reshape(1, tokens_here, 1, 1, tokens_here)
    fresh_maxima, fresh_totals, fresh_weights = block_terms(fresh_scores, allowed)
    fresh_partials = jnp.einsum(
        "tkgqj,tjgd->tkgqd",
        fresh_weights.astype(jnp.bfloat16),
        fresh_values,
        preferred_element_type=jnp.float32,
    )
    _, denominator, numerator = combine(merged, (fresh_maxima, fresh_totals, fresh_partials))
    attended = (
        (numerator / denominator[..., None])
        .astype(jnp.bfloat16)
        .reshape(timelines_here, tokens_here, H * HD)
    )
    heads_in = lax.all_to_all(attended, "gy", split_axis=2, concat_axis=0, tiled=True)
    return lax.psum_scatter(
        jnp.einsum("rke,ed->rkd", heads_in, w_out, preferred_element_type=jnp.float32),
        "gy",
        scatter_dimension=0,
        tiled=True,
    ).astype(jnp.bfloat16)


NX = 4
NY = 4
ROWS = 4
QKV_ROWS = (H + 2 * KVH) // NY * ROWS
OUT_HEADS = H // NY
OUT_ROWS = OUT_HEADS * ROWS
QUERIES = H * ROWS
GROUP_ROWS = QUERIES // KVH
VMEM_SPEC = pl.BlockSpec(memory_space=pltpu.VMEM)
HBM_SPEC = pl.BlockSpec(memory_space=pltpu.HBM)
F32 = jnp.float32
BF16 = jnp.bfloat16


def call(kernel, name, out_shape, operands, scratch=(), mib=8, later=()):
    many = isinstance(out_shape, (list, tuple))
    return pl.pallas_call(
        kernel,
        in_specs=[VMEM_SPEC] * len(operands) + [HBM_SPEC] * len(later),
        out_specs=[VMEM_SPEC] * len(out_shape) if many else VMEM_SPEC,
        out_shape=out_shape,
        scratch_shapes=list(scratch),
        compiler_params=pltpu.CompilerParams(vmem_limit_bytes=mib << 20),
        name=name,
    )(*operands, *(pltpu.with_memory_space_constraint(array, pltpu.HBM) for array in later))


def high_rest(values):
    high = values.astype(BF16).astype(F32)
    return high, values - high


def squares_of(hidden, timeline):
    wide = hidden[timeline].astype(F32)
    return jnp.sum(wide * wide, axis=-1, keepdims=True)


def square_kernel(hidden, gain, out, held, wide_gain):
    wide_gain[...] = gain[...].astype(F32)[None]
    held[...] = hidden[...]
    out[...] = jnp.zeros_like(out)
    for timeline in range(2):
        total = jnp.broadcast_to(squares_of(hidden, timeline), (2, HD))
        out[2 * timeline : 2 * timeline + 2, :] = total


def norm_kernel(h3, h2, h1, h0, squares, gain, later, out):
    for timeline in range(2):
        total = squares[2 * timeline : 2 * timeline + 2, 0:1] + squares_of(h1, timeline)
        total += squares_of(h2, timeline) + squares_of(h3, timeline)
        scale = lax.rsqrt(total / D + EPSILON)
        out[timeline] = (h0[timeline].astype(F32) * scale * gain[...]).astype(BF16)


def project_kernel(n3, n2, n1, n0, w, kept, sent, rows, sums):
    core = lax.axis_index("gx") & 1
    for shift, normed in enumerate((n0, n1, n2, n3)):
        for timeline in range(2):
            at = ROWS * shift + 2 * timeline
            rows[at : at + 2, :] = normed[timeline].astype(F32)
    left = rows[...].astype(BF16)
    width = 512
    deep = w.shape[0] // 2
    for step in range(w.shape[1] // width):
        at = slice(width * step, width * (step + 1))
        part = jnp.dot(left[:, :deep], w[:deep, at], preferred_element_type=F32)
        part += jnp.dot(left[:, deep:], w[deep:, at], preferred_element_type=F32)
        for head in range(width // HD):
            at = (step * (width // HD) + head) * ROWS
            for shift in range(NY):
                sums[shift, at : at + ROWS, :] = part[
                    ROWS * shift : ROWS * (shift + 1), HD * head : HD * (head + 1)
                ]
    for k in range(2):
        kept[k] = sums[(3 * k) ^ core]
        sent[k] = sums[(3 * k) ^ core ^ 1]


def chip_kernel(a, b, *outs):
    for k, out in enumerate(outs):
        out[...] = a[k] + b[k]


def round_kernel(b1, a1, b0, a0, out):
    out[0] = (a0[...] + b0[...]).astype(BF16)
    out[1] = (a1[...] + b1[...]).astype(BF16)


def attend_kernel(
    near, far, cosine, sine, lengths, keys, values, kept, sent, projected, turns, live, table, parts
):
    my_x = lax.axis_index("gx")
    my_y = lax.axis_index("gy")
    core = my_x & 1
    for other, pair in enumerate((near, far)):
        for k in range(2):
            at = pl.multiple_of((my_y ^ (3 * k) ^ core ^ other) * QKV_ROWS, 16)
            projected[pl.ds(at, QKV_ROWS), :] = pair[k].astype(F32)
    for t in range(4):
        turns[0, 2 * t : 2 * t + 2, :] = cosine[t % 2]
        turns[1, 2 * t : 2 * t + 2, :] = sine[t % 2]
        live[2 * t : 2 * t + 2, :] = lengths[t % 2]
    turned = projected[: QUERIES + KVH * ROWS, :]
    swapped = pltpu.roll(turned, HD // 2, 1)
    turned = (
        turned.reshape(-1, 8, HD) * turns[0][None] + swapped.reshape(-1, 8, HD) * turns[1][None]
    ).reshape(-1, HD)
    queries = turned[:QUERIES].astype(BF16)
    new_keys = turned[QUERIES:].astype(BF16)
    new_values = projected[QUERIES + KVH * ROWS :, :].astype(BF16)

    row = lax.broadcasted_iota(jnp.int32, (QUERIES, 1), 0)
    token = row & 1
    timeline = (row >> 1) & 1
    group_rows = GROUP_ROWS
    first = timeline[:GROUP_ROWS] == 0
    for g in range(KVH):
        at = slice(GROUP_ROWS * g, GROUP_ROWS * (g + 1))
        both = [
            lax.dot_general(
                queries[at],
                keys[t, :, HD * g : HD * (g + 1)],
                (((1,), (1,)), ((), ())),
                preferred_element_type=F32,
            )
            for t in range(2)
        ]
        table[at, :] = jnp.where(first, both[0], both[1])
    scaling = HD ** (-0.5)
    scores = []
    for start in range(0, SPAN_DEV, HD):
        slot = my_x * SPAN_DEV + start + lax.broadcasted_iota(jnp.int32, (8, HD), 1)
        usable = (slot < live[...])[None]
        part = table[:, start : start + HD].reshape(-1, 8, HD) * scaling
        scores.append(jnp.where(usable, part, NEGATIVE).reshape(QUERIES, HD))
    scores = jnp.concatenate(scores, axis=1)
    maxima = jnp.maximum(jnp.max(scores, axis=-1, keepdims=True), NEGATIVE / 10)

    wide_queries = queries.astype(F32)
    column = lax.broadcasted_iota(jnp.int32, (QUERIES, KVH * ROWS), 1)
    fresh = []
    for j in range(2):
        pick = jnp.where(column == (row // group_rows) * ROWS + timeline * 2 + j, 1.0, 0.0)
        pick = pick.astype(BF16)
        key = jnp.dot(pick, new_keys, preferred_element_type=F32)
        value = jnp.dot(pick, new_values, preferred_element_type=F32)
        score = jnp.sum(wide_queries * key, axis=-1, keepdims=True) * scaling
        allowed = (token >= j) & (my_x == 0)
        maxima = jnp.maximum(maxima, jnp.where(allowed, score, NEGATIVE))
        fresh.append((score, allowed, value))
    weights = jnp.exp(scores - maxima)
    totals = jnp.sum(weights, axis=-1, keepdims=True)
    rounded = weights.astype(BF16)
    added = jnp.zeros((QUERIES, HD), F32)
    for score, allowed, value in fresh:
        weight = jnp.exp(jnp.where(allowed, score - maxima, NEGATIVE))
        totals += weight
        added += weight.astype(BF16).astype(F32) * value
    for g in range(KVH):
        at = slice(GROUP_ROWS * g, GROUP_ROWS * (g + 1))
        both = [
            jnp.dot(rounded[at], values[t, :, HD * g : HD * (g + 1)], preferred_element_type=F32)
            for t in range(2)
        ]
        inside = GROUP_ROWS * (g % 2)
        parts[g // 2, inside : inside + GROUP_ROWS, :] = added[at] + jnp.where(first, *both)

    lane = lax.broadcasted_iota(jnp.int32, (QUERIES, HD), 1)
    sheet = jnp.where(lane == 0, maxima, jnp.where(lane == 1, totals, 0.0))
    flat = jnp.transpose(sheet)[0:8]
    for q in range(NY):
        half = flat[:, HD * (q // 2) : HD * (q // 2 + 1)]
        parts[q, OUT_ROWS:, :] = half if q % 2 == 0 else pltpu.roll(half, OUT_ROWS, 1)
    for k in range(2):
        kept[k] = parts[my_y ^ (3 * k) ^ core]
        sent[k] = parts[my_y ^ (3 * k) ^ core ^ 1]


def columns_of(rows, sheet):
    sheet[...] = jnp.zeros_like(sheet)
    for k, row in enumerate(rows):
        sheet[k : k + 1, :] = row
    turned = jnp.transpose(sheet[...])[:OUT_ROWS]
    return [turned[:, k : k + 1] for k in range(len(rows))]


def merge_kernel(a, b, o0, o1, sheet):
    line = lax.broadcasted_iota(jnp.int32, (8, HD), 0)
    powers, stats = [], []
    for k in range(2):
        a_stats, b_stats = a[k, OUT_ROWS:, :], b[k, OUT_ROWS:, :]
        highest = jnp.maximum(a_stats[0:1], b_stats[0:1])
        power_a = jnp.exp(a_stats[0:1] - highest)
        power_b = jnp.exp(b_stats[0:1] - highest)
        powers += [power_a, power_b]
        stats.append((highest, a_stats[1:2] * power_a + b_stats[1:2] * power_b))
    factors = columns_of(powers, sheet)
    for k, out in enumerate((o0, o1)):
        merged = a[k, :OUT_ROWS, :] * factors[2 * k] + b[k, :OUT_ROWS, :] * factors[2 * k + 1]
        out[:OUT_ROWS, :] = merged.astype(BF16)
        high, rest = high_rest(stats[k][0])
        middle, low = high_rest(rest)
        pieces = jnp.zeros((8, HD), F32)
        for m, piece in enumerate((high, middle, low, *high_rest(stats[k][1]))):
            pieces = jnp.where(line == m, piece, pieces)
        out[OUT_ROWS:, :] = jnp.concatenate([pieces, jnp.zeros_like(pieces)], axis=0).astype(BF16)


def settle_kernel(b1, a1, b0, a0, out, sheet):
    factors = []
    for pair in ((a0, b0), (a1, b1)):
        maxima, totals = [], []
        for part in pair:
            pieces = part[OUT_ROWS:, :].astype(F32)
            maxima.append((pieces[0:1] + pieces[1:2]) + pieces[2:3])
            totals.append(pieces[3:4] + pieces[4:5])
        highest = jnp.maximum(*maxima)
        powers = [jnp.exp(maximum - highest) for maximum in maxima]
        whole = totals[0] * powers[0] + totals[1] * powers[1]
        factors += [power / whole for power in powers]
    columns = columns_of(factors, sheet)
    for k, (a, b) in enumerate(((a0, b0), (a1, b1))):
        attended = a[:OUT_ROWS, :].astype(F32) * columns[2 * k]
        attended += b[:OUT_ROWS, :].astype(F32) * columns[2 * k + 1]
        out[k] = attended.astype(BF16)


def output_kernel(near, far, w, o0, o1, o2, o3, blocks, wide, sums):
    core = lax.axis_index("gx") & 1
    for other, pair in enumerate((near, far)):
        for k in range(2):
            blocks[(3 * k) ^ core ^ other] = pair[k].astype(F32)
    for shift in range(NY):
        for head in range(OUT_HEADS):
            wide[ROWS * shift : ROWS * (shift + 1), HD * head : HD * (head + 1)] = blocks[
                shift, ROWS * head : ROWS * (head + 1), :
            ]
    left = wide[...].astype(BF16)
    width = 1024
    for step in range(w.shape[1] // width):
        part = jnp.dot(left, w[:, width * step : width * (step + 1)], preferred_element_type=F32)
        for chunk in range(width // HD):
            at = (step * (width // HD) + chunk) * ROWS
            for shift in range(NY):
                sums[shift, at : at + ROWS, :] = part[
                    ROWS * shift : ROWS * (shift + 1), HD * chunk : HD * (chunk + 1)
                ]
    o0[...] = sums[0]
    for shift, out in ((1, o1), (2, o2), (3, o3)):
        out[...] = sums[shift].astype(BF16)


def finish_kernel(d, c, b, a, out, total):
    total[...] = (a[...] + b[...].astype(F32)) + (c[...].astype(F32) + d[...].astype(F32))
    for chunk in range(out.shape[2] // HD):
        for timeline in range(2):
            at = ROWS * chunk + 2 * timeline
            out[timeline, :, HD * chunk : HD * (chunk + 1)] = total[at : at + 2, :].astype(BF16)


def rotation(positions):
    halfway = HD // 2
    frequency = ROPE_BASE ** (-2.0 * jnp.arange(halfway, dtype=F32) / HD)
    places = positions[:, None] + jnp.arange(2, dtype=jnp.int32)[None, :]
    angles = places.astype(F32)[:, :, None] * frequency[None, None, :]
    cosine, sine = jnp.cos(angles), jnp.sin(angles)
    return jnp.concatenate([cosine, cosine], axis=2), jnp.concatenate([-sine, sine], axis=2)


def partner(part, axis, distance):
    return lax.ppermute(part, axis, [(k, k ^ distance) for k in range(lax.axis_size(axis))])


def on_gy(parts):
    return [partner(parts[y], "gy", y) if y else parts[y] for y in (3, 2, 1, 0)]


def on_chips(parts):
    received = {}
    for k in (1, 0):
        for far_x in (1, 0):
            pairs = [
                (x * NY + y, (x ^ (2 * far_x)) * NY + (y ^ (3 * k) ^ (x & 1)))
                for x in range(NX)
                for y in range(NY)
            ]
            received[k, far_x] = lax.ppermute(parts[k], ("gx", "gy"), pairs)
    return [received[k, far_x] for k in (1, 0) for far_x in (1, 0)]


def small_body(hidden, norm_gain, w_qkv, w_out, k_cache, v_cache, cache_len, positions):
    def shape(*dims, dtype=BF16):
        return jax.ShapeDtypeStruct(dims, dtype)

    def pinned(array):
        return pltpu.with_memory_space_constraint(array, pltpu.VMEM)

    columns = w_out.shape[1]
    features = hidden.shape[2]
    count = columns // HD * ROWS
    pinned_w_qkv = pinned(w_qkv)
    w_out, k_cache, v_cache = map(pinned, (w_out, k_cache, v_cache))
    cosine, sine = rotation(positions)
    lengths = jnp.broadcast_to(cache_len[:, None, None], (2, 2, HD))

    others = [partner(hidden, "gx", x) for x in (3, 2, 1)]
    squares, held, wide_gain = call(
        square_kernel,
        "square",
        [shape(8, HD, dtype=F32), shape(*hidden.shape), shape(1, features, dtype=F32)],
        [pinned(hidden), pinned(norm_gain)],
    )
    normed = call(
        norm_kernel,
        "norm",
        shape(*hidden.shape),
        [*others, held, squares, wide_gain],
        later=[w_qkv],
    )
    half = shape(2, QKV_ROWS, HD, dtype=F32)
    kept, sent = call(
        project_kernel,
        "project",
        [half, half],
        [*on_gy([normed] * NY), pinned_w_qkv],
        [pltpu.VMEM((NY * ROWS, features), F32), pltpu.VMEM((NY, QKV_ROWS, HD), F32)],
    )
    block = shape(QKV_ROWS, HD, dtype=F32)
    sums = call(chip_kernel, "chip", [block, block], [kept, partner(sent, "gx", 1)])
    near = call(round_kernel, "round", shape(2, QKV_ROWS, HD), on_chips(sums))

    half = shape(2, OUT_ROWS + 8, HD, dtype=F32)
    kept, sent = call(
        attend_kernel,
        "attend",
        [half, half],
        [near, partner(near, "gx", 1), cosine, sine, lengths, k_cache, v_cache],
        [
            pltpu.VMEM((NY * QKV_ROWS, HD), F32),
            pltpu.VMEM((2, 8, HD), F32),
            pltpu.VMEM((8, HD), jnp.int32),
            pltpu.VMEM((QUERIES, SPAN_DEV), F32),
            pltpu.VMEM((NY, OUT_ROWS + 8, HD), F32),
        ],
        mib=16,
    )
    block = shape(OUT_ROWS + 16, HD)
    merged = call(
        merge_kernel,
        "merge",
        [block, block],
        [kept, partner(sent, "gx", 1)],
        [pltpu.VMEM((HD, HD), F32)],
    )
    near = call(
        settle_kernel,
        "settle",
        shape(2, OUT_ROWS, HD),
        on_chips(merged),
        [pltpu.VMEM((HD, HD), F32)],
    )
    blocks = call(
        output_kernel,
        "output",
        [shape(count, HD, dtype=F32)] + [shape(count, HD)] * (NY - 1),
        [near, partner(near, "gx", 1), w_out],
        [
            pltpu.VMEM((NY, OUT_ROWS, HD), F32),
            pltpu.VMEM((NY * ROWS, w_out.shape[0]), F32),
            pltpu.VMEM((NY, count, HD), F32),
        ],
    )
    return call(
        finish_kernel,
        "finish",
        shape(2, 2, columns),
        on_gy(blocks),
        [pltpu.VMEM((count, HD), F32)],
    )


def solution(mesh):
    small = mesh.shape["gx"] == NX and mesh.shape["gy"] == NY
    body = small_body if small else general_body
    in_specs = (
        P(("group", "gy"), None, "gx"),
        P("gx"),
        P("gx", "gy"),
        P("gy", "gx"),
        P(("group", "gy"), "gx", None),
        P(("group", "gy"), "gx", None),
        P(("group", "gy")),
        P(("group", "gy")),
    )
    out_specs = P(("group", "gy"), None, "gx")
    return jax.shard_map(body, mesh=mesh, in_specs=in_specs, out_specs=out_specs, check_vma=False)
```
